32 devices in a mesh: rep: 8 (over z, y), grp: 4 (over x, core).
Axes of the slice: x: 2, y: 2, z: 4, core: 2. Of those that a mesh axis runs over, the one named last changes fastest.
Arguments:
- inputs: bfloat16 [4096, 2048], P(('rep', 'grp')), may hold values from -6 to 6
- cotangent: bfloat16 [4096, 2048], P(('rep', 'grp')), may hold values from -6 to 6
- segment_ids: int32 [4096], P(('rep', 'grp')), may hold values from 0 to 127, never falling along the last dimension, each value on 1 to 96 neighbouring positions
- weights: bfloat16 [2048, 33408], P(('grp', 'rep')), may hold values from -5 to 3
- master: float32 [2048, 33408], P(('grp', 'rep')), may hold values from -5 to 3
- moment_one: float32 [2048, 33408], P(('grp', 'rep')), may hold values from -6 to 6
- moment_two: float32 [2048, 33408], P(('grp', 'rep')), may hold values from 0.5 to 50
- step: int32 [1], replicated, may hold values from 1 to 8
- learn_rate: float32 [1], replicated, may hold values from 0.05 to 0.3
- beta_one: float32 [1], replicated, may hold values from 0.8 to 0.95
- beta_two: float32 [1], replicated, may hold values from 0.95 to 0.999
Outputs:
- output: bfloat16 [4096, 2048], P(('rep', 'grp'))
- input_grad: bfloat16 [4096, 2048], P(('rep', 'grp'))
- grads: float32 [2048, 33408], P(('grp', 'rep'))
- moment_one_new: float32 [2048, 33408], P(('grp', 'rep'))
- moment_two_new: float32 [2048, 33408], P(('grp', 'rep'))
- master_new: float32 [2048, 33408], P(('grp', 'rep'))
- new_weights: bfloat16 [2048, 33408], P(('grp', 'rep'))
- gain_grads: float32 [2048, 2], P(('grp', 'rep'))
The draws below stay inside these ranges and needn't reach their ends.
Inputs may be any that keep to these rules, and one draw needn't show every extreme that they name: `segment_ids`: never falls from token to token; each document has 1 to 96 tokens, one exactly 96.
All inputs are finite; a program needn't handle non-finite values.
Results may differ from the reference program's by a relative error of at most 0.014.
The reference program's roundings to bfloat16 on the way count: a program that leaves them out, or rounds other values in their place, can miss the bound.
Values may be sent and summed in bfloat16 or wider, within the bound.
A program may use at most 768 MiB of HBM per device.

```python
import math
import jax
import jax.numpy as jnp
import numpy as np
from jax import lax

D = 2048
H = 16
DK = 128
DV = 256
FF = 5632
CONV = 4
SPAN = 64
EXTRA = 128
TOK_DEV = 128
KD = 2048
VD = 4096
COLS = 33408
TOKENS = 4096
SEGS = 128
DOC_MOST = 96


def weight_table(key):
    mixer_end = 2 * KD + 2 * VD
    ffn_start = mixer_end + VD
    down_start = ffn_start + 2 * FF
    extra_start = down_start + FF
    conv_cols = CONV * (2 * KD + VD) // D
    key_list = jax.random.split(key, 5)
    base_draw = jnp.clip(jax.random.normal(key_list[0], (D, COLS), jnp.float32), -6.0, 6.0)
    column = jnp.arange(COLS)
    column_scale = jnp.where(column < mixer_end, D ** (-0.5), 0.0)
    column_scale = column_scale + jnp.where((column >= mixer_end) & (column < ffn_start), 1.5 * VD ** (-0.5), 0.0)
    column_scale = column_scale + jnp.where((column >= ffn_start) & (column < down_start), D ** (-0.5), 0.0)
    column_scale = column_scale + jnp.where((column >= down_start) & (column < extra_start), 1.5 * FF ** (-0.5), 0.0)
    column_scale = column_scale + jnp.where((column >= extra_start) & (column < extra_start + 2 * H), D ** (-0.5), 0.0)
    conv_at = extra_start + 2 * H + 2
    column_scale = column_scale + jnp.where((column >= conv_at) & (column < conv_at + conv_cols), 0.5, 0.0)
    column_scale = column_scale + jnp.where(column >= conv_at + conv_cols, 0.02, 0.0)
    weight_rows = base_draw * column_scale
    gain_pair = jax.random.uniform(key_list[1], (D, 2), jnp.float32, 0.5, 1.5)
    weight_rows = weight_rows.at[:, extra_start + 2 * H:extra_start + 2 * H + 2].set(gain_pair)
    misc_at = conv_at + conv_cols
    row_index = jnp.arange(D)
    a_log = jax.random.uniform(key_list[2], (D,), jnp.float32, math.log(0.02), math.log(2.0))
    dt_bias = jax.random.uniform(key_list[3], (D,), jnp.float32, -5.0, -3.0)
    out_gain = jax.random.uniform(key_list[4], (D,), jnp.float32, 0.5, 1.5)
    misc_column = jnp.where(row_index < H, a_log, jnp.where(row_index < 2 * H, dt_bias, jnp.where(row_index < 2 * H + DV, out_gain, weight_rows[:, misc_at])))
    weight_rows = weight_rows.at[:, misc_at].set(misc_column)
    return weight_rows


def draw_weights(key, part):
    return weight_table(jax.random.fold_in(key, 11)).astype(jnp.bfloat16)


def draw_master(key, part):
    return weight_table(jax.random.fold_in(key, 23))


def shard_levels(rng, dims, shards, smallest, top_value):
    loudness, own = 1.0, jax.random.fold_in(rng, 6)
    for axis_at, blocks in shards:
        draws = jnp.exp(jax.random.uniform(jax.random.fold_in(own, axis_at), (blocks,), jnp.float32, smallest / len(shards), top_value / len(shards)))
        loudness = loudness * jnp.repeat(draws, dims[axis_at] // blocks).reshape([-1 if axis == axis_at else 1 for axis in range(len(dims))])
    return loudness


def length_profile(number_of, total, bound, skew):
    loads = [(1 << 20) // math.isqrt(grade ** skew) + 1 for grade in range(2, number_of + 1)]
    rest, counts = total - bound - (number_of - 1), [1] * (number_of - 1)
    while rest > 0:
        movable = [i for i in range(number_of - 1) if counts[i] < bound]
        mass, left = sum([loads[i] for i in movable]), rest
        for i in movable:
            more = min(bound - counts[i], max(1, left * loads[i] // mass), rest)
            counts[i] = counts[i] + more
            rest = rest - more
    return np.array([bound] + counts)


def ragged_sizes(stream_key, number_of, total, limit, lean):
    if number_of == 2:
        one = jax.random.randint(stream_key, (), max(1, total - limit), min(limit, total - 1) + 1)
        return jnp.stack([one, total - one])
    tallies = jnp.asarray(length_profile(number_of, total, limit, lean), jnp.int32)
    couples = (number_of - 1) // 2
    giver, receiver = tallies[1:1 + 2 * couples:2], tallies[2:2 + 2 * couples:2]
    margin = jnp.minimum(giver - 1, limit - receiver)
    moved = jax.random.randint(jax.random.fold_in(stream_key, 1), (couples,), 0, 1 << 20) % (margin + 1)
    tallies = tallies.at[1:1 + 2 * couples:2].set(giver - moved).at[2:2 + 2 * couples:2].set(receiver + moved)
    return tallies[jax.random.permutation(jax.random.fold_in(stream_key, 2), number_of)]


def noise(key, extent, width, bound, shards=(), held_as=jnp.bfloat16):
    entries = width * jax.random.normal(key, extent, jnp.float32)
    if shards:
        entries = entries * shard_levels(key, extent, shards, -0.22, 0.18)
    return jnp.clip(entries, -bound, bound).astype(held_as)


def setup_inputs(seed: int = 0) -> dict:
    arg_keys = jax.random.split(jax.random.key(seed), 12)
    inputs = noise(arg_keys[0], (TOKENS, D), 1.0, 6.0, ((0, 32),))
    cotangent = noise(arg_keys[1], (TOKENS, D), 1.0, 6.0, ((0, 32),))
    segment_ids = jnp.searchsorted(jnp.cumsum(ragged_sizes(arg_keys[2], SEGS, TOKENS, DOC_MOST, 2)), jnp.arange(TOKENS), side="right").astype(jnp.int32)
    weights = draw_weights(jax.random.fold_in(arg_keys[11], 71), 0)
    master = draw_master(jax.random.fold_in(arg_keys[11], 71), 0)
    moment_one = noise(arg_keys[5], (D, COLS), 1.0, 6.0, ((0, 32),), jnp.float32)
    moment_two = jnp.clip(jnp.exp(math.log(50.0) - 4.6051702 * jax.random.uniform(arg_keys[6], (D, COLS), jnp.float32) ** shard_levels(arg_keys[6], (D, COLS), ((0, 32),), -0.2, 0.2)), 0.5, 50.0)
    step = jax.random.randint(arg_keys[7], (1,), 1, 9).astype(jnp.int32)
    learn_rate = jnp.clip(jax.random.uniform(arg_keys[8], (1,), jnp.float32, 0.05, 0.3), 0.05, 0.3)
    beta_one = jnp.clip(jax.random.uniform(arg_keys[9], (1,), jnp.float32, 0.8, 0.95), 0.8, 0.95)
    beta_two = jnp.clip(jax.random.uniform(arg_keys[10], (1,), jnp.float32, 0.95, 0.999), 0.95, 0.999)
    return {"inputs": inputs, "cotangent": cotangent, "segment_ids": segment_ids, "weights": weights, "master": master, "moment_one": moment_one, "moment_two": moment_two, "step": step, "learn_rate": learn_rate, "beta_one": beta_one, "beta_two": beta_two}


EPS_NORM = 1e-06
EPS_GATED = 1e-05
EPS_ADAM = 1e-08
DECAY_WEIGHT = 0.1
HIGH_PRECISION = lax.Precision.HIGHEST

@jax.custom_vjp
def low(v):
    return lax.optimization_barrier(v.astype(jnp.bfloat16)).astype(jnp.float32)

@jax.custom_vjp
def low_back(v):
    return v

def low_keep(v):
    return (low(v), None)

def low_pass(kept, grad):
    return (grad,)

def back_keep(v):
    return (v, None)

def back_low(kept, grad):
    return (low(grad),)
low.defvjp(low_keep, low_pass)
low_back.defvjp(back_keep, back_low)

def column_starts():
    mixer_end = 2 * KD + 2 * VD
    ffn_start = mixer_end + VD
    down_start = ffn_start + 2 * FF
    extra_start = down_start + FF
    return (mixer_end, ffn_start, down_start, extra_start)

def norm_scale(values, epsilon):
    return lax.rsqrt(lax.optimization_barrier(jnp.mean(values * values, axis=-1, keepdims=True)) + epsilon)

def document_starts(segments):
    leading = jnp.ones(segments.shape[:-1] + (1,), jnp.int32)
    changes = (segments[..., 1:] != segments[..., :-1]).astype(jnp.int32)
    return jnp.concatenate([leading, changes], axis=-1)

def short_conv(channels, kernel, doc_ids):
    summed = channels * kernel[CONV - 1]
    for offset in range(1, CONV):
        shifted = jnp.concatenate([jnp.zeros_like(channels[..., :offset, :]), channels[..., :-offset, :]], axis=-2)
        shifted_docs = jnp.concatenate([jnp.full_like(doc_ids[..., :offset], -1), doc_ids[..., :-offset]], axis=-1)
        same_doc = (shifted_docs == doc_ids).astype(jnp.float32)
        summed = summed + shifted * same_doc[..., None] * kernel[CONV - 1 - offset]
    return summed

def delta_rule(query_vecs, key_vecs, value_vecs, beta_gate, log_decay, starts):
    decay_rate = jnp.exp(log_decay) * (1 - starts).astype(jnp.float32)[..., None]
    batch_count = query_vecs.shape[0]
    blocks = query_vecs.shape[1] // SPAN

    def arrange(member):
        leading = jnp.moveaxis(member, 1, 0)
        return leading.reshape((blocks, SPAN) + leading.shape[1:])

    def token_step(running_memory, pieces):
        query_row, key_row, value_row, beta_row, decay_row = pieces
        kept_memory = running_memory * decay_row[..., None, None]
        recall = jnp.einsum('bhkv,bhk->bhv', kept_memory, key_row, precision=HIGH_PRECISION)
        state_update = beta_row[..., None] * (value_row - recall)
        running_memory = kept_memory + key_row[..., :, None] * state_update[..., None, :]
        return (running_memory, jnp.einsum('bhkv,bhk->bhv', running_memory, query_row, precision=HIGH_PRECISION))

    @jax.checkpoint
    def block_step(running_memory, pieces):
        return lax.scan(token_step, running_memory, pieces)
    initial = jnp.zeros((batch_count, H, DK, DV), jnp.float32)
    pieces = tuple((arrange(member) for member in (query_vecs, key_vecs, value_vecs, beta_gate, decay_rate)))
    final_memory, emitted_output = lax.scan(block_step, initial, pieces)
    emitted_output = emitted_output.reshape((blocks * SPAN, batch_count, H, DV))
    return jnp.moveaxis(emitted_output, 0, 1)

def mixer_core(mixed, gate_pair, extra, starts):
    conv_cols = CONV * (2 * KD + VD) // D
    kernel = extra[:, 2 * H + 2:2 * H + 2 + conv_cols].reshape(CONV, 2 * KD + VD)
    column = extra[:, 2 * H + 2 + conv_cols]
    a_log = column[0:H]
    dt_bias = column[H:2 * H]
    out_gain = column[2 * H:2 * H + DV]
    doc_ids = jnp.cumsum(starts, axis=-1)
    convolved = jax.nn.silu(short_conv(mixed[..., :2 * KD + VD], kernel, doc_ids))
    batch_shape = mixed.shape[:-1]
    query_vecs = convolved[..., :KD].reshape(batch_shape + (H, DK))
    key_vecs = convolved[..., KD:2 * KD].reshape(batch_shape + (H, DK))
    value_vecs = convolved[..., 2 * KD:].reshape(batch_shape + (H, DV))
    query_vecs = query_vecs * lax.rsqrt(lax.optimization_barrier(jnp.sum(query_vecs * query_vecs, axis=-1, keepdims=True)) + EPS_NORM) * DK ** (-0.5)
    key_vecs = key_vecs * lax.rsqrt(lax.optimization_barrier(jnp.sum(key_vecs * key_vecs, axis=-1, keepdims=True)) + EPS_NORM)
    beta_gate = jax.nn.sigmoid(gate_pair[..., H:])
    log_decay = -jnp.exp(a_log) * jax.nn.softplus(gate_pair[..., :H] + dt_bias)
    outputs = delta_rule(query_vecs, key_vecs, value_vecs, beta_gate, log_decay, starts)
    out_gate = mixed[..., 2 * KD + VD:].reshape(batch_shape + (H, DV))
    normed = outputs * norm_scale(outputs, EPS_GATED) * out_gain * jax.nn.silu(out_gate)
    return normed.reshape(batch_shape + (VD,))

def layer_forward(tokens, matrix, starts):
    mixer_end, ffn_start, down_start, extra_start = column_starts()
    extra = matrix[:, extra_start:extra_start + EXTRA]
    gain_one = extra[:, 2 * H]
    gain_two = extra[:, 2 * H + 1]
    normed = low(tokens * norm_scale(tokens, EPS_NORM) * gain_one)
    mixed = low_back(jnp.einsum('bsd,de->bse', normed, matrix[:, :mixer_end], precision=HIGH_PRECISION))
    gate_pair = low_back(jnp.einsum('bsd,de->bse', normed, extra[:, :2 * H], precision=HIGH_PRECISION))
    gated = low(mixer_core(mixed, gate_pair, extra, starts))
    branch = low_back(jnp.einsum('bse,de->bsd', gated, matrix[:, mixer_end:ffn_start], precision=HIGH_PRECISION))
    hidden = tokens + branch
    normed_two = low(hidden * norm_scale(hidden, EPS_NORM) * gain_two)
    gate_up = low_back(jnp.einsum('bsd,df->bsf', normed_two, matrix[:, ffn_start:down_start], precision=HIGH_PRECISION))
    activated = low(jax.nn.silu(gate_up[..., :FF]) * gate_up[..., FF:])
    feed = low_back(jnp.einsum('bsf,df->bsd', activated, matrix[:, down_start:extra_start], precision=HIGH_PRECISION))
    return hidden + feed

def reference(inputs, cotangent, segment_ids, weights, master, moment_one, moment_two, step, learn_rate, beta_one, beta_two):
    seq_count = TOKENS // TOK_DEV
    per_group = math.gcd(seq_count, max(1, 4096 // TOK_DEV))
    group_count = seq_count // per_group
    shaped = (group_count, per_group, TOK_DEV, D)
    token_groups = inputs.astype(jnp.float32).reshape(shaped)
    cot_groups = cotangent.astype(jnp.float32).reshape(shaped)
    seg_groups = segment_ids.reshape(group_count, per_group, TOK_DEV)
    full_weights = weights.astype(jnp.float32)

    def group_step(summed, pieces):
        token_block, cot_block, seg_block = pieces
        starts = document_starts(seg_block)

        def forward_call(tokens, matrix):
            return layer_forward(tokens, matrix, starts)
        emitted_output, pullback = jax.vjp(forward_call, token_block, full_weights)
        token_grad, weight_grad = pullback(cot_block)
        return (summed + weight_grad, (emitted_output.astype(jnp.bfloat16), token_grad.astype(jnp.bfloat16)))
    grads, (emitted_output, token_grads) = lax.scan(group_step, jnp.zeros((D, COLS), jnp.float32), (token_groups, cot_groups, seg_groups))
    extra_start = column_starts()[3]
    gain_grads = grads[:, extra_start + 2 * H:extra_start + 2 * H + 2]
    step_size = learn_rate[0]
    first_beta = beta_one[0]
    second_beta = beta_two[0]
    step_float = step[0].astype(jnp.float32)
    moment_one_new = first_beta * moment_one + (1 - first_beta) * grads
    moment_two_new = second_beta * moment_two + (1 - second_beta) * grads * grads
    first_hat = moment_one_new / (1 - first_beta ** step_float)
    second_hat = moment_two_new / (1 - second_beta ** step_float)
    master_new = master - step_size * (first_hat / (jnp.sqrt(second_hat) + EPS_ADAM) + DECAY_WEIGHT * master)
    return (emitted_output.reshape(TOKENS, D), token_grads.reshape(TOKENS, D), grads, moment_one_new, moment_two_new, master_new, master_new.astype(jnp.bfloat16), gain_grads)
```

```python
import functools

import jax
import jax.numpy as jnp
from jax import lax
from jax.experimental import pallas as pl
from jax.experimental.pallas import tpu as pltpu
from jax.sharding import PartitionSpec as P

D = 2048
H = 16
DK = 128
DV = 256
FF = 5632
CONV = 4
EXTRA = 128
KD = 2048
VD = 4096
MIX_END = 2 * KD + 2 * VD
FFN_START = MIX_END + VD
DOWN_START = FFN_START + 2 * FF
EXTRA_START = DOWN_START + FF
COLS = EXTRA_START + EXTRA

EPS_NORM = 1e-06
EPS_GATED = 1e-05
EPS_ADAM = 1e-08
DECAY_WEIGHT = 0.1
HIGH = lax.Precision.HIGHEST
MESH = pl.DeviceIdType.MESH

RANKS = 8
HEADS = H // RANKS
QW = HEADS * DK
VW = HEADS * DV
MIXW = 2 * QW + 2 * VW + EXTRA
OW = VW
TILES = FF // 128
FULL_RANKS = TILES - (TILES // RANKS) * RANKS
FT = TILES // RANKS + 1
FW = FT * 128
ORDERS = ((4, 2, 1), (2, 1, 4), (1, 4, 2))
PLAIN = ((2, 4, 1), (2, 1, 4))
BF = jnp.bfloat16
F32 = jnp.float32


def rank_of(rep, grp):
    return (grp // 2) * 4 + rep % 4


class Place:
    def __init__(self, copies):
        self.rep = lax.axis_index("rep")
        self.grp = lax.axis_index("grp")
        self.copies = copies
        self.dp = self.rep // 4
        self.core = self.grp % 2
        self.rank = rank_of(self.rep, self.grp)
        self.bits = {4: self.rank // 4, 2: self.rank // 2 % 2, 1: self.rank % 2}

    def flip(self, mask):
        total = 0
        for weight, bit in self.bits.items():
            total = total + weight * ((1 - bit) if mask & weight else bit)
        return total

    def peer(self, mask):
        rank = self.flip(mask)
        return (self.dp * 4 + rank % 4, (rank // 4) * 2 + self.core)

    def sibling(self):
        return (self.rep, self.grp + 1 - 2 * self.core)

    def copy_at(self, shift):
        return (((self.dp + shift) % self.copies) * 4 + self.rep % 4, self.grp)


def meet(devices):
    barrier = pltpu.get_barrier_semaphore()
    for device in devices:
        pl.semaphore_signal(barrier, inc=1, device_id=device, device_id_type=MESH)
    pl.semaphore_wait(barrier, len(devices))


def remote(src, dst, send, recv, device):
    return pltpu.make_async_remote_copy(
        src_ref=src, dst_ref=dst, send_sem=send, recv_sem=recv, device_id=device, device_id_type=MESH
    )


def row_parts(tokens):
    if tokens == 128:
        return ((0, 48), (48, 48), (96, 32))
    third = tokens // 48 * 16
    return ((0, third), (third, third), (2 * third, tokens - 2 * third))


class Gather:
    def __init__(self, place, buf, parts, orders, send, recv):
        self.place, self.buf, self.parts, self.orders = place, buf, parts, orders
        self.send, self.recv = send, recv
        self.flights = {}

    def start(self, part, stage):
        order = self.orders[part]
        delta = order[stage]
        held = [0]
        for earlier in order[:stage]:
            held = held + [mask ^ earlier for mask in held]
        first, rows = self.parts[part]
        begin = 2**stage - 1
        here = []
        for at, mask in enumerate(held):
            block = self.buf.at[self.place.flip(mask), pl.ds(first, rows)]
            slot = begin + at
            copy = remote(
                block, block, self.send.at[part, slot], self.recv.at[part, slot], self.place.peer(delta)
            )
            copy.start()
            here.append(copy)
        self.flights[part, stage] = here

    def landed(self, part, stage):
        for copy in self.flights[part, stage]:
            copy.wait_recv()

    def finish(self):
        for here in self.flights.values():
            for copy in here:
                copy.wait_send()


class Scatter:
    def __init__(self, place, buf, land, parts, orders, send, recv):
        self.place, self.buf, self.land, self.parts, self.orders = place, buf, land, parts, orders
        self.send, self.recv = send, recv
        self.flights = {}
        self.sums = {}

    def held(self, part, stage, mask):
        first, rows = self.parts[part]
        if stage == 0:
            return self.buf.at[self.place.flip(mask), pl.ds(first, rows)]
        return self.land.at[self.sums[part, stage - 1][mask], pl.ds(first, rows)]

    def start(self, part, stage):
        order = self.orders[part]
        delta = order[stage]
        kept = [0]
        for later in order[stage + 1 :]:
            kept = kept + [mask ^ later for mask in kept]
        first, rows = self.parts[part]
        begin = (0, 4, 6)[stage]
        here = []
        for at, mask in enumerate(kept):
            slot = begin + at
            copy = remote(
                self.held(part, stage, mask ^ delta),
                self.land.at[slot, pl.ds(first, rows)],
                self.send.at[part, slot],
                self.recv.at[part, slot],
                self.place.peer(delta),
            )
            copy.start()
            here.append((copy, mask, slot))
        self.flights[part, stage] = here
        self.sums[part, stage] = {mask: slot for _, mask, slot in here}

    def add(self, part, stage):
        first, rows = self.parts[part]
        result = None
        for copy, mask, slot in self.flights[part, stage]:
            copy.wait_recv()
            total = self.held(part, stage, mask)[...].astype(F32) + self.land[
                slot, pl.ds(first, rows)
            ].astype(F32)
            if stage < 2:
                self.land[slot, pl.ds(first, rows)] = total.astype(BF)
            else:
                result = total
        return result

    def finish(self):
        for here in self.flights.values():
            for copy, _, _ in here:
                copy.wait_send()


def tile_start(rank):
    few = FT - 1
    return 128 * jnp.where(rank < FULL_RANKS, FT * rank, FULL_RANKS + few * rank)


def first_columns(rank):
    mixer = (
        (rank * QW, 0, QW),
        (KD + rank * QW, QW, QW),
        (2 * KD + rank * VW, 2 * QW, VW),
        (2 * KD + VD + rank * VW, 2 * QW + VW, VW),
        (EXTRA_START, 2 * QW + 2 * VW, EXTRA),
    )
    outward = ((MIX_END + rank * VW, 0, VW),)
    at = tile_start(rank)
    gates = ((FFN_START + at, 0, FW), (FFN_START + FF + at, FW, FW))
    down = ((DOWN_START + at, 0, FW),)
    return mixer, outward, gates, down


def columns(at, width):
    if not isinstance(at, int):
        at = pl.multiple_of(at, 128)
    return pl.ds(at, width)


def spread_kernel(copies, parts, w_ref, x_ref, s_ref, mix, outward, gates, down, xall, sall,
                  local, send, recv, seg_send, seg_recv, ag_send, ag_recv,
                  copy_send, copy_recv, core_send, core_recv):
    place = Place(copies)
    peers = [place.peer(mask) for mask in range(1, RANKS)]
    partners = [place.copy_at(shift) for shift in range(1, copies)]
    meet(peers + partners + [place.sibling()])
    me = place.rank
    targets = (mix.at[0, 0], outward, gates, down)
    own = []
    firsts = (0, 5, 6, 8)
    for group, pieces in enumerate(first_columns(me)):
        here = []
        for slot, (at, to, width) in enumerate(pieces):
            copy = pltpu.make_async_copy(
                w_ref.at[:, columns(at, width)], targets[group].at[me, :, pl.ds(to, width)],
                local.at[firsts[group] + slot],
            )
            copy.start()
            here.append(copy)
        own.append(here)
    own_x = pltpu.make_async_copy(x_ref, xall.at[me], local.at[9])
    own_x.start()
    own_s = pltpu.make_async_copy(s_ref, sall.at[me], local.at[10])
    own_s.start()

    def send_group(group):
        flights = []
        for mask in range(1, RANKS):
            there = place.flip(mask)
            for slot, (at, to, width) in enumerate(first_columns(there)[group]):
                copy = remote(
                    w_ref.at[:, columns(at, width)],
                    targets[group].at[me, :, pl.ds(to, width)],
                    send.at[firsts[group] + slot, mask - 1],
                    recv.at[group, mask - 1],
                    place.peer(mask),
                )
                copy.start()
                flights.append(copy)
        return flights

    def got(group, mask):
        block = targets[group].at[place.flip(mask)]
        remote(block, block, send.at[0, mask - 1], recv.at[group, mask - 1], place.peer(mask)).wait_recv()

    sent = send_group(0)
    onward = []

    def forward(mask):
        block = mix.at[0, 0, place.flip(mask)]
        for shift in range(1, copies):
            copy = remote(
                block, mix.at[0, copies - shift, place.flip(mask)],
                copy_send.at[shift - 1, mask], copy_recv.at[copies - shift - 1, mask],
                place.copy_at(shift),
            )
            copy.start()
            onward.append(copy)
        copy = remote(
            block, mix.at[1, 0, place.flip(mask)], core_send.at[0, mask], core_recv.at[0, mask],
            place.sibling(),
        )
        copy.start()
        onward.append(copy)

    for copy in own[0]:
        copy.wait()
    forward(0)
    own_s.wait()
    seg_flights = []
    for mask in range(1, RANKS):
        copy = remote(s_ref, sall.at[me], seg_send.at[mask - 1], seg_recv.at[mask - 1], place.peer(mask))
        copy.start()
        seg_flights.append(copy)
    for mask in range(1, RANKS):
        got(0, mask)
        forward(mask)
    own_x.wait()
    gather = Gather(place, xall, parts, PLAIN, ag_send, ag_recv)
    for part in range(len(parts)):
        gather.start(part, 0)
    for group in range(1, 4):
        sent = sent + send_group(group)
    for stage in range(3):
        for part in range(len(parts)):
            gather.landed(part, stage)
            if stage < 2:
                gather.start(part, stage + 1)
    for shift in range(1, copies):
        for mask in range(RANKS):
            block = mix.at[0, shift, place.flip(mask)]
            remote(
                block, block, copy_send.at[shift - 1, mask], copy_recv.at[shift - 1, mask], place.copy_at(shift)
            ).wait_recv()
            copy = remote(
                block, mix.at[1, shift, place.flip(mask)],
                core_send.at[shift, mask], core_recv.at[shift, mask], place.sibling(),
            )
            copy.start()
            onward.append(copy)
    for group in range(1, 4):
        for mask in range(1, RANKS):
            got(group, mask)
    for shift in range(copies):
        for mask in range(RANKS):
            block = mix.at[1, shift, place.flip(mask)]
            remote(
                block, block, core_send.at[shift, mask], core_recv.at[shift, mask], place.sibling()
            ).wait_recv()
    for copy in seg_flights:
        copy.wait()
    for here in own[1:]:
        for copy in here:
            copy.wait()
    for copy in sent + onward:
        copy.wait_send()
    gather.finish()


def any_spec():
    return pl.BlockSpec(memory_space=pl.ANY)


def vmem_spec():
    return pl.BlockSpec(memory_space=pltpu.VMEM)


def dma(*shape):
    return pltpu.SemaphoreType.DMA(shape)


def spread(copies, weights, x, seg):
    rows = weights.shape[0]
    tokens = x.shape[0]
    shape = jax.ShapeDtypeStruct
    return pl.pallas_call(
        functools.partial(spread_kernel, copies, ((0, tokens // 2), (tokens // 2, tokens // 2))),
        out_shape=(
            shape((2, copies, RANKS, rows, MIXW), BF),
            shape((RANKS, rows, OW), BF),
            shape((RANKS, rows, 2 * FW), BF),
            shape((RANKS, rows, FW), BF),
            shape((RANKS, tokens, D), BF),
            shape((RANKS,) + seg.shape, seg.dtype),
        ),
        in_specs=[any_spec()] * 3,
        out_specs=[any_spec()] * 6,
        scratch_shapes=[
            dma(11), dma(9, RANKS - 1), dma(4, RANKS - 1), dma(RANKS - 1), dma(RANKS - 1),
            dma(3, 7), dma(3, 7),
            dma(copies - 1, RANKS), dma(copies - 1, RANKS), dma(copies, RANKS), dma(copies, RANKS),
        ],
        compiler_params=pltpu.CompilerParams(collective_id=1, has_side_effects=True),
        name="spread",
    )(weights, x, seg)


def norm_scale(values, epsilon):
    return lax.rsqrt(jnp.mean(values * values, axis=-1, keepdims=True) + epsilon)


def branch_kernel(copies, parts, part_ref, x_ref, gain_ref, hidden_ref, nall, land,
                  send, recv, ag_send, ag_recv):
    place = Place(copies)
    meet([place.peer(mask) for mask in (4, 2, 1)])
    me = place.rank
    scatter = Scatter(place, part_ref, land, parts, ORDERS, send, recv)
    gather = Gather(place, nall, parts, ORDERS, ag_send, ag_recv)
    for part in range(3):
        scatter.start(part, 0)
    for stage in range(2):
        for part in range(3):
            scatter.add(part, stage)
            scatter.start(part, stage + 1)
    for part in range(3):
        first, rows = parts[part]
        hidden = x_ref[pl.ds(first, rows)].astype(F32) + scatter.add(part, 2)
        hidden_ref[pl.ds(first, rows)] = hidden
        unit = hidden * norm_scale(hidden, EPS_NORM)
        nall[me, pl.ds(first, rows)] = (unit * gain_ref[...]).astype(BF)
        gather.start(part, 0)
    for stage in range(3):
        for part in range(3):
            gather.landed(part, stage)
            if stage < 2:
                gather.start(part, stage + 1)
    scatter.finish()
    gather.finish()


def cube_scratch(tokens):
    return [pltpu.VMEM((7, tokens, D), BF), dma(3, 7), dma(3, 7)]


BIG = 56 * 2**20


def branch(copies, partial, x, gain):
    tokens = x.shape[0]
    shape = jax.ShapeDtypeStruct
    return pl.pallas_call(
        functools.partial(branch_kernel, copies, row_parts(tokens)),
        out_shape=(shape((tokens, D), F32), shape((RANKS, tokens, D), BF)),
        in_specs=[vmem_spec()] * 3,
        out_specs=[vmem_spec()] * 2,
        scratch_shapes=cube_scratch(tokens) + [dma(3, 7), dma(3, 7)],
        compiler_params=pltpu.CompilerParams(collective_id=2, has_side_effects=True, vmem_limit_bytes=BIG),
        name="branch",
    )(partial, x, gain)


def norm_back(grad, values, gain, epsilon):
    scale = norm_scale(values, epsilon)
    unit = values * scale
    scaled = grad * gain
    back = scale * (scaled - unit * jnp.mean(scaled * unit, axis=1, keepdims=True))
    return back, grad * unit


def hidden_back_kernel(copies, parts, part_ref, h_ref, dy_ref, gain_ref, dh_ref, gain_grad, dall, land,
                       send, recv, ag_send, ag_recv):
    place = Place(copies)
    meet([place.peer(mask) for mask in (4, 2, 1)])
    me = place.rank
    scatter = Scatter(place, part_ref, land, parts, ORDERS, send, recv)
    gather = Gather(place, dall, parts, ORDERS, ag_send, ag_recv)
    for part in range(3):
        scatter.start(part, 0)
    for stage in range(2):
        for part in range(3):
            scatter.add(part, stage)
            scatter.start(part, stage + 1)
    total = jnp.zeros((1, D), F32)
    for part in range(3):
        first, rows = parts[part]
        back, gain_part = norm_back(
            scatter.add(part, 2), h_ref[pl.ds(first, rows)], gain_ref[...], EPS_NORM
        )
        back = dy_ref[pl.ds(first, rows)].astype(F32) + back
        dh_ref[pl.ds(first, rows)] = back
        dall[me, pl.ds(first, rows)] = back.astype(BF)
        gather.start(part, 0)
        total = total + jnp.sum(gain_part, axis=0, keepdims=True)
    gain_grad[...] = total
    for stage in range(3):
        for part in range(3):
            gather.landed(part, stage)
            if stage < 2:
                gather.start(part, stage + 1)
    scatter.finish()
    gather.finish()


def hidden_back(copies, partial, hidden, dy, gain):
    tokens = dy.shape[0]
    shape = jax.ShapeDtypeStruct
    return pl.pallas_call(
        functools.partial(hidden_back_kernel, copies, row_parts(tokens)),
        out_shape=(shape((tokens, D), F32), shape((1, D), F32), shape((RANKS, tokens, D), BF)),
        in_specs=[vmem_spec()] * 4,
        out_specs=[vmem_spec()] * 3,
        scratch_shapes=cube_scratch(tokens) + [dma(3, 7), dma(3, 7)],
        compiler_params=pltpu.CompilerParams(collective_id=3, has_side_effects=True, vmem_limit_bytes=BIG),
        name="hidden_back",
    )(partial, hidden, dy, gain)


def ends_kernel(copies, parts, dn_ref, feed_ref, h_ref, dh_ref, x_ref, gain_ref, out_ref, in_grad, gain_grad,
                dn_land, dn_send, dn_recv, feed_land, feed_send, feed_recv):
    place = Place(copies)
    meet([place.peer(mask) for mask in (4, 2, 1)])
    back = Scatter(place, dn_ref, dn_land, parts, ORDERS, dn_send, dn_recv)
    feed = Scatter(place, feed_ref, feed_land, parts, ORDERS, feed_send, feed_recv)
    for part in range(3):
        back.start(part, 0)
    for part in range(3):
        feed.start(part, 0)
    for stage in range(2):
        for one in (back, feed):
            for part in range(3):
                one.add(part, stage)
                one.start(part, stage + 1)
    total = jnp.zeros((1, D), F32)
    for part in range(3):
        first, rows = parts[part]
        grad, gain_part = norm_back(
            back.add(part, 2), x_ref[pl.ds(first, rows)].astype(F32), gain_ref[...], EPS_NORM
        )
        in_grad[pl.ds(first, rows)] = (dh_ref[pl.ds(first, rows)] + grad).astype(BF)
        total = total + jnp.sum(gain_part, axis=0, keepdims=True)
    gain_grad[...] = total
    for part in range(3):
        first, rows = parts[part]
        out_ref[pl.ds(first, rows)] = (h_ref[pl.ds(first, rows)] + feed.add(part, 2)).astype(BF)
    back.finish()
    feed.finish()


def ends(copies, dn_part, feed_part, hidden, d_hidden, x, gain):
    tokens = x.shape[0]
    shape = jax.ShapeDtypeStruct
    return pl.pallas_call(
        functools.partial(ends_kernel, copies, row_parts(tokens)),
        out_shape=(shape((tokens, D), BF), shape((tokens, D), BF), shape((1, D), F32)),
        in_specs=[vmem_spec()] * 6,
        out_specs=[vmem_spec()] * 3,
        scratch_shapes=cube_scratch(tokens) + cube_scratch(tokens),
        compiler_params=pltpu.CompilerParams(collective_id=4, has_side_effects=True, vmem_limit_bytes=BIG),
        name="ends",
    )(dn_part, feed_part, hidden, d_hidden, x, gain)


def home_kernel(copies, groups, base, n_in, *refs):
    ins, out = refs[:n_in], refs[n_in]
    local, send, recv = refs[n_in + 1 :]
    place = Place(copies)
    meet([place.peer(mask) for mask in range(1, RANKS)])
    me = place.rank

    def pieces(rank):
        found = []
        for index, group in enumerate(groups):
            for at, to, width in first_columns(rank)[group]:
                if group == 0 and width == EXTRA and to == 2 * QW + 2 * VW:
                    continue
                if group >= 2:
                    found.append((index, to, at - base, width - 128, False))
                    found.append((index, to + width - 128, at - base + width - 128, 128, True))
                else:
                    found.append((index, to, at - base, width, False))
        return found

    def when(flag, rank, act):
        if flag:
            pl.when(rank < FULL_RANKS)(act)
        else:
            act()

    def run(method):
        for slot, (index, to, at, width, flag) in enumerate(pieces(me)):
            copy = pltpu.make_async_copy(
                ins[index].at[me, :, pl.ds(to, width)], out.at[:, columns(at, width)], local.at[slot]
            )
            when(flag, me, getattr(copy, method))
        for mask in range(1, RANKS):
            there = place.flip(mask)
            for slot, (index, to, at, width, flag) in enumerate(pieces(me)):
                copy = remote(
                    ins[index].at[there, :, pl.ds(to, width)], out.at[:, columns(at, width)],
                    send.at[mask - 1, slot], recv.at[mask - 1, slot], place.peer(mask),
                )
                when(flag, me, copy.start if method == "start" else copy.wait_send)
            if method == "wait":
                for slot, (index, to, at, width, flag) in enumerate(pieces(there)):
                    block = out.at[:, columns(at, width)]
                    copy = remote(
                        block, block, send.at[mask - 1, slot], recv.at[mask - 1, slot], place.peer(mask)
                    )
                    when(flag, there, copy.wait_recv)

    run("start")
    run("wait")


def home(copies, ident, groups, arrays):
    rows = arrays[0].shape[1]
    base = 0 if groups[0] == 0 else MIX_END
    width = MIX_END if groups[0] == 0 else EXTRA_START - MIX_END
    return pl.pallas_call(
        functools.partial(home_kernel, copies, groups, base, len(arrays)),
        out_shape=jax.ShapeDtypeStruct((rows, width), BF),
        in_specs=[any_spec()] * len(arrays),
        out_specs=any_spec(),
        scratch_shapes=[dma(7), dma(RANKS - 1, 7), dma(RANKS - 1, 7)],
        compiler_params=pltpu.CompilerParams(collective_id=ident, has_side_effects=True),
        name="home%d" % ident,
    )(*arrays)


def mul(left, right, axes, precision=HIGH):
    return lax.dot_general(left, right, (axes, ((), ())), precision=precision, preferred_element_type=F32)


NN = ((1,), (0,))
NT = ((1,), (1,))
TN = ((0,), (0,))


def unit_lower_inverse(lower, row, col):
    size = lower.shape[0]
    inverse = jnp.where(row == col, 1.0, jnp.where(row // 2 == col // 2, -lower, 0.0))
    block = 2
    while block < size:
        joined = (row // (2 * block) == col // (2 * block)) & (row // block != col // block)
        part = mul(jnp.where(joined, lower, 0.0), inverse, NN)
        inverse = inverse - mul(inverse, part, NN)
        block = block * 2
    return inverse


class Sequence:
    def __init__(self, seg_row):
        tokens = seg_row.shape[1]
        self.tokens = tokens
        shape = (tokens, tokens)
        self.row = lax.broadcasted_iota(jnp.int32, shape, 0)
        self.col = lax.broadcasted_iota(jnp.int32, shape, 1)
        ids = jnp.broadcast_to(seg_row.astype(F32), shape)
        turned = ids.T
        same = turned == ids
        self.inclusive = same & (self.row >= self.col)
        self.strict = same & (self.row > self.col)
        self.lower = (self.row >= self.col).astype(F32)
        column = turned[:, :1]
        at = self.row[:, :1]
        self.near = [None]
        for back in range(1, CONV):
            before = pltpu.roll(turned, back, 0)[:, :1]
            self.near.append(((before == column) & (at >= back)).astype(F32))

    def conv(self, taps, values):
        total = taps[CONV - 1 : CONV] * values
        for back in range(1, CONV):
            total = total + taps[CONV - 1 - back : CONV - back] * (
                self.near[back] * pltpu.roll(values, back, 0)
            )
        return total

    def conv_back(self, taps, values, grad):
        total = taps[CONV - 1 : CONV] * grad
        rows = [jnp.sum(values * grad, axis=0, keepdims=True)]
        for back in range(1, CONV):
            masked = self.near[back] * grad
            total = total + taps[CONV - 1 - back : CONV - back] * pltpu.roll(
                masked, self.tokens - back, 0
            )
            rows.append(jnp.sum(masked * pltpu.roll(values, back, 0), axis=0, keepdims=True))
        return total, jnp.concatenate(rows[::-1], axis=0)


def pick_lane(block, lane):
    at = lax.broadcasted_iota(jnp.int32, block.shape, 1)
    return jnp.sum(jnp.where(at == lane, block, 0.0), axis=1, keepdims=True)


def softplus(values):
    return jnp.maximum(values, 0.0) + jnp.log1p(jnp.exp(-jnp.abs(values)))


class Head:
    def __init__(self, seq, head, rank, scalars, p_ref, taps_ref):
        q_at, k_at = head * DK, QW + head * DK
        v_at, g_at = 2 * QW + head * DV, 2 * QW + VW + head * DV
        self.q_at, self.k_at, self.v_at, self.g_at = q_at, k_at, v_at, g_at
        self.raw = [p_ref[:, q_at : q_at + DK], p_ref[:, k_at : k_at + DK], p_ref[:, v_at : v_at + DV]]
        self.taps = [taps_ref[:, q_at : q_at + DK], taps_ref[:, k_at : k_at + DK], taps_ref[:, v_at : v_at + DV]]
        self.pre = [seq.conv(taps, raw) for taps, raw in zip(self.taps, self.raw)]
        self.sig = [jax.nn.sigmoid(pre) for pre in self.pre]
        conv_q, conv_k, self.v = [pre * sig for pre, sig in zip(self.pre, self.sig)]
        self.q_scale = lax.rsqrt(jnp.sum(conv_q * conv_q, axis=1, keepdims=True) + EPS_NORM)
        self.k_scale = lax.rsqrt(jnp.sum(conv_k * conv_k, axis=1, keepdims=True) + EPS_NORM)
        self.q_unit = conv_q * self.q_scale
        self.q = self.q_unit * DK**-0.5
        self.k = conv_k * self.k_scale
        pair = p_ref[:, 2 * QW + 2 * VW :]
        self.lane_a = rank * HEADS + head
        self.lane_b = H + rank * HEADS + head
        self.a = pick_lane(pair, self.lane_a) + scalars[HEADS + head]
        self.rate = scalars[head]
        self.beta = jax.nn.sigmoid(pick_lane(pair, self.lane_b))
        self.decay = -self.rate * softplus(self.a)
        spread_out = jnp.where(seq.row > seq.col, jnp.broadcast_to(self.decay, seq.row.shape), 0.0)
        gap = mul(seq.lower, spread_out, NN)
        self.pairs = jnp.where(seq.inclusive, jnp.exp(jnp.where(seq.inclusive, gap, 0.0)), 0.0)
        self.kk = mul(self.k, self.k, NT)
        self.qk = mul(self.q, self.k, NT)
        self.strict_pairs = jnp.where(seq.strict, self.pairs, 0.0)
        self.lower = self.beta * self.strict_pairs * self.kk
        self.attend = self.pairs * self.qk
        self.gate = p_ref[:, g_at : g_at + DV]


def mixer_kernel(rank_ref, scalars, seg_ref, p_ref, taps_ref, gain_ref, z_ref, inv_ref, upd_ref):
    seq = Sequence(seg_ref[0, :1])
    rank = rank_ref[0]
    for head in range(HEADS):
        one = Head(seq, head, rank, scalars, p_ref, taps_ref)
        inverse = unit_lower_inverse(one.lower, seq.row, seq.col)
        update = mul(inverse, one.beta * one.v, NN)
        out = mul(one.attend, update, NN)
        normed = out * norm_scale(out, EPS_GATED) * gain_ref[...]
        z_ref[:, head * DV : (head + 1) * DV] = (normed * (one.gate * jax.nn.sigmoid(one.gate))).astype(BF)
        inv_ref[0, head] = inverse
        upd_ref[0, head] = update


def mixer_back_kernel(rank_ref, scalars, seg_ref, p_ref, taps_ref, gain_ref, inv_ref, upd_ref, dz_ref,
                      dp_ref, dtaps_ref, dgain_ref, dscal_ref):
    @pl.when(pl.program_id(0) == 0)
    def _():
        dtaps_ref[...] = jnp.zeros_like(dtaps_ref)
        dgain_ref[...] = jnp.zeros_like(dgain_ref)
        dscal_ref[...] = jnp.zeros_like(dscal_ref)

    seq = Sequence(seg_ref[0, :1])
    rank = rank_ref[0]
    pair_grad = jnp.zeros((seq.tokens, EXTRA), F32)
    lane = lax.broadcasted_iota(jnp.int32, (seq.tokens, EXTRA), 1)
    scal_row = lax.broadcasted_iota(jnp.int32, (8, 128), 0)
    scal_col = lax.broadcasted_iota(jnp.int32, (8, 128), 1)
    scal = jnp.zeros((8, 128), F32)
    for head in range(HEADS):
        one = Head(seq, head, rank, scalars, p_ref, taps_ref)
        inverse = inv_ref[0, head]
        update = upd_ref[0, head]
        out = mul(one.attend, update, NN)
        dz = dz_ref[:, head * DV : (head + 1) * DV]
        scale = norm_scale(out, EPS_GATED)
        normed = out * scale
        sig = jax.nn.sigmoid(one.gate)
        gate = one.gate * sig
        d_gate = dz * normed * gain_ref[...] * (sig * (1 + one.gate * (1 - sig)))
        dp_ref[:, one.g_at : one.g_at + DV] = d_gate.astype(BF)
        dgain_ref[...] += jnp.sum(dz * normed * gate, axis=0, keepdims=True)
        d_normed = dz * gain_ref[...] * gate
        d_out = scale * (d_normed - normed * jnp.mean(d_normed * normed, axis=1, keepdims=True))
        d_attend = jnp.where(seq.inclusive, mul(d_out, update, NT), 0.0)
        d_update = mul(one.attend, d_out, TN)
        d_scaled = mul(inverse, d_update, TN)
        d_lower = jnp.where(seq.strict, -mul(d_scaled, update, NT), 0.0)
        d_v = one.beta * d_scaled
        d_beta = jnp.sum(d_scaled * one.v, axis=1, keepdims=True) + jnp.sum(
            d_lower * one.strict_pairs * one.kk, axis=1, keepdims=True
        )
        d_gap = d_attend * one.attend + d_lower * one.lower
        d_qk = d_attend * one.pairs
        d_kk = d_lower * (one.beta * one.strict_pairs)
        d_q = mul(d_qk, one.k, NN)
        d_k = mul(d_qk, one.q, TN) + mul(d_kk, one.k, NN) + mul(d_kk, one.k, TN)
        reach = mul(seq.lower, d_gap, TN)
        d_decay = jnp.sum(jnp.where(seq.row > seq.col, reach, 0.0), axis=1, keepdims=True)
        d_a = d_decay * (-one.rate) * jax.nn.sigmoid(one.a)
        d_b = d_beta * one.beta * (1 - one.beta)
        pair_grad = pair_grad + jnp.where(lane == one.lane_a, d_a, 0.0) + jnp.where(lane == one.lane_b, d_b, 0.0)
        sum_rate = jnp.sum(d_decay * one.decay, axis=0, keepdims=True)
        sum_a = jnp.sum(d_a, axis=0, keepdims=True)
        scal = scal + jnp.where((scal_row == 0) & (scal_col == head), sum_rate, 0.0)
        scal = scal + jnp.where((scal_row == 0) & (scal_col == HEADS + head), sum_a, 0.0)
        dq_unit = d_q * DK**-0.5
        dc_q = one.q_scale * (dq_unit - one.q_unit * jnp.sum(dq_unit * one.q_unit, axis=1, keepdims=True))
        dc_k = one.k_scale * (d_k - one.k * jnp.sum(d_k * one.k, axis=1, keepdims=True))
        for grad, pre, sig, raw, taps, at, width in (
            (dc_q, one.pre[0], one.sig[0], one.raw[0], one.taps[0], one.q_at, DK),
            (dc_k, one.pre[1], one.sig[1], one.raw[1], one.taps[1], one.k_at, DK),
            (d_v, one.pre[2], one.sig[2], one.raw[2], one.taps[2], one.v_at, DV),
        ):
            d_pre = grad * (sig * (1 + pre * (1 - sig)))
            d_raw, d_taps = seq.conv_back(taps, raw, d_pre)
            dp_ref[:, at : at + width] = d_raw.astype(BF)
            dtaps_ref[:, at : at + width] += d_taps
    dp_ref[:, 2 * QW + 2 * VW :] = pair_grad.astype(BF)
    dscal_ref[...] += scal


def smem_spec():
    return pl.BlockSpec(memory_space=pltpu.SMEM)


def by_sequence(*shape):
    rest = (0,) * (len(shape) - 1)
    return pl.BlockSpec(shape, lambda at: (at,) + rest)


def whole_block(*shape):
    return pl.BlockSpec(shape, lambda at: (0,) * len(shape))


CHANNELS = 2 * QW + VW


def mixer(rank, scalars, seg, p, taps, gain, tokens):
    count = p.shape[0] // tokens
    shape = jax.ShapeDtypeStruct
    return pl.pallas_call(
        mixer_kernel,
        grid=(count,),
        out_shape=(
            shape((p.shape[0], VW), BF),
            shape((count, HEADS, tokens, tokens), F32),
            shape((count, HEADS, tokens, DV), F32),
        ),
        in_specs=[
            smem_spec(), smem_spec(), by_sequence(1, 8, tokens), by_sequence(tokens, MIXW),
            whole_block(CONV, CHANNELS), whole_block(1, DV),
        ],
        out_specs=[
            by_sequence(tokens, VW), by_sequence(1, HEADS, tokens, tokens), by_sequence(1, HEADS, tokens, DV),
        ],
        compiler_params=pltpu.CompilerParams(vmem_limit_bytes=40 * 2**20),
        name="mixer",
    )(rank, scalars, seg, p, taps, gain)


def mixer_back(rank, scalars, seg, p, taps, gain, inverse, update, dz, tokens):
    count = p.shape[0] // tokens
    shape = jax.ShapeDtypeStruct
    return pl.pallas_call(
        mixer_back_kernel,
        grid=(count,),
        out_shape=(
            shape((p.shape[0], MIXW), BF),
            shape((CONV, CHANNELS), F32),
            shape((1, DV), F32),
            shape((8, 128), F32),
        ),
        in_specs=[
            smem_spec(), smem_spec(), by_sequence(1, 8, tokens), by_sequence(tokens, MIXW),
            whole_block(CONV, CHANNELS), whole_block(1, DV),
            by_sequence(1, HEADS, tokens, tokens), by_sequence(1, HEADS, tokens, DV), by_sequence(tokens, VW),
        ],
        out_specs=[
            by_sequence(tokens, MIXW), whole_block(CONV, CHANNELS), whole_block(1, DV), whole_block(8, 128),
        ],
        compiler_params=pltpu.CompilerParams(vmem_limit_bytes=40 * 2**20),
        name="mixer_back",
    )(rank, scalars, seg, p, taps, gain, inverse, update, dz)


def turn(blocks, shift, axis):
    size = blocks.shape[axis]
    twice = jnp.concatenate([blocks, blocks], axis=axis)
    return lax.dynamic_slice_in_dim(twice, shift % size, size, axis)


class Order:
    def __init__(self, copies, core, dp):
        self.copies, self.core, self.dp = copies, core, dp

    def relative(self, values, axis):
        lead, tail = values.shape[:axis], values.shape[axis + 1 :]
        whole = values.reshape(lead + (2, 2, self.copies, D // (4 * self.copies)) + tail)
        whole = turn(turn(whole, self.core, axis + 1), self.dp, axis + 2)
        whole = jnp.moveaxis(whole, axis, axis + 2)
        return whole.reshape(values.shape)

    def plain(self, values, axis):
        lead, tail = values.shape[:axis], values.shape[axis + 1 :]
        whole = values.reshape(lead + (2, self.copies, 2, D // (4 * self.copies)) + tail)
        whole = jnp.moveaxis(whole, axis + 2, axis)
        whole = turn(turn(whole, 2 - self.core, axis + 1), self.copies - self.dp, axis + 2)
        return whole.reshape(values.shape)


def dot(left, right, axes):
    return lax.dot_general(left, right, (axes, ((), ())), preferred_element_type=F32)


def on_device(inputs, cotangent, segment_ids, weights, master, moment_one, moment_two,
              step, learn_rate, beta_one, beta_two):
    tokens = inputs.shape[0]
    rows = weights.shape[0]
    replicas = lax.axis_size("rep")
    copies = replicas // 4
    members = replicas * 4
    rep = lax.axis_index("rep")
    grp = lax.axis_index("grp")
    core = grp % 2
    dp = rep // 4
    rank = rank_of(rep, grp)
    order = Order(copies, core, dp)
    axes = ("rep", "grp")
    group_tokens = RANKS * tokens
    block_rows = RANKS * rows

    def pairs_to(move):
        return [(at, move(at // 4, at % 4)) for at in range(members)]

    core_pairs = pairs_to(lambda r, g: r * 4 + (g ^ 1))
    copy_pairs = [
        pairs_to(lambda r, g, shift=shift: ((r + 4 * shift) % replicas) * 4 + g) for shift in range(1, copies)
    ]

    x = order.relative(inputs, 1)
    dy = order.relative(cotangent, 1)
    seg = jnp.broadcast_to(segment_ids[None, :], (8, tokens))
    mix_blocks, out_block, gate_block, down_block, x_all, seg_all = spread(copies, weights, x, seg)
    x_all = x_all.reshape(group_tokens, D)
    w_mix = mix_blocks.reshape(D, MIXW)

    def collect(block):
        block = block.reshape(block_rows, block.shape[2])
        mine = [block]
        for shift in range(1, copies):
            mine.append(lax.ppermute(block, axes, copy_pairs[copies - shift - 1]))
        theirs = [lax.ppermute(one, axes, core_pairs) for one in mine]
        return jnp.concatenate(mine + theirs, axis=0)

    w_out = collect(out_block)
    w_gates = collect(gate_block)
    w_down = collect(down_block)

    pieces = [dy]
    for mask in range(1, RANKS):
        def to_rank(r, g, mask=mask):
            there = ((g // 2) * 4 + r % 4) ^ mask
            return ((r // 4) * 4 + there % 4) * 4 + (there // 4) * 2 + g % 2
        pieces.append(lax.ppermute(dy, axes, pairs_to(to_rank)))
    dy_all = jnp.zeros((RANKS, tokens, D), BF)
    for mask in range(RANKS):
        there = ((rank // 4) ^ (mask // 4)) * 4 + ((rank // 2 % 2) ^ (mask // 2 % 2)) * 2 + ((rank % 2) ^ (mask % 2))
        dy_all = lax.dynamic_update_slice(dy_all, pieces[mask][None], (there, 0, 0))
    dy_all = dy_all.reshape(group_tokens, D)

    extra_rel = w_mix[:, MIXW - EXTRA :]
    gain_one = extra_rel[:, 2 * H].astype(F32)[None]
    gain_two = extra_rel[:, 2 * H + 1].astype(F32)[None]
    extra = order.plain(extra_rel, 0).astype(F32)
    conv_cols = CONV * (2 * KD + VD) // D
    kernel = extra[:, 2 * H + 2 : 2 * H + 2 + conv_cols].reshape(CONV, 2 * KD + VD)
    taps = jnp.concatenate(
        [
            lax.dynamic_slice_in_dim(kernel, rank * QW, QW, 1),
            lax.dynamic_slice_in_dim(kernel, KD + rank * QW, QW, 1),
            lax.dynamic_slice_in_dim(kernel, 2 * KD + rank * VW, VW, 1),
        ],
        axis=1,
    )
    column = extra[:, 2 * H + 2 + conv_cols]
    scalars = jnp.concatenate(
        [
            jnp.exp(lax.dynamic_slice_in_dim(column, rank * HEADS, HEADS, 0)),
            lax.dynamic_slice_in_dim(column, H + rank * HEADS, HEADS, 0),
        ]
    )
    out_gain = column[2 * H : 2 * H + DV][None]
    rank_arg = jnp.reshape(rank, (1,)).astype(jnp.int32)

    tokens_all = x_all.astype(F32)
    normed = (tokens_all * norm_scale(tokens_all, EPS_NORM) * gain_one).astype(BF)
    p = dot(normed, w_mix, NN)
    gated, inverse, update = mixer(rank_arg, scalars, seg_all, p, taps, out_gain, tokens)
    partial = dot(gated, w_out, NT).astype(BF)
    hidden, normed_two = branch(copies, partial.reshape(RANKS, tokens, D), x, gain_two)
    normed_two = normed_two.reshape(group_tokens, D)

    gate_up = dot(normed_two, w_gates, NN)
    gate_part, up_part = gate_up[:, :FW], gate_up[:, FW:]
    tile_count = jnp.where(rank < FULL_RANKS, FT, FT - 1)
    real = (jnp.arange(FW) < tile_count * 128)[None]
    sigmoid_gate = jax.nn.sigmoid(gate_part)
    activated = jnp.where(real, gate_part * sigmoid_gate * up_part, 0.0).astype(BF)
    feed = dot(activated, w_down, NT).astype(BF)
    d_act = dot(dy_all, w_down, NN)
    d_gate = d_act * up_part * sigmoid_gate * (1 + gate_part * (1 - sigmoid_gate))
    d_up = d_act * gate_part * sigmoid_gate
    real_two = jnp.concatenate([real, real], axis=1)
    d_gate_up = jnp.where(real_two, jnp.concatenate([d_gate, d_up], axis=1), 0.0).astype(BF)
    d_normed_two = dot(d_gate_up, w_gates, NT).astype(BF)
    d_hidden, gain_two_grad, d_hidden_all = hidden_back(
        copies, d_normed_two.reshape(RANKS, tokens, D), hidden, dy, gain_two
    )
    d_hidden_all = d_hidden_all.reshape(group_tokens, D)
    d_gated = dot(d_hidden_all, w_out, NN)
    d_mix, d_taps, d_out_gain, d_scalars = mixer_back(
        rank_arg, scalars, seg_all, p, taps, out_gain, inverse, update, d_gated, tokens
    )
    d_normed = dot(d_mix, w_mix, NT).astype(BF)
    out_rel, in_grad_rel, gain_one_grad = ends(
        copies, d_normed.reshape(RANKS, tokens, D), feed.reshape(RANKS, tokens, D), hidden, d_hidden, x, gain_one
    )
    output = order.plain(out_rel, 1)
    input_grad = order.plain(in_grad_rel, 1)

    def reduce_rows(left, right):
        half = copies * block_rows
        theirs = dot(left[:, half:], right, TN).astype(BF)
        got = lax.ppermute(theirs, axes, core_pairs)
        away = [
            (dot(left[:, at * block_rows : (at + 1) * block_rows], right, TN)
             + got[at * block_rows : (at + 1) * block_rows].astype(F32)).astype(BF)
            for at in range(1, copies)
        ]
        total = dot(left[:, :block_rows], right, TN) + got[:block_rows].astype(F32)
        for shift in range(1, copies):
            total = total + lax.ppermute(away[shift - 1], axes, copy_pairs[shift - 1]).astype(F32)
        return total.astype(BF).reshape(RANKS, rows, right.shape[1])

    down_rows = reduce_rows(dy_all, activated)
    gate_rows = reduce_rows(normed_two, d_gate_up)
    out_rows = reduce_rows(d_hidden_all, gated)
    mix_rows = reduce_rows(normed, d_mix)
    grads_rest = home(copies, 5, (1, 2, 3), (out_rows, gate_rows, down_rows))
    grads_mix = home(copies, 6, (0,), (mix_rows,))

    pair_grad = dot(normed, d_mix[:, MIXW - EXTRA :], TN)
    lanes = jnp.arange(EXTRA)[None]
    rel_grad = (
        pair_grad
        + jnp.where(lanes == 2 * H, gain_one_grad.reshape(D, 1), 0.0)
        + jnp.where(lanes == 2 * H + 1, gain_two_grad.reshape(D, 1), 0.0)
    )
    tap_grad = jnp.zeros((CONV, 2 * KD + VD), F32)
    tap_grad = lax.dynamic_update_slice(tap_grad, d_taps[:, :QW], (0, rank * QW))
    tap_grad = lax.dynamic_update_slice(tap_grad, d_taps[:, QW : 2 * QW], (0, KD + rank * QW))
    tap_grad = lax.dynamic_update_slice(tap_grad, d_taps[:, 2 * QW :], (0, 2 * KD + rank * VW))
    small = jnp.zeros((D,), F32)
    small = lax.dynamic_update_slice(small, d_scalars[0, :HEADS], (rank * HEADS,))
    small = lax.dynamic_update_slice(small, d_scalars[0, HEADS : 2 * HEADS], (H + rank * HEADS,))
    small = lax.dynamic_update_slice(small, d_out_gain[0], (2 * H,))
    core_grad = jnp.concatenate(
        [
            jnp.zeros((D, 2 * H + 2), F32),
            tap_grad.reshape(D, conv_cols),
            small[:, None],
            jnp.zeros((D, EXTRA - 2 * H - 3 - conv_cols), F32),
        ],
        axis=1,
    )
    extra_grad = order.plain(rel_grad, 0) + core_grad
    extra_grad = jnp.swapaxes(extra_grad.reshape(4, replicas, rows, EXTRA), 0, 1).reshape(D, EXTRA)
    extra_rows = lax.psum_scatter(extra_grad, axes, scatter_dimension=0, tiled=True)

    grads = jnp.concatenate([grads_mix.astype(F32), grads_rest.astype(F32), extra_rows], axis=1)
    gain_grads = extra_rows[:, 2 * H : 2 * H + 2]
    step_size = learn_rate[0]
    first_beta = beta_one[0]
    second_beta = beta_two[0]
    step_float = step[0].astype(F32)
    moment_one_new = first_beta * moment_one + (1 - first_beta) * grads
    moment_two_new = second_beta * moment_two + (1 - second_beta) * grads * grads
    first_hat = moment_one_new / (1 - first_beta**step_float)
    second_hat = moment_two_new / (1 - second_beta**step_float)
    master_new = master - step_size * (first_hat / (jnp.sqrt(second_hat) + EPS_ADAM) + DECAY_WEIGHT * master)
    return (output, input_grad, grads, moment_one_new, moment_two_new, master_new,
            master_new.astype(BF), gain_grads)


def solution(mesh):
    by_token = P(("rep", "grp"), None)
    by_row = P(("grp", "rep"), None)
    return jax.shard_map(
        on_device,
        mesh=mesh,
        in_specs=(by_token, by_token, P(("rep", "grp")), by_row, by_row, by_row, by_row, P(), P(), P(), P()),
        out_specs=(by_token, by_token) + (by_row,) * 6,
        check_vma=False,
    )
```

```python
import functools

import jax
import jax.numpy as jnp
from jax import lax
from jax.experimental import pallas as pl
from jax.experimental.pallas import tpu as pltpu
from jax.sharding import PartitionSpec as P

D = 2048
H = 16
DK = 128
DV = 256
FF = 5632
CONV = 4
EXTRA = 128
KD = 2048
VD = 4096
MIX_END = 2 * KD + 2 * VD
FFN_START = MIX_END + VD
DOWN_START = FFN_START + 2 * FF
EXTRA_START = DOWN_START + FF
COLS = EXTRA_START + EXTRA

EPS_NORM = 1e-06
EPS_GATED = 1e-05
EPS_ADAM = 1e-08
DECAY_WEIGHT = 0.1
MESH = pl.DeviceIdType.MESH

RANKS = 8
HEADS = H // RANKS
QW = HEADS * DK
VW = HEADS * DV
MIXW = 2 * QW + 2 * VW + EXTRA
OW = VW
TILES = FF // 128
FULL_RANKS = TILES - (TILES // RANKS) * RANKS
FT = TILES // RANKS + 1
FW = FT * 128
SPLIT = ((4, 1, 2), (1, 2, 4), (2, 4, 1))
MEET = ((2, 1, 4), (4, 2, 1), (1, 4, 2))
MEET_EARLY = ((2, 4, 1), (2, 1, 4))
BF = jnp.bfloat16
F32 = jnp.float32


def rank_of(rep, grp):
    return (grp // 2) * 4 + rep % 4


class Place:
    def __init__(self, copies):
        self.rep = lax.axis_index("rep")
        self.grp = lax.axis_index("grp")
        self.copies = copies
        self.dp = self.rep // 4
        self.core = self.grp % 2
        self.rank = rank_of(self.rep, self.grp)
        self.bits = {4: self.rank // 4, 2: self.rank // 2 % 2, 1: self.rank % 2}

    def flip(self, mask):
        total = 0
        for weight, bit in self.bits.items():
            total = total + weight * ((1 - bit) if mask & weight else bit)
        return total

    def peer(self, mask):
        rank = self.flip(mask)
        return (self.dp * 4 + rank % 4, (rank // 4) * 2 + self.core)

    def sibling(self):
        return (self.rep, self.grp + 1 - 2 * self.core)

    def copy_at(self, shift):
        return (((self.dp + shift) % self.copies) * 4 + self.rep % 4, self.grp)


def meet(devices):
    barrier = pltpu.get_barrier_semaphore()
    for device in devices:
        pl.semaphore_signal(barrier, inc=1, device_id=device, device_id_type=MESH)
    pl.semaphore_wait(barrier, len(devices))


def remote(src, dst, send, recv, device):
    return pltpu.make_async_remote_copy(
        src_ref=src, dst_ref=dst, send_sem=send, recv_sem=recv, device_id=device, device_id_type=MESH
    )


def row_parts(tokens, count):
    tiles = tokens // 16
    sizes = [16 * (tiles * (at + 1) // count - tiles * at // count) for at in range(count)]
    sizes.sort(reverse=True)
    return tuple((sum(sizes[:at]), sizes[at]) for at in range(count))


class Gather:
    def __init__(self, place, buf, parts, orders, send, recv):
        self.place, self.buf, self.parts, self.orders = place, buf, parts, orders
        self.send, self.recv = send, recv
        self.flights = {}

    def start(self, part, stage):
        order = self.orders[part]
        delta = order[stage]
        held = [0]
        for earlier in order[:stage]:
            held = held + [mask ^ earlier for mask in held]
        first, rows = self.parts[part]
        begin = 2**stage - 1
        here = []
        for at, mask in enumerate(held):
            block = self.buf.at[self.place.flip(mask), pl.ds(first, rows)]
            slot = begin + at
            copy = remote(
                block, block, self.send.at[part, slot], self.recv.at[part, slot], self.place.peer(delta)
            )
            copy.start()
            here.append(copy)
        self.flights[part, stage] = here

    def landed(self, part, stage):
        for copy in self.flights[part, stage]:
            copy.wait_recv()

    def finish(self):
        for here in self.flights.values():
            for copy in here:
                copy.wait_send()


class Scatter:
    def __init__(self, place, buf, land, parts, orders, send, recv):
        self.place, self.buf, self.land, self.parts, self.orders = place, buf, land, parts, orders
        self.send, self.recv = send, recv
        self.flights = {}
        self.sums = {}

    def held(self, part, stage, mask):
        first, rows = self.parts[part]
        if stage == 0:
            return self.buf.at[self.place.flip(mask), pl.ds(first, rows)]
        return self.land.at[self.sums[part, stage - 1][mask], pl.ds(first, rows)]

    def start(self, part, stage):
        order = self.orders[part]
        delta = order[stage]
        kept = [0]
        for later in order[stage + 1 :]:
            kept = kept + [mask ^ later for mask in kept]
        first, rows = self.parts[part]
        begin = (0, 4, 6)[stage]
        here = []
        for at, mask in enumerate(kept):
            slot = begin + at
            copy = remote(
                self.held(part, stage, mask ^ delta),
                self.land.at[slot, pl.ds(first, rows)],
                self.send.at[part, slot],
                self.recv.at[part, slot],
                self.place.peer(delta),
            )
            copy.start()
            here.append((copy, mask, slot))
        self.flights[part, stage] = here
        self.sums[part, stage] = {mask: slot for _, mask, slot in here}

    def add(self, part, stage):
        first, rows = self.parts[part]
        result = None
        for copy, mask, slot in self.flights[part, stage]:
            copy.wait_recv()
            total = self.held(part, stage, mask)[...].astype(F32) + self.land[
                slot, pl.ds(first, rows)
            ].astype(F32)
            if stage < 2:
                self.land[slot, pl.ds(first, rows)] = total.astype(BF)
            else:
                result = total
        return result

    def finish(self):
        for here in self.flights.values():
            for copy, _, _ in here:
                copy.wait_send()


def tile_start(rank):
    few = FT - 1
    return 128 * jnp.where(rank < FULL_RANKS, FT * rank, FULL_RANKS + few * rank)


def first_columns(rank):
    mixer = (
        (rank * QW, 0, QW),
        (KD + rank * QW, QW, QW),
        (2 * KD + rank * VW, 2 * QW, VW),
        (2 * KD + VD + rank * VW, 2 * QW + VW, VW),
        (EXTRA_START, 2 * QW + 2 * VW, EXTRA),
    )
    outward = ((MIX_END + rank * VW, 0, VW),)
    at = tile_start(rank)
    gates = ((FFN_START + at, 0, FW), (FFN_START + FF + at, FW, FW))
    down = ((DOWN_START + at, 0, FW),)
    return mixer, outward, gates, down


def feature_blocks(place):
    copies = place.copies
    width = D // (4 * copies)
    if width % 128:
        return [(0, 0, D)]
    found = []
    for core in range(2):
        for copy in range(copies):
            for x in range(2):
                block = (x * 2 + (place.core + core) % 2) * copies + (place.dp + copy) % copies
                found.append((block * width, ((core * copies + copy) * 2 + x) * width, width))
    return found


def columns(at, width):
    if not isinstance(at, int):
        at = pl.multiple_of(at, 128)
    return pl.ds(at, width)


def spread_kernel(copies, parts, w_ref, x_ref, dy_ref, s_ref, mix, outward, gates, down, xall, sall, x_own, dy_own,
                  pack, pack_sem, local, send, recv, seg_send, seg_recv,
                  ag_send, ag_recv, copy_send, copy_recv, core_send, core_recv, side_send, side_recv, turned):
    place = Place(copies)
    peers = [place.peer(mask) for mask in range(1, RANKS)]
    partners = [place.copy_at(shift) for shift in range(1, copies)]
    meet(peers + partners + [place.sibling()])
    me = place.rank
    targets = (mix.at[0, 0], outward.at[0], gates.at[0], down.at[0])
    others = (None, outward.at[1], gates.at[1], down.at[1])
    own = []
    firsts = (0, 5, 6, 8)
    packed = []
    for mask in range(RANKS):
        there = place.flip(mask)
        here = []
        for slot, (at, to, width) in enumerate(first_columns(there)[0]):
            copy = pltpu.make_async_copy(
                w_ref.at[:, columns(at, width)], pack.at[mask, :, pl.ds(to, width)], pack_sem.at[mask, slot]
            )
            copy.start()
            here.append(copy)
        packed.append(here)
    own_mix = pltpu.make_async_copy(pack.at[0], mix.at[0, 0, me], local.at[0])
    def send_group(group):
        flights = []
        for mask in range(1, RANKS):
            there = place.flip(mask)
            for slot, (at, to, width) in enumerate(first_columns(there)[group]):
                copy = remote(
                    w_ref.at[:, columns(at, width)],
                    targets[group].at[me, :, pl.ds(to, width)],
                    send.at[firsts[group] + slot, mask - 1],
                    recv.at[group, mask - 1],
                    place.peer(mask),
                )
                copy.start()
                flights.append(copy)
        return flights

    def got(group, mask):
        block = targets[group].at[place.flip(mask)]
        remote(block, block, send.at[0, mask - 1], recv.at[group, mask - 1], place.peer(mask)).wait_recv()

    sent = []
    onward = []

    def forward(mask):
        block = mix.at[0, 0, place.flip(mask)] if mask else pack.at[0]
        for shift in range(1, copies):
            copy = remote(
                block, mix.at[0, copies - shift, place.flip(mask)],
                copy_send.at[shift - 1, mask], copy_recv.at[copies - shift - 1, mask],
                place.copy_at(shift),
            )
            copy.start()
            onward.append(copy)
        copy = remote(
            block, mix.at[1, 0, place.flip(mask)], core_send.at[0, mask], core_recv.at[0, mask],
            place.sibling(),
        )
        copy.start()
        onward.append(copy)

    for mask in range(1, RANKS):
        for copy in packed[mask]:
            copy.wait()
        copy = remote(
            pack.at[mask], mix.at[0, 0, me], send.at[0, mask - 1], recv.at[0, mask - 1], place.peer(mask)
        )
        copy.start()
        sent.append(copy)
    for copy in packed[0]:
        copy.wait()
    own_mix.start()
    forward(0)
    turns = []
    for row, (source, target) in enumerate(((x_ref, xall.at[me]), (x_ref, x_own), (dy_ref, dy_own))):
        here = []
        for slot, (at, to, width) in enumerate(feature_blocks(place)):
            copy = pltpu.make_async_copy(
                source.at[:, columns(at, width)], target.at[:, pl.ds(to, width)], turned.at[row, slot]
            )
            copy.start()
            here.append(copy)
        turns.append(here)
    own_s = pltpu.make_async_copy(s_ref, sall.at[me], local.at[10])
    own_s.start()

    for group in range(1, 4):
        here = []
        for slot, (at, to, width) in enumerate(first_columns(me)[group]):
            copy = pltpu.make_async_copy(
                w_ref.at[:, columns(at, width)], targets[group].at[me, :, pl.ds(to, width)],
                local.at[firsts[group] + slot],
            )
            copy.start()
            here.append(copy)
        own.append(here)
    own_s.wait()
    seg_flights = []
    for mask in range(1, RANKS):
        copy = remote(s_ref, sall.at[me], seg_send.at[mask - 1], seg_recv.at[mask - 1], place.peer(mask))
        copy.start()
        seg_flights.append(copy)
    for mask in range(1, RANKS):
        got(0, mask)
        forward(mask)
    for copy in turns[0]:
        copy.wait()
    gather = Gather(place, xall, parts, MEET_EARLY, ag_send, ag_recv)
    for part in range(len(parts)):
        gather.start(part, 0)
    for group in range(1, 4):
        sent = sent + send_group(group)
    for stage in range(3):
        for part in range(len(parts)):
            gather.landed(part, stage)
            if stage < 2:
                gather.start(part, stage + 1)
    for shift in range(1, copies):
        for mask in range(RANKS):
            block = mix.at[0, shift, place.flip(mask)]
            remote(
                block, block, copy_send.at[shift - 1, mask], copy_recv.at[shift - 1, mask], place.copy_at(shift)
            ).wait_recv()
            copy = remote(
                block, mix.at[1, shift, place.flip(mask)],
                core_send.at[shift, mask], core_recv.at[shift, mask], place.sibling(),
            )
            copy.start()
            onward.append(copy)
    for group in range(1, 4):
        for copy in own[group - 1]:
            copy.wait()
        for mask in range(RANKS):
            if mask:
                got(group, mask)
            copy = remote(
                targets[group].at[place.flip(mask)], others[group].at[place.flip(mask)],
                side_send.at[group - 1, mask], side_recv.at[group - 1, mask], place.sibling(),
            )
            copy.start()
            onward.append(copy)
    for group in range(1, 4):
        for mask in range(RANKS):
            block = others[group].at[place.flip(mask)]
            remote(
                block, block, side_send.at[group - 1, mask], side_recv.at[group - 1, mask], place.sibling()
            ).wait_recv()
    for shift in range(copies):
        for mask in range(RANKS):
            block = mix.at[1, shift, place.flip(mask)]
            remote(
                block, block, core_send.at[shift, mask], core_recv.at[shift, mask], place.sibling()
            ).wait_recv()
    for copy in seg_flights:
        copy.wait()
    own_mix.wait()
    for here in turns[1:]:
        for copy in here:
            copy.wait()
    for copy in sent + onward:
        copy.wait_send()
    gather.finish()


def any_spec():
    return pl.BlockSpec(memory_space=pl.ANY)


def vmem_spec():
    return pl.BlockSpec(memory_space=pltpu.VMEM)


def takes(micros):
    return pl.CostEstimate(flops=0, bytes_accessed=int(micros * 1e3), transcendentals=0)


def dma(*shape):
    return pltpu.SemaphoreType.DMA(shape)


def spread(copies, weights, x, dy, seg):
    rows = weights.shape[0]
    tokens = x.shape[0]
    shape = jax.ShapeDtypeStruct
    return pl.pallas_call(
        functools.partial(spread_kernel, copies, ((0, tokens // 2), (tokens // 2, tokens // 2))),
        out_shape=(
            shape((2, copies, RANKS, rows, MIXW), BF),
            shape((2, RANKS, rows, OW), BF),
            shape((2, RANKS, rows, 2 * FW), BF),
            shape((2, RANKS, rows, FW), BF),
            shape((RANKS, tokens, D), BF),
            shape((RANKS,) + seg.shape, seg.dtype),
            shape((tokens, D), BF),
            shape((tokens, D), BF),
        ),
        in_specs=[any_spec(), vmem_spec(), vmem_spec(), any_spec()],
        out_specs=[any_spec()] * 8,
        scratch_shapes=[
            pltpu.VMEM((RANKS, rows, MIXW), BF), dma(RANKS, 5), dma(11), dma(9, RANKS - 1), dma(4, RANKS - 1),
            dma(RANKS - 1), dma(RANKS - 1), dma(3, 7), dma(3, 7),
            dma(copies - 1, RANKS), dma(copies - 1, RANKS), dma(copies, RANKS), dma(copies, RANKS),
            dma(3, RANKS), dma(3, RANKS), dma(3, 4 * copies),
        ],
        compiler_params=pltpu.CompilerParams(collective_id=1, has_side_effects=True),
        cost_estimate=takes(5),
        name="spread",
    )(weights, x, dy, seg)


def norm_scale(values, epsilon):
    return lax.rsqrt(jnp.mean(values * values, axis=-1, keepdims=True) + epsilon)


def sum_then_gather(scatter, gather, finish_rows):
    parts = range(len(scatter.parts))
    for part in parts:
        scatter.start(part, 0)
    for stage in range(2):
        for part in parts:
            scatter.add(part, stage)
            scatter.start(part, stage + 1)
    for part in parts:
        finish_rows(part, scatter.add(part, 2))
        gather.start(part, 0)
    for stage in range(3):
        for part in parts:
            gather.landed(part, stage)
            if stage < 2:
                gather.start(part, stage + 1)
    scatter.finish()
    gather.finish()


def branch_kernel(copies, parts, part_ref, x_ref, gain_ref, hidden_ref, nall, land,
                  send, recv, ag_send, ag_recv):
    place = Place(copies)
    meet([place.peer(mask) for mask in (4, 2, 1)])
    me = place.rank
    scatter = Scatter(place, part_ref, land, parts, SPLIT, send, recv)
    gather = Gather(place, nall, parts, MEET, ag_send, ag_recv)

    def finish_rows(part, total):
        first, rows = parts[part]
        hidden = x_ref[pl.ds(first, rows)].astype(F32) + total
        hidden_ref[pl.ds(first, rows)] = hidden
        unit = hidden * norm_scale(hidden, EPS_NORM)
        nall[me, pl.ds(first, rows)] = (unit * gain_ref[...]).astype(BF)

    sum_then_gather(scatter, gather, finish_rows)


def cube_scratch(tokens):
    return [pltpu.VMEM((7, tokens, D), BF), dma(3, 7), dma(3, 7)]


BIG = 56 * 2**20


def branch(copies, partial, x, gain):
    tokens = x.shape[0]
    shape = jax.ShapeDtypeStruct
    return pl.pallas_call(
        functools.partial(branch_kernel, copies, row_parts(tokens, 3)),
        out_shape=(shape((tokens, D), F32), shape((RANKS, tokens, D), BF)),
        in_specs=[vmem_spec()] * 3,
        out_specs=[vmem_spec()] * 2,
        scratch_shapes=cube_scratch(tokens) + [dma(3, 7), dma(3, 7)],
        compiler_params=pltpu.CompilerParams(collective_id=2, has_side_effects=True, vmem_limit_bytes=BIG),
        cost_estimate=takes(5),
        name="branch",
    )(partial, x, gain)


def norm_back(grad, values, gain, epsilon):
    scale = norm_scale(values, epsilon)
    unit = values * scale
    scaled = grad * gain
    back = scale * (scaled - unit * jnp.mean(scaled * unit, axis=1, keepdims=True))
    return back, grad * unit


def hidden_back_kernel(copies, parts, part_ref, h_ref, dy_ref, gain_ref, dh_ref, gain_grad, dall, land,
                       send, recv, ag_send, ag_recv):
    place = Place(copies)
    meet([place.peer(mask) for mask in (4, 2, 1)])
    me = place.rank
    scatter = Scatter(place, part_ref, land, parts, SPLIT, send, recv)
    gather = Gather(place, dall, parts, MEET, ag_send, ag_recv)
    gain_grad[...] = jnp.zeros_like(gain_grad)

    def finish_rows(part, total):
        first, rows = parts[part]
        back, gain_part = norm_back(total, h_ref[pl.ds(first, rows)], gain_ref[...], EPS_NORM)
        back = dy_ref[pl.ds(first, rows)].astype(F32) + back
        dh_ref[pl.ds(first, rows)] = back
        dall[me, pl.ds(first, rows)] = back.astype(BF)
        gain_grad[...] += jnp.sum(gain_part, axis=0, keepdims=True)

    sum_then_gather(scatter, gather, finish_rows)


def hidden_back(copies, partial, hidden, dy, gain):
    tokens = dy.shape[0]
    shape = jax.ShapeDtypeStruct
    return pl.pallas_call(
        functools.partial(hidden_back_kernel, copies, row_parts(tokens, 3)),
        out_shape=(shape((tokens, D), F32), shape((1, D), F32), shape((RANKS, tokens, D), BF)),
        in_specs=[vmem_spec()] * 4,
        out_specs=[vmem_spec()] * 3,
        scratch_shapes=cube_scratch(tokens) + [dma(3, 7), dma(3, 7)],
        compiler_params=pltpu.CompilerParams(collective_id=3, has_side_effects=True, vmem_limit_bytes=BIG),
        cost_estimate=takes(5),
        name="hidden_back",
    )(partial, hidden, dy, gain)


class Home:
    def __init__(self, place, groups, ins, out, local, send, recv):
        self.place, self.groups, self.ins, self.out = place, groups, ins, out
        self.local, self.send, self.recv = local, send, recv

    def pieces(self, rank):
        found = []
        for group, source in zip(self.groups, self.ins):
            for at, to, width in first_columns(rank)[group]:
                if group == 0 and to == 2 * QW + 2 * VW:
                    continue
                if group == 2:
                    found.append((source[to // FW], 0, at, width - 128, False))
                    found.append((source[to // FW], width - 128, at + width - 128, 128, True))
                elif group == 3:
                    found.append((source, 0, at, width - 128, False))
                    found.append((source, width - 128, at + width - 128, 128, True))
                else:
                    found.append((source, to, at, width, False))
        return found

    def when(self, flag, rank, act):
        if flag:
            pl.when(rank < FULL_RANKS)(act)
        else:
            act()

    def run(self, method):
        place = self.place
        me = place.rank
        for slot, (source, to, at, width, flag) in enumerate(self.pieces(me)):
            copy = pltpu.make_async_copy(
                source.at[me, :, pl.ds(to, width)],
                self.out.at[:, columns(at, width)],
                self.local.at[slot],
            )
            self.when(flag, me, getattr(copy, method))
        for mask in range(1, RANKS):
            there = place.flip(mask)
            for slot, (source, to, at, width, flag) in enumerate(self.pieces(me)):
                copy = remote(
                    source.at[there, :, pl.ds(to, width)],
                    self.out.at[:, columns(at, width)],
                    self.send.at[mask - 1, slot],
                    self.recv.at[mask - 1, slot],
                    place.peer(mask),
                )
                self.when(flag, me, copy.start if method == "start" else copy.wait_send)
            if method == "wait":
                for slot, (source, to, at, width, flag) in enumerate(self.pieces(there)):
                    block = self.out.at[:, columns(at, width)]
                    copy = remote(
                        block, block, self.send.at[mask - 1, slot], self.recv.at[mask - 1, slot], place.peer(mask)
                    )
                    self.when(flag, there, copy.wait_recv)


def home_scratch():
    return [dma(7), dma(RANKS - 1, 7), dma(RANKS - 1, 7)]


def home_kernel(copies, mix_ref, extra_ref, out, extra_out, local, send, recv, land, own, far, near):
    place = Place(copies)
    meet([place.peer(mask) for mask in range(1, RANKS)])
    way = Home(place, (0,), (mix_ref,), out, local, send, recv)
    flights = []
    for mask in range(1, RANKS):
        copy = remote(
            extra_ref.at[place.flip(mask)], land.at[mask - 1], far.at[mask - 1], near.at[mask - 1], place.peer(mask)
        )
        copy.start()
        flights.append(copy)
    way.run("start")
    mine = pltpu.make_async_copy(extra_ref.at[place.rank], own, local.at[6])
    mine.start()
    mine.wait()
    total = own[...]
    for mask in range(1, RANKS):
        flights[mask - 1].wait_recv()
        total = total + land[mask - 1]
    extra_out[...] = total
    for copy in flights:
        copy.wait_send()
    way.run("wait")


def home(copies, array, extra):
    rows = array.shape[1]
    shape = jax.ShapeDtypeStruct
    return pl.pallas_call(
        functools.partial(home_kernel, copies),
        out_shape=(shape((rows, MIX_END), BF), shape((rows, EXTRA), F32)),
        in_specs=[any_spec()] * 2,
        out_specs=(any_spec(), vmem_spec()),
        scratch_shapes=home_scratch()
        + [pltpu.VMEM((RANKS - 1, rows, EXTRA), F32), pltpu.VMEM((rows, EXTRA), F32), dma(RANKS - 1), dma(RANKS - 1)],
        compiler_params=pltpu.CompilerParams(collective_id=6, has_side_effects=True),
        cost_estimate=takes(5),
        name="home",
    )(array, extra)


def home_rest_kernel(copies, out_rows, gate_rows, up_rows, down_rows, rest, local, send, recv):
    place = Place(copies)
    meet([place.peer(mask) for mask in range(1, RANKS)])
    way = Home(place, (1, 2, 3), (out_rows, (gate_rows, up_rows), down_rows), rest, local, send, recv)
    way.run("start")
    way.run("wait")


def home_rest(copies, grad_rows):
    rows = grad_rows[0].shape[1]
    return pl.pallas_call(
        functools.partial(home_rest_kernel, copies),
        out_shape=jax.ShapeDtypeStruct((rows, EXTRA_START), BF),
        in_specs=[any_spec()] * 4,
        out_specs=any_spec(),
        scratch_shapes=home_scratch(),
        compiler_params=pltpu.CompilerParams(collective_id=4, has_side_effects=True),
        cost_estimate=takes(5),
        name="home_rest",
    )(*grad_rows)


def dot(left, right, axes):
    return lax.dot_general(left, right, (axes, ((), ())), preferred_element_type=F32)


def halves(values):
    high = values.astype(BF)
    return high, (values - high.astype(F32)).astype(BF)


def mul(left, right, axes):
    left_high, left_low = halves(left)
    right_high, right_low = halves(right)
    return dot(left_high, right_high, axes) + (dot(left_high, right_low, axes) + dot(left_low, right_high, axes))


def mul_mask(mask, right, axes):
    right_high, right_low = halves(right)
    return dot(mask, right_high, axes) + dot(mask, right_low, axes)


NN = ((1,), (0,))
NT = ((1,), (1,))
TN = ((0,), (0,))


def unit_lower_inverses(lowers, row, col):
    size = lowers[0].shape[0]
    pair = (row >> 1) == (col >> 1)
    inverses = [jnp.where(row == col, 1.0, jnp.where(pair, -lower, 0.0)) for lower in lowers]
    level = 1
    while 2**level < size:
        joined = ((row >> (level + 1)) == (col >> (level + 1))) & ((row >> level) != (col >> level))
        parts = [mul(jnp.where(joined, lower, 0.0), inverse, NN) for lower, inverse in zip(lowers, inverses)]
        inverses = [inverse - mul(inverse, part, NN) for inverse, part in zip(inverses, parts)]
        level = level + 1
    return inverses


class Sequence:
    def __init__(self, seg_row):
        tokens = seg_row.shape[1]
        self.tokens = tokens
        shape = (tokens, tokens)
        self.row = lax.broadcasted_iota(jnp.int32, shape, 0)
        self.col = lax.broadcasted_iota(jnp.int32, shape, 1)
        ids = jnp.broadcast_to(seg_row.astype(F32), shape)
        turned = ids.T
        same = turned == ids
        self.inclusive = same & (self.row >= self.col)
        self.strict = same & (self.row > self.col)
        self.lower = (self.row >= self.col).astype(BF)
        column = turned[:, :1]
        at = self.row[:, :1]
        self.near = [None]
        for back in range(1, CONV):
            before = pltpu.roll(turned, back, 0)[:, :1]
            self.near.append(((before == column) & (at >= back)).astype(F32))

    def conv(self, taps, values):
        total = taps[CONV - 1 : CONV] * values
        for back in range(1, CONV):
            total = total + taps[CONV - 1 - back : CONV - back] * (
                self.near[back] * pltpu.roll(values, back, 0)
            )
        return total

    def conv_back(self, taps, values, grad):
        total = taps[CONV - 1 : CONV] * grad
        rows = [jnp.sum(values * grad, axis=0, keepdims=True)]
        for back in range(1, CONV):
            masked = self.near[back] * grad
            total = total + taps[CONV - 1 - back : CONV - back] * pltpu.roll(
                masked, self.tokens - back, 0
            )
            rows.append(jnp.sum(masked * pltpu.roll(values, back, 0), axis=0, keepdims=True))
        return total, jnp.concatenate(rows[::-1], axis=0)


def pick_lane(block, lane):
    at = lax.broadcasted_iota(jnp.int32, block.shape, 1)
    return jnp.sum(jnp.where(at == lane, block, 0.0), axis=1, keepdims=True)


def softplus(values):
    return jnp.maximum(values, 0.0) + jnp.log1p(jnp.exp(-jnp.abs(values)))


class Head:
    def __init__(self, seq, head, rank, scalars, p_ref, taps_ref):
        q_at, k_at = head * DK, QW + head * DK
        v_at, g_at = 2 * QW + head * DV, 2 * QW + VW + head * DV
        self.q_at, self.k_at, self.v_at, self.g_at = q_at, k_at, v_at, g_at
        self.raw = [p_ref[:, q_at : q_at + DK], p_ref[:, k_at : k_at + DK], p_ref[:, v_at : v_at + DV]]
        self.taps = [taps_ref[:, q_at : q_at + DK], taps_ref[:, k_at : k_at + DK], taps_ref[:, v_at : v_at + DV]]
        self.pre = [seq.conv(taps, raw) for taps, raw in zip(self.taps, self.raw)]
        self.sig = [jax.nn.sigmoid(pre) for pre in self.pre]
        conv_q, conv_k, self.v = [pre * sig for pre, sig in zip(self.pre, self.sig)]
        self.q_scale = lax.rsqrt(jnp.sum(conv_q * conv_q, axis=1, keepdims=True) + EPS_NORM)
        self.k_scale = lax.rsqrt(jnp.sum(conv_k * conv_k, axis=1, keepdims=True) + EPS_NORM)
        self.q_unit = conv_q * self.q_scale
        self.q = self.q_unit * DK**-0.5
        self.k = conv_k * self.k_scale
        pair = p_ref[:, 2 * QW + 2 * VW :]
        self.lane_a = rank * HEADS + head
        self.lane_b = H + rank * HEADS + head
        self.a = pick_lane(pair, self.lane_a) + scalars[HEADS + head]
        self.rate = scalars[head]
        self.beta = jax.nn.sigmoid(pick_lane(pair, self.lane_b))
        self.decay = -self.rate * softplus(self.a)
        spread_out = jnp.where(seq.row > seq.col, jnp.broadcast_to(self.decay, seq.row.shape), 0.0)
        gap = mul_mask(seq.lower, spread_out, NN)
        self.pairs = jnp.where(seq.inclusive, jnp.exp(jnp.where(seq.inclusive, gap, 0.0)), 0.0)
        self.kk = mul(self.k, self.k, NT)
        self.qk = mul(self.q, self.k, NT)
        self.strict_pairs = jnp.where(seq.strict, self.pairs, 0.0)
        self.lower = self.beta * self.strict_pairs * self.kk
        self.attend = self.pairs * self.qk
        self.gate = p_ref[:, g_at : g_at + DV]


def mixer_kernel(rank_ref, scalars, seg_ref, p_ref, taps_ref, gain_ref, z_ref, inv_ref, upd_ref):
    seq = Sequence(seg_ref[0, :1])
    rank = rank_ref[0]
    ones = [Head(seq, head, rank, scalars, p_ref, taps_ref) for head in range(HEADS)]
    inverses = unit_lower_inverses([one.lower for one in ones], seq.row, seq.col)
    updates = [mul(inverse, one.beta * one.v, NN) for inverse, one in zip(inverses, ones)]
    outs = [mul(one.attend, update, NN) for one, update in zip(ones, updates)]
    for head, (one, inverse, update, out) in enumerate(zip(ones, inverses, updates, outs)):
        normed = out * norm_scale(out, EPS_GATED) * gain_ref[...]
        z_ref[:, head * DV : (head + 1) * DV] = (normed * (one.gate * jax.nn.sigmoid(one.gate))).astype(BF)
        inv_ref[0, head] = inverse
        upd_ref[0, head] = update


def mixer_back_kernel(rank_ref, scalars, seg_ref, p_ref, taps_ref, gain_ref, inv_ref, upd_ref, dz_ref,
                      dp_ref, dtaps_ref, dgain_ref, dscal_ref):
    @pl.when(pl.program_id(0) == 0)
    def _():
        dtaps_ref[...] = jnp.zeros_like(dtaps_ref)
        dgain_ref[...] = jnp.zeros_like(dgain_ref)
        dscal_ref[...] = jnp.zeros_like(dscal_ref)

    seq = Sequence(seg_ref[0, :1])
    rank = rank_ref[0]
    pair_grad = jnp.zeros((seq.tokens, EXTRA), F32)
    lane = lax.broadcasted_iota(jnp.int32, (seq.tokens, EXTRA), 1)
    scal_row = lax.broadcasted_iota(jnp.int32, (8, 128), 0)
    scal_col = lax.broadcasted_iota(jnp.int32, (8, 128), 1)
    scal = jnp.zeros((8, 128), F32)
    for head in range(HEADS):
        one = Head(seq, head, rank, scalars, p_ref, taps_ref)
        inverse = inv_ref[0, head]
        update = upd_ref[0, head]
        out = mul(one.attend, update, NN)
        dz = dz_ref[:, head * DV : (head + 1) * DV]
        scale = norm_scale(out, EPS_GATED)
        normed = out * scale
        sig = jax.nn.sigmoid(one.gate)
        gate = one.gate * sig
        d_gate = dz * normed * gain_ref[...] * (sig * (1 + one.gate * (1 - sig)))
        dp_ref[:, one.g_at : one.g_at + DV] = d_gate.astype(BF)
        dgain_ref[...] += jnp.sum(dz * normed * gate, axis=0, keepdims=True)
        d_normed = dz * gain_ref[...] * gate
        d_out = scale * (d_normed - normed * jnp.mean(d_normed * normed, axis=1, keepdims=True))
        d_attend = jnp.where(seq.inclusive, mul(d_out, update, NT), 0.0)
        d_update = mul(one.attend, d_out, TN)
        d_scaled = mul(inverse, d_update, TN)
        d_lower = jnp.where(seq.strict, -mul(d_scaled, update, NT), 0.0)
        d_v = one.beta * d_scaled
        d_beta = jnp.sum(d_scaled * one.v, axis=1, keepdims=True) + jnp.sum(
            d_lower * one.strict_pairs * one.kk, axis=1, keepdims=True
        )
        d_gap = d_attend * one.attend + d_lower * one.lower
        d_qk = d_attend * one.pairs
        d_kk = d_lower * (one.beta * one.strict_pairs)
        d_q = mul(d_qk, one.k, NN)
        d_k = mul(d_qk, one.q, TN) + mul(d_kk, one.k, NN) + mul(d_kk, one.k, TN)
        reach = mul_mask(seq.lower, d_gap, TN)
        d_decay = jnp.sum(jnp.where(seq.row > seq.col, reach, 0.0), axis=1, keepdims=True)
        d_a = d_decay * (-one.rate) * jax.nn.sigmoid(one.a)
        d_b = d_beta * one.beta * (1 - one.beta)
        pair_grad = pair_grad + jnp.where(lane == one.lane_a, d_a, 0.0) + jnp.where(lane == one.lane_b, d_b, 0.0)
        sum_rate = jnp.sum(d_decay * one.decay, axis=0, keepdims=True)
        sum_a = jnp.sum(d_a, axis=0, keepdims=True)
        scal = scal + jnp.where((scal_row == 0) & (scal_col == head), sum_rate, 0.0)
        scal = scal + jnp.where((scal_row == 0) & (scal_col == HEADS + head), sum_a, 0.0)
        dq_unit = d_q * DK**-0.5
        dc_q = one.q_scale * (dq_unit - one.q_unit * jnp.sum(dq_unit * one.q_unit, axis=1, keepdims=True))
        dc_k = one.k_scale * (d_k - one.k * jnp.sum(d_k * one.k, axis=1, keepdims=True))
        for grad, pre, sig, raw, taps, at, width in (
            (dc_q, one.pre[0], one.sig[0], one.raw[0], one.taps[0], one.q_at, DK),
            (dc_k, one.pre[1], one.sig[1], one.raw[1], one.taps[1], one.k_at, DK),
            (d_v, one.pre[2], one.sig[2], one.raw[2], one.taps[2], one.v_at, DV),
        ):
            d_pre = grad * (sig * (1 + pre * (1 - sig)))
            d_raw, d_taps = seq.conv_back(taps, raw, d_pre)
            dp_ref[:, at : at + width] = d_raw.astype(BF)
            dtaps_ref[:, at : at + width] += d_taps
    dp_ref[:, 2 * QW + 2 * VW :] = pair_grad.astype(BF)
    dscal_ref[...] += scal


def smem_spec():
    return pl.BlockSpec(memory_space=pltpu.SMEM)


def by_sequence(*shape):
    rest = (0,) * (len(shape) - 1)
    return pl.BlockSpec(shape, lambda at: (at,) + rest)


def whole_block(*shape):
    return pl.BlockSpec(shape, lambda at: (0,) * len(shape))


CHANNELS = 2 * QW + VW


def mixer(rank, scalars, seg, p, taps, gain, tokens):
    count = p.shape[0] // tokens
    shape = jax.ShapeDtypeStruct
    return pl.pallas_call(
        mixer_kernel,
        grid=(count,),
        out_shape=(
            shape((p.shape[0], VW), BF),
            shape((count, HEADS, tokens, tokens), F32),
            shape((count, HEADS, tokens, DV), F32),
        ),
        in_specs=[
            smem_spec(), smem_spec(), by_sequence(1, 8, tokens), by_sequence(tokens, MIXW),
            whole_block(CONV, CHANNELS), whole_block(1, DV),
        ],
        out_specs=[
            by_sequence(tokens, VW), by_sequence(1, HEADS, tokens, tokens), by_sequence(1, HEADS, tokens, DV),
        ],
        compiler_params=pltpu.CompilerParams(vmem_limit_bytes=40 * 2**20),
        cost_estimate=takes(5),
        name="mixer",
    )(rank, scalars, seg, p, taps, gain)


def mixer_back(rank, scalars, seg, p, taps, gain, inverse, update, dz, tokens):
    count = p.shape[0] // tokens
    shape = jax.ShapeDtypeStruct
    return pl.pallas_call(
        mixer_back_kernel,
        grid=(count,),
        out_shape=(
            shape((p.shape[0], MIXW), BF),
            shape((CONV, CHANNELS), F32),
            shape((1, DV), F32),
            shape((8, 128), F32),
        ),
        in_specs=[
            smem_spec(), smem_spec(), by_sequence(1, 8, tokens), by_sequence(tokens, MIXW),
            whole_block(CONV, CHANNELS), whole_block(1, DV),
            by_sequence(1, HEADS, tokens, tokens), by_sequence(1, HEADS, tokens, DV), by_sequence(tokens, VW),
        ],
        out_specs=[
            by_sequence(tokens, MIXW), whole_block(CONV, CHANNELS), whole_block(1, DV), whole_block(8, 128),
        ],
        compiler_params=pltpu.CompilerParams(vmem_limit_bytes=40 * 2**20),
        cost_estimate=takes(5),
        name="mixer_back",
    )(rank, scalars, seg, p, taps, gain, inverse, update, dz)


def adam_kernel(filled, scalars, grad_ref, one_ref, two_ref, master_ref, *refs):
    grad_out, one_out, two_out, master_out, weight_out = refs[filled:]
    beta_one, beta_two, rate = scalars[0], scalars[1], scalars[2]
    grad = grad_ref[...].astype(F32)
    one = beta_one * one_ref[...] + (1 - beta_one) * grad
    two = beta_two * two_ref[...] + (1 - beta_two) * grad * grad
    master = master_ref[...]
    change = (one / scalars[3]) / (jnp.sqrt(two / scalars[4]) + EPS_ADAM) + DECAY_WEIGHT * master
    master = master - rate * change
    grad_out[...] = grad
    one_out[...] = one
    two_out[...] = two
    master_out[...] = master
    weight_out[...] = master.astype(BF)


def adam(scalars, grads, state, done, first, width, count):
    rows = grads.shape[0]
    at_first = first // width
    grad_first = at_first if grads.shape[1] > first else 0
    shape = jax.ShapeDtypeStruct
    there = pl.BlockSpec((rows, width), lambda at: (0, at + at_first))
    filled = () if done is None else tuple(done)
    return pl.pallas_call(
        functools.partial(adam_kernel, len(filled)),
        grid=(count,),
        out_shape=(shape((rows, COLS), F32),) * 4 + (shape((rows, COLS), BF),),
        in_specs=[smem_spec(), pl.BlockSpec((rows, width), lambda at: (0, at + grad_first))]
        + [there] * 3 + [any_spec()] * len(filled),
        out_specs=[there] * 5,
        input_output_aliases={5 + at: at for at in range(len(filled))},
        compiler_params=pltpu.CompilerParams(vmem_limit_bytes=40 * 2**20),
        cost_estimate=takes(5),
        name="adam",
    )(scalars, grads, *state, *filled)


def weight_grad_kernel(left_ref, right_ref, *refs):
    total = dot(left_ref[...], right_ref[...], TN)
    for ref in refs[:-1]:
        total = total + ref[...].astype(F32)
    refs[-1][...] = total.astype(BF)


def weight_grad(left, right, at, width, adds=()):
    tokens, count = right.shape
    tile = 768 if count % 768 == 0 else count

    def add_spec(row, column):
        return pl.BlockSpec((width, tile), lambda step: (row, step + column // tile))

    return pl.pallas_call(
        weight_grad_kernel,
        grid=(count // tile,),
        out_shape=jax.ShapeDtypeStruct((width, count), BF),
        in_specs=[
            pl.BlockSpec((tokens, width), lambda step: (0, at)),
            pl.BlockSpec((tokens, tile), lambda step: (0, step)),
        ]
        + [add_spec(row, column) for _, row, column in adds],
        out_specs=pl.BlockSpec((width, tile), lambda step: (0, step)),
        compiler_params=pltpu.CompilerParams(vmem_limit_bytes=40 * 2**20),
        cost_estimate=takes(1),
        name="weight_grad",
    )(left, right, *[array for array, _, _ in adds])


def input_back_kernel(grad_ref, w_ref, x_ref, scale_ref, out_ref, gain_ref):
    grad = dot(grad_ref[...], w_ref[...], NT)
    out_ref[...] = grad.astype(BF)
    unit = x_ref[...].astype(F32) * scale_ref[:, :1]
    gain_ref[...] = jnp.sum(grad * unit, axis=0, keepdims=True)


def input_back(grad, w, x, scale):
    tokens, count = grad.shape
    tile = 512
    shape = jax.ShapeDtypeStruct
    return pl.pallas_call(
        input_back_kernel,
        grid=(D // tile,),
        out_shape=(shape((tokens, D), BF), shape((1, D), F32)),
        in_specs=[
            whole_block(tokens, count),
            pl.BlockSpec((tile, count), lambda step: (step, 0)),
            pl.BlockSpec((tokens, tile), lambda step: (0, step)),
            whole_block(tokens, 128),
        ],
        out_specs=[
            pl.BlockSpec((tokens, tile), lambda step: (0, step)), pl.BlockSpec((1, tile), lambda step: (0, step)),
        ],
        compiler_params=pltpu.CompilerParams(vmem_limit_bytes=48 * 2**20),
        cost_estimate=takes(1),
        name="input_back",
    )(grad, w, x, scale)


def project_kernel(x_ref, w_ref, normed_ref, p_ref, gains_ref, scale_ref, gain):
    @pl.when(pl.program_id(0) == 0)
    def _():
        row = lax.broadcasted_iota(jnp.int32, (8, EXTRA), 0)
        col = lax.broadcasted_iota(jnp.int32, (8, EXTRA), 1)
        pick = (col == row + 2 * H).astype(BF)
        gain[...] = dot(pick, w_ref[:, MIXW - EXTRA :], NT)
        gains_ref[...] = gain[...]

    x = x_ref[...].astype(F32)
    scale = norm_scale(x, EPS_NORM)
    scale_ref[...] = jnp.broadcast_to(scale, scale_ref.shape)
    normed = (x * scale * gain[:1]).astype(BF)
    normed_ref[...] = normed
    p_ref[...] = dot(normed, w_ref[...], NN)


def project(x, w):
    count = x.shape[0]
    rows = 256
    shape = jax.ShapeDtypeStruct
    return pl.pallas_call(
        project_kernel,
        grid=(count // rows,),
        out_shape=(shape((count, D), BF), shape((count, MIXW), F32), shape((8, D), F32), shape((count, 128), F32)),
        in_specs=[by_sequence(rows, D), whole_block(D, MIXW)],
        out_specs=[by_sequence(rows, D), by_sequence(rows, MIXW), whole_block(8, D), by_sequence(rows, 128)],
        scratch_shapes=[pltpu.VMEM((8, D), F32)],
        compiler_params=pltpu.CompilerParams(vmem_limit_bytes=40 * 2**20),
        cost_estimate=takes(1),
        name="project",
    )(x, w)


def finish_kernel(copies, at_ref, hidden_ref, feed_ref, grad_ref, x_ref, d_hidden_ref, gain_ref, out_ref, in_grad_ref):
    out = (hidden_ref[...] + feed_ref[...].astype(F32)).astype(BF)
    back, _ = norm_back(grad_ref[...].astype(F32), x_ref[...].astype(F32), gain_ref[...], EPS_NORM)
    in_grad = (d_hidden_ref[...] + back).astype(BF)
    width = D // (4 * copies)
    for core in range(2):
        for copy in range(copies):
            for x in range(2):
                block = (x * 2 + (at_ref[0] + core) % 2) * copies + (at_ref[1] + copy) % copies
                to = pl.ds(pl.multiple_of(block * width, 128), width)
                at = ((core * copies + copy) * 2 + x) * width
                out_ref[:, to] = out[:, at : at + width]
                in_grad_ref[:, to] = in_grad[:, at : at + width]


def finish(place, copies, hidden, feed, grad, x, d_hidden, gain):
    shape = jax.ShapeDtypeStruct(x.shape, BF)
    return pl.pallas_call(
        functools.partial(finish_kernel, copies),
        out_shape=(shape, shape),
        in_specs=[smem_spec()] + [vmem_spec()] * 6,
        out_specs=[vmem_spec()] * 2,
        compiler_params=pltpu.CompilerParams(vmem_limit_bytes=40 * 2**20),
        cost_estimate=takes(1),
        name="finish",
    )(place, hidden, feed, grad, x, d_hidden, gain)


def turn(blocks, shift, axis):
    size = blocks.shape[axis]
    twice = jnp.concatenate([blocks, blocks], axis=axis)
    return lax.dynamic_slice_in_dim(twice, shift % size, size, axis)


class Order:
    def __init__(self, copies, core, dp):
        self.copies, self.core, self.dp = copies, core, dp

    def relative(self, values, axis):
        lead, tail = values.shape[:axis], values.shape[axis + 1 :]
        whole = values.reshape(lead + (2, 2, self.copies, D // (4 * self.copies)) + tail)
        whole = turn(turn(whole, self.core, axis + 1), self.dp, axis + 2)
        whole = jnp.moveaxis(whole, axis, axis + 2)
        return whole.reshape(values.shape)

    def plain(self, values, axis):
        lead, tail = values.shape[:axis], values.shape[axis + 1 :]
        whole = values.reshape(lead + (2, self.copies, 2, D // (4 * self.copies)) + tail)
        whole = jnp.moveaxis(whole, axis + 2, axis)
        whole = turn(turn(whole, 2 - self.core, axis + 1), self.copies - self.dp, axis + 2)
        return whole.reshape(values.shape)


def on_device(inputs, cotangent, segment_ids, weights, master, moment_one, moment_two,
              step, learn_rate, beta_one, beta_two):
    tokens = inputs.shape[0]
    rows = weights.shape[0]
    replicas = lax.axis_size("rep")
    copies = replicas // 4
    members = replicas * 4
    rep = lax.axis_index("rep")
    grp = lax.axis_index("grp")
    core = grp % 2
    dp = rep // 4
    rank = rank_of(rep, grp)
    order = Order(copies, core, dp)
    axes = ("rep", "grp")
    group_tokens = RANKS * tokens
    block_rows = RANKS * rows

    def pairs_to(move):
        return [(at, move(at // 4, at % 4)) for at in range(members)]

    core_pairs = pairs_to(lambda r, g: r * 4 + (g ^ 1))
    copy_pairs = [
        pairs_to(lambda r, g, shift=shift: ((r + 4 * shift) % replicas) * 4 + g) for shift in range(1, copies)
    ]

    in_place = (D // (4 * copies)) % 128 == 0
    x, dy = (inputs, cotangent) if in_place else (order.relative(inputs, 1), order.relative(cotangent, 1))
    seg = jnp.broadcast_to(segment_ids[None, :], (8, tokens))
    mix_blocks, out_block, gate_block, down_block, x_all, seg_all, x, dy = spread(copies, weights, x, dy, seg)
    cubes = [
        [(copy * 4 + j % 4) * 4 + (j // 4) * 2 + side for j in range(RANKS)]
        for copy in range(copies)
        for side in range(2)
    ]
    dy_all = lax.all_gather(dy, axes, axis_index_groups=cubes, axis=0, tiled=True)
    x_all = x_all.reshape(group_tokens, D)
    w_mix = mix_blocks.reshape(D, MIXW)

    def from_copies(blocks):
        block = blocks[0].reshape(block_rows, blocks.shape[3])
        return [lax.ppermute(block, axes, copy_pairs[copies - shift - 1]) for shift in range(1, copies)]

    def collect(blocks, landed):
        mine = [blocks[0].reshape(block_rows, blocks.shape[3])] + landed
        theirs = [blocks[1].reshape(block_rows, blocks.shape[3])]
        theirs = theirs + [lax.ppermute(one, axes, core_pairs) for one in landed]
        return jnp.concatenate(mine + theirs, axis=0)

    together = lax.optimization_barrier
    out_landed = from_copies(out_block)
    gate_landed = from_copies(gate_block)
    down_landed = from_copies(down_block)
    normed, p, gains, x_scale = project(x_all, w_mix)
    gain_one, gain_two = gains[:1], gains[1:2]
    extra = order.plain(w_mix[:, MIXW - EXTRA :], 0).astype(F32)
    conv_cols = CONV * (2 * KD + VD) // D
    conv_at = 2 * H + 2

    tap_rows = D // CONV
    table = extra[:, conv_at : conv_at + conv_cols].reshape(CONV, tap_rows, conv_cols)
    ranges = ((0, QW), (KD, QW), (2 * KD, VW))

    def own_channels(first, width):
        return first // conv_cols + rank * (width // conv_cols), width // conv_cols

    taps = jnp.concatenate(
        [
            lax.dynamic_slice_in_dim(table, *own_channels(first, width), 1).reshape(CONV, width)
            for first, width in ranges
        ],
        axis=1,
    )
    column = extra[: 2 * H + DV, conv_at + conv_cols]
    scalars = jnp.concatenate(
        [
            jnp.exp(lax.dynamic_slice_in_dim(column, rank * HEADS, HEADS, 0)),
            lax.dynamic_slice_in_dim(column, H + rank * HEADS, HEADS, 0),
        ]
    )
    out_gain = column[2 * H : 2 * H + DV][None]
    rank_arg = jnp.reshape(rank, (1,)).astype(jnp.int32)
    gated, inverse, update = mixer(rank_arg, scalars, seg_all, p, taps, out_gain, tokens)
    w_out = collect(out_block, out_landed)
    partial = dot(gated, w_out, NT).astype(BF)
    hidden, normed_two = branch(copies, partial.reshape(RANKS, tokens, D), x, gain_two)
    normed_two = normed_two.reshape(group_tokens, D)
    normed_two, gate_landed, down_landed = together((normed_two, gate_landed, down_landed))
    w_gates = collect(gate_block, gate_landed)
    w_down = collect(down_block, down_landed)
    gate_up = dot(normed_two, w_gates, NN)
    gate_part, up_part = gate_up[:, :FW], gate_up[:, FW:]
    tile_count = jnp.where(rank < FULL_RANKS, FT, FT - 1)
    real = (jnp.arange(FW) < tile_count * 128)[None]
    sigmoid_gate = jax.nn.sigmoid(gate_part)
    activated = jnp.where(real, gate_part * sigmoid_gate * up_part, 0.0).astype(BF)
    half = copies * block_rows

    def block_of(values, at):
        return values[:, at * block_rows : (at + 1) * block_rows]

    def first_half(left, right):
        theirs = dot(left[:, half:], right, TN).astype(BF)
        return theirs, lax.ppermute(theirs, axes, core_pairs)

    def away_rows(left, right, got):
        return [
            (dot(block_of(left, at), right, TN) + got[at * block_rows : (at + 1) * block_rows].astype(F32)).astype(BF)
            for at in range(1, copies)
        ]

    def to_copies(away):
        return [lax.ppermute(one, axes, pairs) for one, pairs in zip(away, copy_pairs)]

    def for_copies(left, right, got):
        away = away_rows(left, right, got)
        return away, to_copies(away)

    down_half, down_got = first_half(dy_all, activated)
    down_half, activated = together((down_half, activated))
    feed = dot(activated, w_down, NT).astype(BF)
    d_act = dot(dy_all, w_down, NN)
    d_gate = d_act * up_part * sigmoid_gate * (1 + gate_part * (1 - sigmoid_gate))
    d_up = d_act * gate_part * sigmoid_gate
    real_two = jnp.concatenate([real, real], axis=1)
    d_gate_up = jnp.where(real_two, jnp.concatenate([d_gate, d_up], axis=1), 0.0).astype(BF)
    gate_half, gate_got = first_half(normed_two, d_gate_up)
    down_away, down_landed = for_copies(dy_all, activated, down_got)
    gate_half, down_away, d_gate_up = together((gate_half, down_away, d_gate_up))
    d_normed_two = dot(d_gate_up, w_gates, NT).astype(BF)
    d_gate_part, d_up_part = d_gate_up[:, :FW], d_gate_up[:, FW:]
    gate_away = away_rows(normed_two, d_gate_part, gate_got[:, :FW])
    up_away = away_rows(normed_two, d_up_part, gate_got[:, FW:])
    gate_away, up_away, d_normed_two = together((gate_away, up_away, d_normed_two))
    d_hidden, gain_two_grad, d_hidden_all = hidden_back(
        copies, d_normed_two.reshape(RANKS, tokens, D), hidden, dy, gain_two
    )
    d_hidden_all = d_hidden_all.reshape(group_tokens, D)
    d_hidden_all, up_away, gate_away, down_landed, feed = together((d_hidden_all, up_away, gate_away, down_landed, feed))
    feed = lax.psum_scatter(feed, axes, axis_index_groups=cubes, scatter_dimension=0, tiled=True)
    up_landed = to_copies(up_away)
    gate_landed = to_copies(gate_away)
    out_half, out_got = first_half(d_hidden_all, gated)
    out_half, d_hidden_all = together((out_half, d_hidden_all))
    d_gated = dot(d_hidden_all, w_out, NN)
    out_away = away_rows(d_hidden_all, gated, out_got)
    out_away, d_gated = together((out_away, d_gated))
    out_landed = to_copies(out_away)
    d_mix, d_taps, d_out_gain, d_scalars = mixer_back(
        rank_arg, scalars, seg_all, p, taps, out_gain, inverse, update, d_gated, tokens
    )
    d_mix, up_landed = together((d_mix, up_landed))
    d_wide = d_mix[:, : MIXW - EXTRA]
    mix_half = weight_grad(normed, d_wide, 1, half)
    mix_got = lax.ppermute(mix_half, axes, core_pairs)
    mix_half, d_mix = together((mix_half, d_mix))
    d_normed, gain_one_grad = input_back(d_mix, w_mix, x_all, x_scale)
    gain_one_grad = gain_one_grad[0]
    d_normed, gain_one_grad, mix_got, gate_landed, out_landed = together(
        (d_normed, gain_one_grad, mix_got, gate_landed, out_landed)
    )
    mix_away = [
        weight_grad(normed, d_wide, at, block_rows, ((mix_got, at, 0),)) for at in range(1, copies)
    ]
    mix_landed = to_copies(mix_away)
    d_input = lax.psum_scatter(d_normed, axes, axis_index_groups=cubes, scatter_dimension=0, tiled=True)
    mix_away, d_gate_part, d_up_part, activated, gated = together(
        (mix_away, d_gate_part, d_up_part, activated, gated)
    )

    def own_rows(left, right, got, column, landed):
        total = weight_grad(left, right, 0, block_rows, ((got, 0, column),) + tuple((one, 0, 0) for one in landed))
        return total.reshape(RANKS, rows, right.shape[1])

    up_rows = own_rows(normed_two, d_up_part, gate_got, FW, up_landed)
    gate_rows = own_rows(normed_two, d_gate_part, gate_got, 0, gate_landed)
    down_rows = own_rows(dy_all, activated, down_got, 0, down_landed)
    out_rows = own_rows(d_hidden_all, gated, out_got, 0, out_landed)
    out_rows, d_taps, d_scalars, d_out_gain, gain_two_grad = together(
        (out_rows, d_taps, d_scalars, d_out_gain, gain_two_grad)
    )
    tap_grad = jnp.zeros((CONV, tap_rows, conv_cols), F32)
    at = 0
    for first, width in ranges:
        start, count = own_channels(first, width)
        piece = d_taps[:, at : at + width].reshape(CONV, count, conv_cols)
        tap_grad = lax.dynamic_update_slice(tap_grad, piece, (0, start, 0))
        at = at + width
    small = jnp.zeros((D,), F32)
    small = lax.dynamic_update_slice(small, d_scalars[0, :HEADS], (rank * HEADS,))
    small = lax.dynamic_update_slice(small, d_scalars[0, HEADS : 2 * HEADS], (H + rank * HEADS,))
    small = lax.dynamic_update_slice(small, d_out_gain[0], (2 * H,))
    core_grad = jnp.concatenate(
        [
            jnp.zeros((D, conv_at), F32),
            tap_grad.reshape(D, conv_cols),
            small[:, None],
            jnp.zeros((D, EXTRA - conv_at - 1 - conv_cols), F32),
        ],
        axis=1,
    )
    lanes = jnp.arange(EXTRA)[None]
    extra_grad = (
        dot(normed, d_mix[:, MIXW - EXTRA :], TN)
        + jnp.where(lanes == 2 * H, gain_one_grad[:, None], 0.0)
        + jnp.where(lanes == 2 * H + 1, gain_two_grad.reshape(D, 1), 0.0)
        + order.relative(core_grad, 0)
    )
    extra_got = lax.ppermute(extra_grad[half:], axes, core_pairs)
    extra_sum = extra_grad[:half] + extra_got
    extra_landed = [
        lax.ppermute(extra_sum[at * block_rows : (at + 1) * block_rows], axes, pairs)
        for at, pairs in zip(range(1, copies), copy_pairs)
    ]
    extra_sum, out_rows = together((extra_sum, out_rows))
    grads_rest = home_rest(copies, (out_rows, gate_rows, up_rows, down_rows))
    if in_place:
        output, input_grad = finish(
            jnp.stack([core, dp]).astype(jnp.int32), copies, hidden, feed, d_input, x, d_hidden, gain_one
        )
    else:
        output = order.plain((hidden + feed.astype(F32)).astype(BF), 1)
        back, _ = norm_back(d_input.astype(F32), x.astype(F32), gain_one, EPS_NORM)
        input_grad = order.plain((d_hidden + back).astype(BF), 1)
    extra_rows = extra_sum[:block_rows]
    for one in extra_landed:
        extra_rows = extra_rows + one
    step_float = step[0].astype(F32)
    adam_scalars = jnp.stack(
        [beta_one[0], beta_two[0], learn_rate[0], 1 - beta_one[0] ** step_float, 1 - beta_two[0] ** step_float]
    )
    state = (moment_one, moment_two, master)
    done = adam(adam_scalars, grads_rest, state, None, MIX_END, 2048, 4)
    done = adam(adam_scalars, grads_rest, state, done, MIX_END + 4 * 2048, 2560, 5)
    done, extra_rows, output, input_grad, normed = together((done, extra_rows, output, input_grad, normed))
    mix_rows = own_rows(normed, d_wide, mix_got, 0, mix_landed)
    grads_mix, extra_rows = home(copies, mix_rows, extra_rows.reshape(RANKS, rows, EXTRA))
    done = adam(adam_scalars, extra_rows, state, done, EXTRA_START, EXTRA, 1)
    done = adam(adam_scalars, grads_mix, state, done, 0, 2048, 6)
    gain_grads = extra_rows[:, 2 * H : 2 * H + 2]
    return (output, input_grad) + tuple(done) + (gain_grads,)


def solution(mesh):
    by_token = P(("rep", "grp"), None)
    by_row = P(("grp", "rep"), None)
    return jax.shard_map(
        on_device,
        mesh=mesh,
        in_specs=(by_token, by_token, P(("rep", "grp")), by_row, by_row, by_row, by_row, P(), P(), P(), P()),
        out_specs=(by_token, by_token) + (by_row,) * 6,
        check_vma=False,
    )
```

```python
import functools

import jax
import jax.numpy as jnp
from jax import lax
from jax.experimental import pallas as pl
from jax.experimental.pallas import tpu as pltpu
from jax.sharding import PartitionSpec as P

D = 2048
H = 16
DK = 128
DV = 256
FF = 5632
CONV = 4
EXTRA = 128
KD = 2048
VD = 4096
MIX_END = 2 * KD + 2 * VD
FFN_START = MIX_END + VD
DOWN_START = FFN_START + 2 * FF
EXTRA_START = DOWN_START + FF
COLS = EXTRA_START + EXTRA

EPS_NORM = 1e-06
EPS_GATED = 1e-05
EPS_ADAM = 1e-08
DECAY_WEIGHT = 0.1
MESH = pl.DeviceIdType.MESH
BIG = 60 * 2**20

RANKS = 8
HEADS = H // RANKS
QW = HEADS * DK
VW = HEADS * DV
MIXW = 2 * QW + 2 * VW + EXTRA
OW = VW
TILES = FF // 128
FULL_RANKS = TILES - (TILES // RANKS) * RANKS
FT = TILES // RANKS + 1
FW = FT * 128
SPLIT = ((4, 1, 2), (1, 2, 4), (2, 4, 1))
MEET = ((2, 1, 4), (4, 2, 1), (1, 4, 2))
MEET_EARLY = ((2, 4, 1), (2, 1, 4))
BF = jnp.bfloat16
F32 = jnp.float32


def rank_of(rep, grp):
    return (grp // 2) * 4 + rep % 4


class Place:
    def __init__(self, copies):
        self.rep = lax.axis_index("rep")
        self.grp = lax.axis_index("grp")
        self.copies = copies
        self.dp = self.rep // 4
        self.core = self.grp % 2
        self.rank = rank_of(self.rep, self.grp)
        self.bits = {4: self.rank // 4, 2: self.rank // 2 % 2, 1: self.rank % 2}

    def flip(self, mask):
        total = 0
        for weight, bit in self.bits.items():
            total = total + weight * ((1 - bit) if mask & weight else bit)
        return total

    def peer(self, mask):
        rank = self.flip(mask)
        return (self.dp * 4 + rank % 4, (rank // 4) * 2 + self.core)

    def sibling(self):
        return (self.rep, self.grp + 1 - 2 * self.core)

    def copy_at(self, shift):
        return (((self.dp + shift) % self.copies) * 4 + self.rep % 4, self.grp)


def meet(devices):
    barrier = pltpu.get_barrier_semaphore()
    for device in devices:
        pl.semaphore_signal(barrier, inc=1, device_id=device, device_id_type=MESH)
    pl.semaphore_wait(barrier, len(devices))


def remote(src, dst, send, recv, device):
    return pltpu.make_async_remote_copy(
        src_ref=src, dst_ref=dst, send_sem=send, recv_sem=recv, device_id=device, device_id_type=MESH
    )


def row_parts(tokens, count):
    tiles = tokens // 16
    sizes = [16 * (tiles * (at + 1) // count - tiles * at // count) for at in range(count)]
    sizes.sort(reverse=True)
    return tuple((sum(sizes[:at]), sizes[at]) for at in range(count))


class Gather:
    def __init__(self, place, buf, parts, orders, send, recv):
        self.place, self.buf, self.parts, self.orders = place, buf, parts, orders
        self.send, self.recv = send, recv
        self.flights = {}

    def start(self, part, stage):
        order = self.orders[part]
        delta = order[stage]
        held = [0]
        for earlier in order[:stage]:
            held = held + [mask ^ earlier for mask in held]
        first, rows = self.parts[part]
        begin = 2**stage - 1
        here = []
        for at, mask in enumerate(held):
            block = self.buf.at[self.place.flip(mask), pl.ds(first, rows)]
            slot = begin + at
            copy = remote(
                block, block, self.send.at[part, slot], self.recv.at[part, slot], self.place.peer(delta)
            )
            copy.start()
            here.append(copy)
        self.flights[part, stage] = here

    def landed(self, part, stage):
        for copy in self.flights[part, stage]:
            copy.wait_recv()

    def finish(self):
        for here in self.flights.values():
            for copy in here:
                copy.wait_send()


class Scatter:
    def __init__(self, place, buf, land, parts, orders, send, recv):
        self.place, self.buf, self.land, self.parts, self.orders = place, buf, land, parts, orders
        self.send, self.recv = send, recv
        self.flights = {}
        self.sums = {}

    def held(self, part, stage, mask):
        first, rows = self.parts[part]
        if stage == 0:
            return self.buf.at[self.place.flip(mask), pl.ds(first, rows)]
        return self.land.at[self.sums[part, stage - 1][mask], pl.ds(first, rows)]

    def start(self, part, stage):
        order = self.orders[part]
        delta = order[stage]
        kept = [0]
        for later in order[stage + 1 :]:
            kept = kept + [mask ^ later for mask in kept]
        first, rows = self.parts[part]
        begin = (0, 4, 6)[stage]
        here = []
        for at, mask in enumerate(kept):
            slot = begin + at
            copy = remote(
                self.held(part, stage, mask ^ delta),
                self.land.at[slot, pl.ds(first, rows)],
                self.send.at[part, slot],
                self.recv.at[part, slot],
                self.place.peer(delta),
            )
            copy.start()
            here.append((copy, mask, slot))
        self.flights[part, stage] = here
        self.sums[part, stage] = {mask: slot for _, mask, slot in here}

    def add(self, part, stage):
        first, rows = self.parts[part]
        result = None
        for copy, mask, slot in self.flights[part, stage]:
            copy.wait_recv()
            total = self.held(part, stage, mask)[...].astype(F32) + self.land[
                slot, pl.ds(first, rows)
            ].astype(F32)
            if stage < 2:
                self.land[slot, pl.ds(first, rows)] = total.astype(BF)
            else:
                result = total
        return result

    def finish(self):
        for here in self.flights.values():
            for copy, _, _ in here:
                copy.wait_send()


def tile_start(rank):
    few = FT - 1
    return 128 * jnp.where(rank < FULL_RANKS, FT * rank, FULL_RANKS + few * rank)


def first_columns(rank):
    mixer = (
        (rank * QW, 0, QW),
        (KD + rank * QW, QW, QW),
        (2 * KD + rank * VW, 2 * QW, VW),
        (2 * KD + VD + rank * VW, 2 * QW + VW, VW),
        (EXTRA_START, 2 * QW + 2 * VW, EXTRA),
    )
    outward = ((MIX_END + rank * VW, 0, VW),)
    at = tile_start(rank)
    gates = ((FFN_START + at, 0, FW), (FFN_START + FF + at, FW, FW))
    down = ((DOWN_START + at, 0, FW),)
    return mixer, outward, gates, down


def feature_blocks(place):
    copies = place.copies
    width = D // (4 * copies)
    if width % 128:
        return [(0, 0, D)]
    found = []
    for core in range(2):
        for copy in range(copies):
            for x in range(2):
                block = (x * 2 + (place.core + core) % 2) * copies + (place.dp + copy) % copies
                found.append((block * width, ((core * copies + copy) * 2 + x) * width, width))
    return found


def columns(at, width):
    if not isinstance(at, int):
        at = pl.multiple_of(at, 128)
    return pl.ds(at, width)


def spread_kernel(copies, parts, w_ref, x_ref, dy_ref, s_ref, mix, outward, gates, down,
                  gates_side, down_side, xall, sall, x_own, dy_own,
                  pack, pack_sem, local, send, recv, seg_send, seg_recv,
                  ag_send, ag_recv, copy_send, copy_recv, core_send, core_recv, side_send, side_recv, turned):
    place = Place(copies)
    peers = [place.peer(mask) for mask in range(1, RANKS)]
    partners = [place.copy_at(shift) for shift in range(1, copies)]
    meet(peers + partners + [place.sibling()])
    me = place.rank
    targets = (mix.at[0, 0], outward.at[0, 0], gates, down)
    others = (None, None, gates_side, down_side)
    wide = (mix, outward)
    own = []
    firsts = (0, 5, 6, 8)
    packed = []
    for mask in range(RANKS):
        there = place.flip(mask)
        here = []
        for slot, (at, to, width) in enumerate(first_columns(there)[0]):
            copy = pltpu.make_async_copy(
                w_ref.at[:, columns(at, width)], pack.at[mask, :, pl.ds(to, width)], pack_sem.at[mask, slot]
            )
            copy.start()
            here.append(copy)
        packed.append(here)
    own_mix = pltpu.make_async_copy(pack.at[0], mix.at[0, 0, me], local.at[0])
    def send_group(group):
        flights = []
        for mask in range(1, RANKS):
            there = place.flip(mask)
            for slot, (at, to, width) in enumerate(first_columns(there)[group]):
                copy = remote(
                    w_ref.at[:, columns(at, width)],
                    targets[group].at[me, :, pl.ds(to, width)],
                    send.at[firsts[group] + slot, mask - 1],
                    recv.at[group, mask - 1],
                    place.peer(mask),
                )
                copy.start()
                flights.append(copy)
        return flights

    def got(group, mask):
        block = targets[group].at[place.flip(mask)]
        remote(block, block, send.at[0, mask - 1], recv.at[group, mask - 1], place.peer(mask)).wait_recv()

    sent = []
    onward = []

    def forward(group, mask, block):
        whole = wide[group]
        there = place.flip(mask)
        for shift in range(1, copies):
            copy = remote(
                block, whole.at[0, copies - shift, there],
                copy_send.at[group, shift - 1, mask], copy_recv.at[group, copies - shift - 1, mask],
                place.copy_at(shift),
            )
            copy.start()
            onward.append(copy)
        copy = remote(
            block, whole.at[1, 0, there],
            core_send.at[group, 0, mask], core_recv.at[group, 0, mask], place.sibling(),
        )
        copy.start()
        onward.append(copy)

    def got_and_forward(group, mask):
        got(group, mask)
        forward(group, mask, wide[group].at[0, 0, place.flip(mask)])

    def from_copies(group):
        whole = wide[group]
        for shift in range(1, copies):
            for mask in range(RANKS):
                there = place.flip(mask)
                block = whole.at[0, shift, there]
                remote(
                    block, block, copy_send.at[group, shift - 1, mask], copy_recv.at[group, shift - 1, mask],
                    place.copy_at(shift),
                ).wait_recv()
                copy = remote(
                    block, whole.at[1, shift, there],
                    core_send.at[group, shift, mask], core_recv.at[group, shift, mask], place.sibling(),
                )
                copy.start()
                onward.append(copy)

    def from_sibling(group):
        for shift in range(copies):
            for mask in range(RANKS):
                block = wide[group].at[1, shift, place.flip(mask)]
                remote(
                    block, block, core_send.at[group, shift, mask], core_recv.at[group, shift, mask], place.sibling()
                ).wait_recv()

    for mask in range(1, RANKS):
        for copy in packed[mask]:
            copy.wait()
        copy = remote(
            pack.at[mask], mix.at[0, 0, me], send.at[0, mask - 1], recv.at[0, mask - 1], place.peer(mask)
        )
        copy.start()
        sent.append(copy)
    for copy in packed[0]:
        copy.wait()
    own_mix.start()
    forward(0, 0, pack.at[0])
    turns = []
    for row, (source, target) in enumerate(((x_ref, xall.at[me]), (x_ref, x_own), (dy_ref, dy_own))):
        here = []
        for slot, (at, to, width) in enumerate(feature_blocks(place)):
            copy = pltpu.make_async_copy(
                source.at[:, columns(at, width)], target.at[:, pl.ds(to, width)], turned.at[row, slot]
            )
            copy.start()
            here.append(copy)
        turns.append(here)
    own_s = pltpu.make_async_copy(s_ref, sall.at[me], local.at[10])
    own_s.start()

    for group in range(1, 4):
        here = []
        for slot, (at, to, width) in enumerate(first_columns(me)[group]):
            copy = pltpu.make_async_copy(
                w_ref.at[:, columns(at, width)], targets[group].at[me, :, pl.ds(to, width)],
                local.at[firsts[group] + slot],
            )
            copy.start()
            here.append(copy)
        own.append(here)
    own_s.wait()
    seg_flights = []
    for mask in range(1, RANKS):
        copy = remote(s_ref, sall.at[me], seg_send.at[mask - 1], seg_recv.at[mask - 1], place.peer(mask))
        copy.start()
        seg_flights.append(copy)
    sent = sent + send_group(1)
    for mask in range(1, RANKS):
        got_and_forward(0, mask)
    for copy in turns[0]:
        copy.wait()
    gather = Gather(place, xall, parts, MEET_EARLY, ag_send, ag_recv)
    for part in range(len(parts)):
        gather.start(part, 0)
    for group in range(2, 4):
        sent = sent + send_group(group)
    for copy in own[0]:
        copy.wait()
    forward(1, 0, wide[1].at[0, 0, me])
    for mask in range(1, RANKS):
        got_and_forward(1, mask)
    for stage in range(3):
        for part in range(len(parts)):
            gather.landed(part, stage)
            if stage < 2:
                gather.start(part, stage + 1)
    from_copies(0)
    from_copies(1)
    for group in range(2, 4):
        for copy in own[group - 1]:
            copy.wait()
        for mask in range(RANKS):
            if mask:
                got(group, mask)
            copy = remote(
                targets[group].at[place.flip(mask)], others[group].at[place.flip(mask)],
                side_send.at[group - 2, mask], side_recv.at[group - 2, mask], place.sibling(),
            )
            copy.start()
            onward.append(copy)
    for group in range(2, 4):
        for mask in range(RANKS):
            block = others[group].at[place.flip(mask)]
            remote(
                block, block, side_send.at[group - 2, mask], side_recv.at[group - 2, mask], place.sibling()
            ).wait_recv()
    from_sibling(0)
    from_sibling(1)
    for copy in seg_flights:
        copy.wait()
    own_mix.wait()
    for here in turns[1:]:
        for copy in here:
            copy.wait()
    for copy in sent + onward:
        copy.wait_send()
    gather.finish()


def any_spec():
    return pl.BlockSpec(memory_space=pl.ANY)


def vmem_spec():
    return pl.BlockSpec(memory_space=pltpu.VMEM)


def takes(micros):
    return pl.CostEstimate(flops=0, bytes_accessed=int(micros * 1e3), transcendentals=0)


def dma(*shape):
    return pltpu.SemaphoreType.DMA(shape)


def spread(copies, weights, x, dy, seg):
    rows = weights.shape[0]
    tokens = x.shape[0]
    shape = jax.ShapeDtypeStruct
    return pl.pallas_call(
        functools.partial(spread_kernel, copies, ((0, tokens // 2), (tokens // 2, tokens // 2))),
        out_shape=(
            shape((2, copies, RANKS, rows, MIXW), BF),
            shape((2, copies, RANKS, rows, OW), BF),
        )
        + (
            shape((RANKS, rows, 2 * FW), BF),
            shape((RANKS, rows, FW), BF),
        )
        * 2
        + (
            shape((RANKS, tokens, D), BF),
            shape((RANKS,) + seg.shape, seg.dtype),
            shape((tokens, D), BF),
            shape((tokens, D), BF),
        ),
        in_specs=[any_spec(), vmem_spec(), vmem_spec(), any_spec()],
        out_specs=[any_spec()] * 10,
        scratch_shapes=[
            pltpu.VMEM((RANKS, rows, MIXW), BF), dma(RANKS, 5), dma(11), dma(9, RANKS - 1), dma(4, RANKS - 1),
            dma(RANKS - 1), dma(RANKS - 1), dma(3, 7), dma(3, 7),
            dma(2, copies - 1, RANKS), dma(2, copies - 1, RANKS), dma(2, copies, RANKS), dma(2, copies, RANKS),
            dma(2, RANKS), dma(2, RANKS), dma(3, 4 * copies),
        ],
        compiler_params=pltpu.CompilerParams(collective_id=1, has_side_effects=True, vmem_limit_bytes=BIG),
        cost_estimate=takes(5),
        name="spread",
    )(weights, x, dy, seg)


def norm_scale(values, epsilon):
    return lax.rsqrt(jnp.mean(values * values, axis=-1, keepdims=True) + epsilon)


def sum_then_gather(scatter, gather, finish_rows):
    parts = range(len(scatter.parts))
    for part in parts:
        scatter.start(part, 0)
    for stage in range(2):
        for part in parts:
            scatter.add(part, stage)
            scatter.start(part, stage + 1)
    for part in parts:
        finish_rows(part, scatter.add(part, 2))
        gather.start(part, 0)
    for stage in range(3):
        for part in parts:
            gather.landed(part, stage)
            if stage < 2:
                gather.start(part, stage + 1)
    scatter.finish()
    gather.finish()


def branch_kernel(copies, parts, part_ref, x_ref, gain_ref, hidden_ref, nall, land,
                  send, recv, ag_send, ag_recv):
    place = Place(copies)
    meet([place.peer(mask) for mask in (4, 2, 1)])
    me = place.rank
    scatter = Scatter(place, part_ref, land, parts, SPLIT, send, recv)
    gather = Gather(place, nall, parts, MEET, ag_send, ag_recv)

    def finish_rows(part, total):
        first, rows = parts[part]
        hidden = x_ref[pl.ds(first, rows)].astype(F32) + total
        hidden_ref[pl.ds(first, rows)] = hidden
        unit = hidden * norm_scale(hidden, EPS_NORM)
        nall[me, pl.ds(first, rows)] = (unit * gain_ref[...]).astype(BF)

    sum_then_gather(scatter, gather, finish_rows)


def cube_scratch(tokens):
    return [pltpu.VMEM((7, tokens, D), BF), dma(3, 7), dma(3, 7)]


def branch(copies, partial, x, gain):
    tokens = x.shape[0]
    shape = jax.ShapeDtypeStruct
    return pl.pallas_call(
        functools.partial(branch_kernel, copies, row_parts(tokens, 3)),
        out_shape=(shape((tokens, D), F32), shape((RANKS, tokens, D), BF)),
        in_specs=[vmem_spec()] * 3,
        out_specs=[vmem_spec()] * 2,
        scratch_shapes=cube_scratch(tokens) + [dma(3, 7), dma(3, 7)],
        compiler_params=pltpu.CompilerParams(collective_id=2, has_side_effects=True, vmem_limit_bytes=BIG),
        cost_estimate=takes(5),
        name="branch",
    )(partial, x, gain)


def norm_back(grad, values, gain, epsilon):
    scale = norm_scale(values, epsilon)
    unit = values * scale
    scaled = grad * gain
    back = scale * (scaled - unit * jnp.mean(scaled * unit, axis=1, keepdims=True))
    return back, grad * unit


def hidden_back_kernel(copies, parts, part_ref, h_ref, dy_ref, gain_ref, dh_ref, gain_grad, dall, land,
                       send, recv, ag_send, ag_recv):
    place = Place(copies)
    meet([place.peer(mask) for mask in (4, 2, 1)])
    me = place.rank
    scatter = Scatter(place, part_ref, land, parts, SPLIT, send, recv)
    gather = Gather(place, dall, parts, MEET, ag_send, ag_recv)
    gain_grad[...] = jnp.zeros_like(gain_grad)

    def finish_rows(part, total):
        first, rows = parts[part]
        back, gain_part = norm_back(total, h_ref[pl.ds(first, rows)], gain_ref[...], EPS_NORM)
        back = dy_ref[pl.ds(first, rows)].astype(F32) + back
        dh_ref[pl.ds(first, rows)] = back
        dall[me, pl.ds(first, rows)] = back.astype(BF)
        gain_grad[...] += jnp.sum(gain_part, axis=0, keepdims=True)

    sum_then_gather(scatter, gather, finish_rows)


def hidden_back(copies, partial, hidden, dy, gain):
    tokens = dy.shape[0]
    shape = jax.ShapeDtypeStruct
    return pl.pallas_call(
        functools.partial(hidden_back_kernel, copies, row_parts(tokens, 3)),
        out_shape=(shape((tokens, D), F32), shape((1, D), F32), shape((RANKS, tokens, D), BF)),
        in_specs=[vmem_spec()] * 4,
        out_specs=[vmem_spec()] * 3,
        scratch_shapes=cube_scratch(tokens) + [dma(3, 7), dma(3, 7)],
        compiler_params=pltpu.CompilerParams(collective_id=3, has_side_effects=True, vmem_limit_bytes=BIG),
        cost_estimate=takes(5),
        name="hidden_back",
    )(partial, hidden, dy, gain)


class Home:
    def __init__(self, place, groups, ins, out, local, send, recv):
        self.place, self.groups, self.ins, self.out = place, groups, ins, out
        self.local, self.send, self.recv = local, send, recv

    def pieces(self, rank):
        found = []
        for group, source in zip(self.groups, self.ins):
            for at, to, width in first_columns(rank)[group]:
                if group == 0 and to == 2 * QW + 2 * VW:
                    continue
                if group == 2:
                    found.append((source[to // FW], 0, at, width - 128, False))
                    found.append((source[to // FW], width - 128, at + width - 128, 128, True))
                elif group == 3:
                    found.append((source, 0, at, width - 128, False))
                    found.append((source, width - 128, at + width - 128, 128, True))
                else:
                    found.append((source, to, at, width, False))
        return found

    def when(self, flag, rank, act):
        if flag:
            pl.when(rank < FULL_RANKS)(act)
        else:
            act()

    def run(self, method):
        place = self.place
        me = place.rank
        for slot, (source, to, at, width, flag) in enumerate(self.pieces(me)):
            copy = pltpu.make_async_copy(
                source.at[me, :, pl.ds(to, width)],
                self.out.at[:, columns(at, width)],
                self.local.at[slot],
            )
            self.when(flag, me, getattr(copy, method))
        for mask in range(1, RANKS):
            there = place.flip(mask)
            for slot, (source, to, at, width, flag) in enumerate(self.pieces(me)):
                copy = remote(
                    source.at[there, :, pl.ds(to, width)],
                    self.out.at[:, columns(at, width)],
                    self.send.at[mask - 1, slot],
                    self.recv.at[mask - 1, slot],
                    place.peer(mask),
                )
                self.when(flag, me, copy.start if method == "start" else copy.wait_send)
            if method == "wait":
                for slot, (source, to, at, width, flag) in enumerate(self.pieces(there)):
                    block = self.out.at[:, columns(at, width)]
                    copy = remote(
                        block, block, self.send.at[mask - 1, slot], self.recv.at[mask - 1, slot], place.peer(mask)
                    )
                    self.when(flag, there, copy.wait_recv)


def home_scratch():
    return [dma(7), dma(RANKS - 1, 7), dma(RANKS - 1, 7)]


def home_kernel(copies, mix_ref, extra_ref, out, extra_out, local, send, recv, land, own, far, near):
    place = Place(copies)
    meet([place.peer(mask) for mask in range(1, RANKS)])
    way = Home(place, (0,), (mix_ref,), out, local, send, recv)
    flights = []
    for mask in range(1, RANKS):
        copy = remote(
            extra_ref.at[place.flip(mask)], land.at[mask - 1], far.at[mask - 1], near.at[mask - 1], place.peer(mask)
        )
        copy.start()
        flights.append(copy)
    way.run("start")
    mine = pltpu.make_async_copy(extra_ref.at[place.rank], own, local.at[6])
    mine.start()
    mine.wait()
    total = own[...]
    for mask in range(1, RANKS):
        flights[mask - 1].wait_recv()
        total = total + land[mask - 1]
    extra_out[...] = total
    for copy in flights:
        copy.wait_send()
    way.run("wait")


def home(copies, array, extra):
    rows = array.shape[1]
    shape = jax.ShapeDtypeStruct
    return pl.pallas_call(
        functools.partial(home_kernel, copies),
        out_shape=(shape((rows, MIX_END), BF), shape((rows, EXTRA), F32)),
        in_specs=[any_spec()] * 2,
        out_specs=(any_spec(), vmem_spec()),
        scratch_shapes=home_scratch()
        + [pltpu.VMEM((RANKS - 1, rows, EXTRA), F32), pltpu.VMEM((rows, EXTRA), F32), dma(RANKS - 1), dma(RANKS - 1)],
        compiler_params=pltpu.CompilerParams(collective_id=6, has_side_effects=True, vmem_limit_bytes=BIG),
        cost_estimate=takes(5),
        name="home",
    )(array, extra)


def home_rest_kernel(copies, out_rows, gate_rows, up_rows, down_rows, rest, local, send, recv):
    place = Place(copies)
    meet([place.peer(mask) for mask in range(1, RANKS)])
    way = Home(place, (1, 2, 3), (out_rows, (gate_rows, up_rows), down_rows), rest, local, send, recv)
    way.run("start")
    way.run("wait")


def home_rest(copies, grad_rows):
    rows = grad_rows[0].shape[1]
    return pl.pallas_call(
        functools.partial(home_rest_kernel, copies),
        out_shape=jax.ShapeDtypeStruct((rows, EXTRA_START), BF),
        in_specs=[any_spec()] * 4,
        out_specs=any_spec(),
        scratch_shapes=home_scratch(),
        compiler_params=pltpu.CompilerParams(collective_id=4, has_side_effects=True, vmem_limit_bytes=BIG),
        cost_estimate=takes(5),
        name="home_rest",
    )(*grad_rows)


def dot(left, right, axes):
    return lax.dot_general(left, right, (axes, ((), ())), preferred_element_type=F32)


def halves(values):
    high = values.astype(BF)
    return high, (values - high.astype(F32)).astype(BF)


def mul(left, right, axes):
    left_high, left_low = halves(left)
    right_high, right_low = halves(right)
    return dot(left_high, right_high, axes) + (dot(left_high, right_low, axes) + dot(left_low, right_high, axes))


def mul_mask(mask, right, axes):
    right_high, right_low = halves(right)
    return dot(mask, right_high, axes) + dot(mask, right_low, axes)


NN = ((1,), (0,))
NT = ((1,), (1,))
TN = ((0,), (0,))


def unit_lower_inverses(lowers, row, col):
    size = lowers[0].shape[0]
    pair = (row >> 1) == (col >> 1)
    inverses = [jnp.where(row == col, 1.0, jnp.where(pair, -lower, 0.0)) for lower in lowers]
    level = 1
    while 2**level < size:
        joined = ((row >> (level + 1)) == (col >> (level + 1))) & ((row >> level) != (col >> level))
        parts = [mul(jnp.where(joined, lower, 0.0), inverse, NN) for lower, inverse in zip(lowers, inverses)]
        inverses = [inverse - mul(inverse, part, NN) for inverse, part in zip(inverses, parts)]
        level = level + 1
    return inverses


class Sequence:
    def __init__(self, seg_row):
        tokens = seg_row.shape[1]
        self.tokens = tokens
        shape = (tokens, tokens)
        self.row = lax.broadcasted_iota(jnp.int32, shape, 0)
        self.col = lax.broadcasted_iota(jnp.int32, shape, 1)
        ids = jnp.broadcast_to(seg_row.astype(F32), shape)
        turned = ids.T
        same = turned == ids
        self.inclusive = same & (self.row >= self.col)
        self.strict = same & (self.row > self.col)
        self.lower = (self.row >= self.col).astype(BF)
        column = turned[:, :1]
        at = self.row[:, :1]
        self.near = [None]
        for back in range(1, CONV):
            before = pltpu.roll(turned, back, 0)[:, :1]
            self.near.append(((before == column) & (at >= back)).astype(F32))

    def conv(self, taps, values):
        total = taps[CONV - 1 : CONV] * values
        for back in range(1, CONV):
            total = total + taps[CONV - 1 - back : CONV - back] * (
                self.near[back] * pltpu.roll(values, back, 0)
            )
        return total

    def conv_back(self, taps, values, grad):
        total = taps[CONV - 1 : CONV] * grad
        rows = [jnp.sum(values * grad, axis=0, keepdims=True)]
        for back in range(1, CONV):
            masked = self.near[back] * grad
            total = total + taps[CONV - 1 - back : CONV - back] * pltpu.roll(
                masked, self.tokens - back, 0
            )
            rows.append(jnp.sum(masked * pltpu.roll(values, back, 0), axis=0, keepdims=True))
        return total, jnp.concatenate(rows[::-1], axis=0)


def pick_lane(block, lane):
    at = lax.broadcasted_iota(jnp.int32, block.shape, 1)
    return jnp.sum(jnp.where(at == lane, block, 0.0), axis=1, keepdims=True)


def softplus(values):
    return jnp.maximum(values, 0.0) + jnp.log1p(jnp.exp(-jnp.abs(values)))


class Head:
    def __init__(self, seq, head, rank, scalars, p_ref, taps_ref):
        q_at, k_at = head * DK, QW + head * DK
        v_at, g_at = 2 * QW + head * DV, 2 * QW + VW + head * DV
        self.q_at, self.k_at, self.v_at, self.g_at = q_at, k_at, v_at, g_at
        self.raw = [p_ref[:, q_at : q_at + DK], p_ref[:, k_at : k_at + DK], p_ref[:, v_at : v_at + DV]]
        self.taps = [taps_ref[:, q_at : q_at + DK], taps_ref[:, k_at : k_at + DK], taps_ref[:, v_at : v_at + DV]]
        self.pre = [seq.conv(taps, raw) for taps, raw in zip(self.taps, self.raw)]
        self.sig = [jax.nn.sigmoid(pre) for pre in self.pre]
        conv_q, conv_k, self.v = [pre * sig for pre, sig in zip(self.pre, self.sig)]
        self.q_scale = lax.rsqrt(jnp.sum(conv_q * conv_q, axis=1, keepdims=True) + EPS_NORM)
        self.k_scale = lax.rsqrt(jnp.sum(conv_k * conv_k, axis=1, keepdims=True) + EPS_NORM)
        self.q_unit = conv_q * self.q_scale
        self.q = self.q_unit * DK**-0.5
        self.k = conv_k * self.k_scale
        pair = p_ref[:, 2 * QW + 2 * VW :]
        self.lane_a = rank * HEADS + head
        self.lane_b = H + rank * HEADS + head
        self.a = pick_lane(pair, self.lane_a) + scalars[HEADS + head]
        self.rate = scalars[head]
        self.beta = jax.nn.sigmoid(pick_lane(pair, self.lane_b))
        self.decay = -self.rate * softplus(self.a)
        spread_out = jnp.where(seq.row > seq.col, jnp.broadcast_to(self.decay, seq.row.shape), 0.0)
        gap = mul_mask(seq.lower, spread_out, NN)
        self.pairs = jnp.where(seq.inclusive, jnp.exp(jnp.where(seq.inclusive, gap, 0.0)), 0.0)
        self.kk = mul(self.k, self.k, NT)
        self.qk = mul(self.q, self.k, NT)
        self.strict_pairs = jnp.where(seq.strict, self.pairs, 0.0)
        self.lower = self.beta * self.strict_pairs * self.kk
        self.attend = self.pairs * self.qk
        self.gate = p_ref[:, g_at : g_at + DV]


def mixer_kernel(rank_ref, scalars, seg_ref, p_ref, taps_ref, gain_ref, z_ref, inv_ref, upd_ref):
    seq = Sequence(seg_ref[0, :1])
    rank = rank_ref[0]
    ones = [Head(seq, head, rank, scalars, p_ref, taps_ref) for head in range(HEADS)]
    inverses = unit_lower_inverses([one.lower for one in ones], seq.row, seq.col)
    updates = [mul(inverse, one.beta * one.v, NN) for inverse, one in zip(inverses, ones)]
    outs = [mul(one.attend, update, NN) for one, update in zip(ones, updates)]
    for head, (one, inverse, update, out) in enumerate(zip(ones, inverses, updates, outs)):
        normed = out * norm_scale(out, EPS_GATED) * gain_ref[...]
        z_ref[:, head * DV : (head + 1) * DV] = (normed * (one.gate * jax.nn.sigmoid(one.gate))).astype(BF)
        inv_ref[0, head] = inverse
        upd_ref[0, head] = update


def mixer_back_kernel(rank_ref, scalars, seg_ref, p_ref, taps_ref, gain_ref, inv_ref, upd_ref, dz_ref,
                      dp_ref, dtaps_ref, dgain_ref, dscal_ref):
    @pl.when(pl.program_id(0) == 0)
    def _():
        dtaps_ref[...] = jnp.zeros_like(dtaps_ref)
        dgain_ref[...] = jnp.zeros_like(dgain_ref)
        dscal_ref[...] = jnp.zeros_like(dscal_ref)

    seq = Sequence(seg_ref[0, :1])
    rank = rank_ref[0]
    pair_grad = jnp.zeros((seq.tokens, EXTRA), F32)
    lane = lax.broadcasted_iota(jnp.int32, (seq.tokens, EXTRA), 1)
    scal_row = lax.broadcasted_iota(jnp.int32, (8, 128), 0)
    scal_col = lax.broadcasted_iota(jnp.int32, (8, 128), 1)
    scal = jnp.zeros((8, 128), F32)
    for head in range(HEADS):
        one = Head(seq, head, rank, scalars, p_ref, taps_ref)
        inverse = inv_ref[0, head]
        update = upd_ref[0, head]
        out = mul(one.attend, update, NN)
        dz = dz_ref[:, head * DV : (head + 1) * DV]
        scale = norm_scale(out, EPS_GATED)
        normed = out * scale
        sig = jax.nn.sigmoid(one.gate)
        gate = one.gate * sig
        d_gate = dz * normed * gain_ref[...] * (sig * (1 + one.gate * (1 - sig)))
        dp_ref[:, one.g_at : one.g_at + DV] = d_gate.astype(BF)
        dgain_ref[...] += jnp.sum(dz * normed * gate, axis=0, keepdims=True)
        d_normed = dz * gain_ref[...] * gate
        d_out = scale * (d_normed - normed * jnp.mean(d_normed * normed, axis=1, keepdims=True))
        d_attend = jnp.where(seq.inclusive, mul(d_out, update, NT), 0.0)
        d_update = mul(one.attend, d_out, TN)
        d_scaled = mul(inverse, d_update, TN)
        d_lower = jnp.where(seq.strict, -mul(d_scaled, update, NT), 0.0)
        d_v = one.beta * d_scaled
        d_beta = jnp.sum(d_scaled * one.v, axis=1, keepdims=True) + jnp.sum(
            d_lower * one.strict_pairs * one.kk, axis=1, keepdims=True
        )
        d_gap = d_attend * one.attend + d_lower * one.lower
        d_qk = d_attend * one.pairs
        d_kk = d_lower * (one.beta * one.strict_pairs)
        d_q = mul(d_qk, one.k, NN)
        d_k = mul(d_qk, one.q, TN) + mul(d_kk, one.k, NN) + mul(d_kk, one.k, TN)
        reach = mul_mask(seq.lower, d_gap, TN)
        d_decay = jnp.sum(jnp.where(seq.row > seq.col, reach, 0.0), axis=1, keepdims=True)
        d_a = d_decay * (-one.rate) * jax.nn.sigmoid(one.a)
        d_b = d_beta * one.beta * (1 - one.beta)
        pair_grad = pair_grad + jnp.where(lane == one.lane_a, d_a, 0.0) + jnp.where(lane == one.lane_b, d_b, 0.0)
        sum_rate = jnp.sum(d_decay * one.decay, axis=0, keepdims=True)
        sum_a = jnp.sum(d_a, axis=0, keepdims=True)
        scal = scal + jnp.where((scal_row == 0) & (scal_col == head), sum_rate, 0.0)
        scal = scal + jnp.where((scal_row == 0) & (scal_col == HEADS + head), sum_a, 0.0)
        dq_unit = d_q * DK**-0.5
        dc_q = one.q_scale * (dq_unit - one.q_unit * jnp.sum(dq_unit * one.q_unit, axis=1, keepdims=True))
        dc_k = one.k_scale * (d_k - one.k * jnp.sum(d_k * one.k, axis=1, keepdims=True))
        for grad, pre, sig, raw, taps, at, width in (
            (dc_q, one.pre[0], one.sig[0], one.raw[0], one.taps[0], one.q_at, DK),
            (dc_k, one.pre[1], one.sig[1], one.raw[1], one.taps[1], one.k_at, DK),
            (d_v, one.pre[2], one.sig[2], one.raw[2], one.taps[2], one.v_at, DV),
        ):
            d_pre = grad * (sig * (1 + pre * (1 - sig)))
            d_raw, d_taps = seq.conv_back(taps, raw, d_pre)
            dp_ref[:, at : at + width] = d_raw.astype(BF)
            dtaps_ref[:, at : at + width] += d_taps
    dp_ref[:, 2 * QW + 2 * VW :] = pair_grad.astype(BF)
    dscal_ref[...] += scal


def smem_spec():
    return pl.BlockSpec(memory_space=pltpu.SMEM)


def by_sequence(*shape):
    rest = (0,) * (len(shape) - 1)
    return pl.BlockSpec(shape, lambda at: (at,) + rest)


def whole_block(*shape):
    return pl.BlockSpec(shape, lambda at: (0,) * len(shape))


CHANNELS = 2 * QW + VW


def mixer(rank, scalars, seg, p, taps, gain, tokens):
    count = p.shape[0] // tokens
    shape = jax.ShapeDtypeStruct
    return pl.pallas_call(
        mixer_kernel,
        grid=(count,),
        out_shape=(
            shape((p.shape[0], VW), BF),
            shape((count, HEADS, tokens, tokens), F32),
            shape((count, HEADS, tokens, DV), F32),
        ),
        in_specs=[
            smem_spec(), smem_spec(), by_sequence(1, 8, tokens), by_sequence(tokens, MIXW),
            whole_block(CONV, CHANNELS), whole_block(1, DV),
        ],
        out_specs=[
            by_sequence(tokens, VW), by_sequence(1, HEADS, tokens, tokens), by_sequence(1, HEADS, tokens, DV),
        ],
        compiler_params=pltpu.CompilerParams(vmem_limit_bytes=BIG),
        cost_estimate=takes(5),
        name="mixer",
    )(rank, scalars, seg, p, taps, gain)


def mixer_back(rank, scalars, seg, p, taps, gain, inverse, update, dz, tokens):
    count = p.shape[0] // tokens
    shape = jax.ShapeDtypeStruct
    return pl.pallas_call(
        mixer_back_kernel,
        grid=(count,),
        out_shape=(
            shape((p.shape[0], MIXW), BF),
            shape((CONV, CHANNELS), F32),
            shape((1, DV), F32),
            shape((8, 128), F32),
        ),
        in_specs=[
            smem_spec(), smem_spec(), by_sequence(1, 8, tokens), by_sequence(tokens, MIXW),
            whole_block(CONV, CHANNELS), whole_block(1, DV),
            by_sequence(1, HEADS, tokens, tokens), by_sequence(1, HEADS, tokens, DV), by_sequence(tokens, VW),
        ],
        out_specs=[
            by_sequence(tokens, MIXW), whole_block(CONV, CHANNELS), whole_block(1, DV), whole_block(8, 128),
        ],
        compiler_params=pltpu.CompilerParams(vmem_limit_bytes=BIG),
        cost_estimate=takes(5),
        name="mixer_back",
    )(rank, scalars, seg, p, taps, gain, inverse, update, dz)


def adam_kernel(filled, scalars, grad_ref, one_ref, two_ref, master_ref, *refs):
    grad_out, one_out, two_out, master_out, weight_out = refs[filled:]
    beta_one, beta_two, rate = scalars[0], scalars[1], scalars[2]
    grad = grad_ref[...].astype(F32)
    one = beta_one * one_ref[...] + (1 - beta_one) * grad
    two = beta_two * two_ref[...] + (1 - beta_two) * grad * grad
    master = master_ref[...]
    change = (one / scalars[3]) / (jnp.sqrt(two / scalars[4]) + EPS_ADAM) + DECAY_WEIGHT * master
    master = master - rate * change
    grad_out[...] = grad
    one_out[...] = one
    two_out[...] = two
    master_out[...] = master
    weight_out[...] = master.astype(BF)


def adam(scalars, grads, state, done, first, width, count):
    rows = grads.shape[0]
    at_first = first // width
    grad_first = at_first if grads.shape[1] > first else 0
    shape = jax.ShapeDtypeStruct
    there = pl.BlockSpec((rows, width), lambda at: (0, at + at_first))
    filled = () if done is None else tuple(done)
    return pl.pallas_call(
        functools.partial(adam_kernel, len(filled)),
        grid=(count,),
        out_shape=(shape((rows, COLS), F32),) * 4 + (shape((rows, COLS), BF),),
        in_specs=[smem_spec(), pl.BlockSpec((rows, width), lambda at: (0, at + grad_first))]
        + [there] * 3 + [any_spec()] * len(filled),
        out_specs=[there] * 5,
        input_output_aliases={5 + at: at for at in range(len(filled))},
        compiler_params=pltpu.CompilerParams(vmem_limit_bytes=BIG),
        cost_estimate=takes(5),
        name="adam",
    )(scalars, grads, *state, *filled)


def weight_grad_kernel(left_ref, right_ref, *refs):
    total = dot(left_ref[...], right_ref[...], TN)
    for ref in refs[:-1]:
        total = total + ref[...].astype(F32)
    refs[-1][...] = total.astype(BF)


def weight_grad(left, right, at, width, adds=(), count=None):
    tokens = right.shape[0]
    count = right.shape[1] if count is None else count
    tile = 768 if count % 768 == 0 else count

    def add_spec(row, column):
        return pl.BlockSpec((width, tile), lambda step: (row, step + column // tile))

    return pl.pallas_call(
        weight_grad_kernel,
        grid=(count // tile,),
        out_shape=jax.ShapeDtypeStruct((width, count), BF),
        in_specs=[
            pl.BlockSpec((tokens, width), lambda step: (0, at)),
            pl.BlockSpec((tokens, tile), lambda step: (0, step)),
        ]
        + [add_spec(row, column) for _, row, column in adds],
        out_specs=pl.BlockSpec((width, tile), lambda step: (0, step)),
        compiler_params=pltpu.CompilerParams(vmem_limit_bytes=BIG),
        cost_estimate=takes(1),
        name="weight_grad",
    )(left, right, *[array for array, _, _ in adds])


def input_back_kernel(grad_ref, w_ref, x_ref, scale_ref, out_ref, gain_ref):
    grad = dot(grad_ref[...], w_ref[...], NT)
    out_ref[...] = grad.astype(BF)
    unit = x_ref[...].astype(F32) * scale_ref[:, :1]
    gain_ref[...] = jnp.sum(grad * unit, axis=0, keepdims=True)


def input_back(grad, w, x, scale):
    tokens, count = grad.shape
    tile = 512
    shape = jax.ShapeDtypeStruct
    return pl.pallas_call(
        input_back_kernel,
        grid=(D // tile,),
        out_shape=(shape((tokens, D), BF), shape((1, D), F32)),
        in_specs=[
            whole_block(tokens, count),
            pl.BlockSpec((tile, count), lambda step: (step, 0)),
            pl.BlockSpec((tokens, tile), lambda step: (0, step)),
            whole_block(tokens, 128),
        ],
        out_specs=[
            pl.BlockSpec((tokens, tile), lambda step: (0, step)), pl.BlockSpec((1, tile), lambda step: (0, step)),
        ],
        compiler_params=pltpu.CompilerParams(vmem_limit_bytes=BIG),
        cost_estimate=takes(1),
        name="input_back",
    )(grad, w, x, scale)


def project_kernel(x_ref, w_ref, normed_ref, p_ref, gains_ref, scale_ref, gain):
    @pl.when(pl.program_id(0) == 0)
    def _():
        row = lax.broadcasted_iota(jnp.int32, (8, EXTRA), 0)
        col = lax.broadcasted_iota(jnp.int32, (8, EXTRA), 1)
        pick = (col == row + 2 * H).astype(BF)
        gain[...] = dot(pick, w_ref[:, MIXW - EXTRA :], NT)
        gains_ref[...] = gain[...]

    x = x_ref[...].astype(F32)
    scale = norm_scale(x, EPS_NORM)
    scale_ref[...] = jnp.broadcast_to(scale, scale_ref.shape)
    normed = (x * scale * gain[:1]).astype(BF)
    normed_ref[...] = normed
    p_ref[...] = dot(normed, w_ref[...], NN)


def project(x, w):
    count = x.shape[0]
    rows = 256
    shape = jax.ShapeDtypeStruct
    return pl.pallas_call(
        project_kernel,
        grid=(count // rows,),
        out_shape=(shape((count, D), BF), shape((count, MIXW), F32), shape((8, D), F32), shape((count, 128), F32)),
        in_specs=[by_sequence(rows, D), whole_block(D, MIXW)],
        out_specs=[by_sequence(rows, D), by_sequence(rows, MIXW), whole_block(8, D), by_sequence(rows, 128)],
        scratch_shapes=[pltpu.VMEM((8, D), F32)],
        compiler_params=pltpu.CompilerParams(vmem_limit_bytes=BIG),
        cost_estimate=takes(1),
        name="project",
    )(x, w)


def finish_kernel(copies, at_ref, hidden_ref, feed_ref, grad_ref, x_ref, d_hidden_ref, gain_ref, out_ref, in_grad_ref):
    out = (hidden_ref[...] + feed_ref[...].astype(F32)).astype(BF)
    back, _ = norm_back(grad_ref[...].astype(F32), x_ref[...].astype(F32), gain_ref[...], EPS_NORM)
    in_grad = (d_hidden_ref[...] + back).astype(BF)
    width = D // (4 * copies)
    for core in range(2):
        for copy in range(copies):
            for x in range(2):
                block = (x * 2 + (at_ref[0] + core) % 2) * copies + (at_ref[1] + copy) % copies
                to = pl.ds(pl.multiple_of(block * width, 128), width)
                at = ((core * copies + copy) * 2 + x) * width
                out_ref[:, to] = out[:, at : at + width]
                in_grad_ref[:, to] = in_grad[:, at : at + width]


def finish(place, copies, hidden, feed, grad, x, d_hidden, gain):
    shape = jax.ShapeDtypeStruct(x.shape, BF)
    return pl.pallas_call(
        functools.partial(finish_kernel, copies),
        out_shape=(shape, shape),
        in_specs=[smem_spec()] + [vmem_spec()] * 6,
        out_specs=[vmem_spec()] * 2,
        compiler_params=pltpu.CompilerParams(vmem_limit_bytes=BIG),
        cost_estimate=takes(1),
        name="finish",
    )(place, hidden, feed, grad, x, d_hidden, gain)


def turn(blocks, shift, axis):
    size = blocks.shape[axis]
    twice = jnp.concatenate([blocks, blocks], axis=axis)
    return lax.dynamic_slice_in_dim(twice, shift % size, size, axis)


class Order:
    def __init__(self, copies, core, dp):
        self.copies, self.core, self.dp = copies, core, dp

    def relative(self, values, axis):
        lead, tail = values.shape[:axis], values.shape[axis + 1 :]
        whole = values.reshape(lead + (2, 2, self.copies, D // (4 * self.copies)) + tail)
        whole = turn(turn(whole, self.core, axis + 1), self.dp, axis + 2)
        whole = jnp.moveaxis(whole, axis, axis + 2)
        return whole.reshape(values.shape)

    def plain(self, values, axis):
        lead, tail = values.shape[:axis], values.shape[axis + 1 :]
        whole = values.reshape(lead + (2, self.copies, 2, D // (4 * self.copies)) + tail)
        whole = jnp.moveaxis(whole, axis + 2, axis)
        whole = turn(turn(whole, 2 - self.core, axis + 1), self.copies - self.dp, axis + 2)
        return whole.reshape(values.shape)


def on_device(inputs, cotangent, segment_ids, weights, master, moment_one, moment_two,
              step, learn_rate, beta_one, beta_two):
    tokens = inputs.shape[0]
    rows = weights.shape[0]
    replicas = lax.axis_size("rep")
    copies = replicas // 4
    members = replicas * 4
    rep = lax.axis_index("rep")
    grp = lax.axis_index("grp")
    core = grp % 2
    dp = rep // 4
    rank = rank_of(rep, grp)
    order = Order(copies, core, dp)
    axes = ("rep", "grp")
    group_tokens = RANKS * tokens
    block_rows = RANKS * rows

    def pairs_to(move):
        return [(at, move(at // 4, at % 4)) for at in range(members)]

    core_pairs = pairs_to(lambda r, g: r * 4 + (g ^ 1))
    copy_pairs = [
        pairs_to(lambda r, g, shift=shift: ((r + 4 * shift) % replicas) * 4 + g) for shift in range(1, copies)
    ]

    in_place = (D // (4 * copies)) % 128 == 0
    x, dy = (inputs, cotangent) if in_place else (order.relative(inputs, 1), order.relative(cotangent, 1))
    seg = jnp.broadcast_to(segment_ids[None, :], (8, tokens))
    mix_blocks, out_blocks, gate_block, down_block, gate_side, down_side, x_all, seg_all, x, dy = spread(
        copies, weights, x, dy, seg
    )
    cubes = [
        [(copy * 4 + j % 4) * 4 + (j // 4) * 2 + side for j in range(RANKS)]
        for copy in range(copies)
        for side in range(2)
    ]
    dy_all = lax.all_gather(dy, axes, axis_index_groups=cubes, axis=0, tiled=True)
    x_all = x_all.reshape(group_tokens, D)
    w_mix = mix_blocks.reshape(D, MIXW)
    w_out = out_blocks.reshape(D, OW)

    def from_copies(blocks):
        block = blocks.reshape(block_rows, blocks.shape[2])
        return [lax.ppermute(block, axes, copy_pairs[copies - shift - 1]) for shift in range(1, copies)]

    def collect(blocks, side, landed):
        mine = [blocks.reshape(block_rows, blocks.shape[2])] + landed
        theirs = [side.reshape(block_rows, side.shape[2])]
        theirs = theirs + [lax.ppermute(one, axes, core_pairs) for one in landed]
        return jnp.concatenate(mine + theirs, axis=0)

    together = lax.optimization_barrier
    gate_landed = from_copies(gate_block)
    down_landed = from_copies(down_block)
    normed, p, gains, x_scale = project(x_all, w_mix)
    gain_one, gain_two = gains[:1], gains[1:2]
    extra = order.plain(w_mix[:, MIXW - EXTRA :], 0).astype(F32)
    conv_cols = CONV * (2 * KD + VD) // D
    conv_at = 2 * H + 2

    tap_rows = D // CONV
    table = extra[:, conv_at : conv_at + conv_cols].reshape(CONV, tap_rows, conv_cols)
    ranges = ((0, QW), (KD, QW), (2 * KD, VW))

    def own_channels(first, width):
        return first // conv_cols + rank * (width // conv_cols), width // conv_cols

    taps = jnp.concatenate(
        [
            lax.dynamic_slice_in_dim(table, *own_channels(first, width), 1).reshape(CONV, width)
            for first, width in ranges
        ],
        axis=1,
    )
    column = extra[: 2 * H + DV, conv_at + conv_cols]
    scalars = jnp.concatenate(
        [
            jnp.exp(lax.dynamic_slice_in_dim(column, rank * HEADS, HEADS, 0)),
            lax.dynamic_slice_in_dim(column, H + rank * HEADS, HEADS, 0),
        ]
    )
    out_gain = column[2 * H : 2 * H + DV][None]
    rank_arg = jnp.reshape(rank, (1,)).astype(jnp.int32)
    gated, inverse, update = mixer(rank_arg, scalars, seg_all, p, taps, out_gain, tokens)
    partial = dot(gated, w_out, NT).astype(BF)
    hidden, normed_two = branch(copies, partial.reshape(RANKS, tokens, D), x, gain_two)
    normed_two = normed_two.reshape(group_tokens, D)
    normed_two, gate_landed, down_landed = together((normed_two, gate_landed, down_landed))
    w_gates = collect(gate_block, gate_side, gate_landed)
    w_down = collect(down_block, down_side, down_landed)
    gate_up = dot(normed_two, w_gates, NN)
    gate_part, up_part = gate_up[:, :FW], gate_up[:, FW:]
    tile_count = jnp.where(rank < FULL_RANKS, FT, FT - 1)
    real = (jnp.arange(FW) < tile_count * 128)[None]
    sigmoid_gate = jax.nn.sigmoid(gate_part)
    activated = jnp.where(real, gate_part * sigmoid_gate * up_part, 0.0).astype(BF)
    half = copies * block_rows

    def block_of(values, at):
        return values[:, at * block_rows : (at + 1) * block_rows]

    def first_half(left, right):
        theirs = dot(left[:, half:], right, TN).astype(BF)
        return theirs, lax.ppermute(theirs, axes, core_pairs)

    def away_rows(left, right, got):
        return [
            (dot(block_of(left, at), right, TN) + got[at * block_rows : (at + 1) * block_rows].astype(F32)).astype(BF)
            for at in range(1, copies)
        ]

    def to_copies(away):
        return [lax.ppermute(one, axes, pairs) for one, pairs in zip(away, copy_pairs)]

    def for_copies(left, right, got):
        away = away_rows(left, right, got)
        return away, to_copies(away)

    down_half, down_got = first_half(dy_all, activated)
    down_half, activated = together((down_half, activated))
    feed = dot(activated, w_down, NT).astype(BF)
    d_act = dot(dy_all, w_down, NN)
    d_gate = d_act * up_part * sigmoid_gate * (1 + gate_part * (1 - sigmoid_gate))
    d_up = d_act * gate_part * sigmoid_gate
    real_two = jnp.concatenate([real, real], axis=1)
    d_gate_up = jnp.where(real_two, jnp.concatenate([d_gate, d_up], axis=1), 0.0).astype(BF)
    gate_half, gate_got = first_half(normed_two, d_gate_up)
    down_away, down_landed = for_copies(dy_all, activated, down_got)
    gate_half, down_away, d_gate_up = together((gate_half, down_away, d_gate_up))
    d_normed_two = dot(d_gate_up, w_gates, NT).astype(BF)
    d_gate_part, d_up_part = d_gate_up[:, :FW], d_gate_up[:, FW:]
    gate_away = away_rows(normed_two, d_gate_part, gate_got[:, :FW])
    up_away = away_rows(normed_two, d_up_part, gate_got[:, FW:])
    gate_away, up_away, d_normed_two = together((gate_away, up_away, d_normed_two))
    up_landed = to_copies(up_away)
    d_hidden, gain_two_grad, d_hidden_all = hidden_back(
        copies, d_normed_two.reshape(RANKS, tokens, D), hidden, dy, gain_two
    )
    d_hidden_all = d_hidden_all.reshape(group_tokens, D)
    d_hidden_all, up_landed, gate_away, down_landed, feed = together(
        (d_hidden_all, up_landed, gate_away, down_landed, feed)
    )
    feed = lax.psum_scatter(feed, axes, axis_index_groups=cubes, scatter_dimension=0, tiled=True)
    gate_landed = to_copies(gate_away)
    out_half, out_got = first_half(d_hidden_all, gated)
    out_half, d_hidden_all = together((out_half, d_hidden_all))
    d_gated = dot(d_hidden_all, w_out, NN)
    out_away = away_rows(d_hidden_all, gated, out_got)
    out_away, d_gated = together((out_away, d_gated))
    out_landed = to_copies(out_away)
    d_mix, d_taps, d_out_gain, d_scalars = mixer_back(
        rank_arg, scalars, seg_all, p, taps, out_gain, inverse, update, d_gated, tokens
    )
    d_mix, gate_landed, out_landed = together((d_mix, gate_landed, out_landed))
    mix_columns = MIXW - EXTRA
    mix_half = weight_grad(normed, d_mix, 1, half, (), mix_columns)
    mix_got = lax.ppermute(mix_half, axes, core_pairs)
    mix_half, d_mix = together((mix_half, d_mix))
    d_normed, gain_one_grad = input_back(d_mix, w_mix, x_all, x_scale)
    gain_one_grad = gain_one_grad[0]
    d_normed, gain_one_grad, mix_got = together((d_normed, gain_one_grad, mix_got))
    mix_away = [
        weight_grad(normed, d_mix, at, block_rows, ((mix_got, at, 0),), mix_columns) for at in range(1, copies)
    ]
    mix_landed = to_copies(mix_away)
    d_input = lax.psum_scatter(d_normed, axes, axis_index_groups=cubes, scatter_dimension=0, tiled=True)
    mix_away, d_gate_part, d_up_part, activated, gated = together(
        (mix_away, d_gate_part, d_up_part, activated, gated)
    )

    def own_rows(left, right, got, column, landed, count=None):
        adds = ((got, 0, column),) + tuple((one, 0, 0) for one in landed)
        total = weight_grad(left, right, 0, block_rows, adds, count)
        return total.reshape(RANKS, rows, total.shape[1])

    up_rows = own_rows(normed_two, d_up_part, gate_got, FW, up_landed)
    gate_rows = own_rows(normed_two, d_gate_part, gate_got, 0, gate_landed)
    down_rows = own_rows(dy_all, activated, down_got, 0, down_landed)
    out_rows = own_rows(d_hidden_all, gated, out_got, 0, out_landed)
    out_rows, d_taps, d_scalars, d_out_gain, gain_two_grad = together(
        (out_rows, d_taps, d_scalars, d_out_gain, gain_two_grad)
    )
    tap_grad = jnp.zeros((CONV, tap_rows, conv_cols), F32)
    at = 0
    for first, width in ranges:
        start, count = own_channels(first, width)
        piece = d_taps[:, at : at + width].reshape(CONV, count, conv_cols)
        tap_grad = lax.dynamic_update_slice(tap_grad, piece, (0, start, 0))
        at = at + width
    small = jnp.zeros((D,), F32)
    small = lax.dynamic_update_slice(small, d_scalars[0, :HEADS], (rank * HEADS,))
    small = lax.dynamic_update_slice(small, d_scalars[0, HEADS : 2 * HEADS], (H + rank * HEADS,))
    small = lax.dynamic_update_slice(small, d_out_gain[0], (2 * H,))
    core_grad = jnp.concatenate(
        [
            jnp.zeros((D, conv_at), F32),
            tap_grad.reshape(D, conv_cols),
            small[:, None],
            jnp.zeros((D, EXTRA - conv_at - 1 - conv_cols), F32),
        ],
        axis=1,
    )
    lanes = jnp.arange(EXTRA)[None]
    extra_grad = (
        dot(normed, d_mix[:, MIXW - EXTRA :], TN)
        + jnp.where(lanes == 2 * H, gain_one_grad[:, None], 0.0)
        + jnp.where(lanes == 2 * H + 1, gain_two_grad.reshape(D, 1), 0.0)
        + order.relative(core_grad, 0)
    )
    extra_got = lax.ppermute(extra_grad[half:], axes, core_pairs)
    extra_sum = extra_grad[:half] + extra_got
    extra_landed = [
        lax.ppermute(extra_sum[at * block_rows : (at + 1) * block_rows], axes, pairs)
        for at, pairs in zip(range(1, copies), copy_pairs)
    ]
    extra_sum, out_rows = together((extra_sum, out_rows))
    grads_rest = home_rest(copies, (out_rows, gate_rows, up_rows, down_rows))
    if in_place:
        output, input_grad = finish(
            jnp.stack([core, dp]).astype(jnp.int32), copies, hidden, feed, d_input, x, d_hidden, gain_one
        )
    else:
        output = order.plain((hidden + feed.astype(F32)).astype(BF), 1)
        back, _ = norm_back(d_input.astype(F32), x.astype(F32), gain_one, EPS_NORM)
        input_grad = order.plain((d_hidden + back).astype(BF), 1)
    extra_rows = extra_sum[:block_rows]
    for one in extra_landed:
        extra_rows = extra_rows + one
    step_float = step[0].astype(F32)
    adam_scalars = jnp.stack(
        [beta_one[0], beta_two[0], learn_rate[0], 1 - beta_one[0] ** step_float, 1 - beta_two[0] ** step_float]
    )
    state = (moment_one, moment_two, master)
    done = adam(adam_scalars, grads_rest, state, None, MIX_END, 2048, 4)
    done = adam(adam_scalars, grads_rest, state, done, MIX_END + 4 * 2048, 2560, 5)
    done, extra_rows, output, input_grad, normed = together((done, extra_rows, output, input_grad, normed))
    mix_rows = own_rows(normed, d_mix, mix_got, 0, mix_landed, mix_columns)
    grads_mix, extra_rows = home(copies, mix_rows, extra_rows.reshape(RANKS, rows, EXTRA))
    done = adam(adam_scalars, extra_rows, state, done, EXTRA_START, EXTRA, 1)
    done = adam(adam_scalars, grads_mix, state, done, 0, 2048, 6)
    gain_grads = extra_rows[:, 2 * H : 2 * H + 2]
    return (output, input_grad) + tuple(done) + (gain_grads,)


def solution(mesh):
    by_token = P(("rep", "grp"), None)
    by_row = P(("grp", "rep"), None)
    return jax.shard_map(
        on_device,
        mesh=mesh,
        in_specs=(by_token, by_token, P(("rep", "grp")), by_row, by_row, by_row, by_row, P(), P(), P(), P()),
        out_specs=(by_token, by_token) + (by_row,) * 6,
        check_vma=False,
    )
```

```python
import functools

import jax
import jax.numpy as jnp
from jax import lax
from jax.experimental import pallas as pl
from jax.experimental.pallas import tpu as pltpu
from jax.sharding import PartitionSpec as P

D = 2048
H = 16
DK = 128
DV = 256
FF = 5632
CONV = 4
EXTRA = 128
KD = 2048
VD = 4096
MIX_END = 2 * KD + 2 * VD
FFN_START = MIX_END + VD
DOWN_START = FFN_START + 2 * FF
EXTRA_START = DOWN_START + FF
COLS = EXTRA_START + EXTRA

EPS_NORM = 1e-06
EPS_GATED = 1e-05
EPS_ADAM = 1e-08
DECAY_WEIGHT = 0.1
MESH = pl.DeviceIdType.MESH
BIG = 60 * 2**20

RANKS = 8
HEADS = H // RANKS
QW = HEADS * DK
VW = HEADS * DV
MIXW = 2 * QW + 2 * VW + EXTRA
OW = VW
TILES = FF // 128
FULL_RANKS = TILES - (TILES // RANKS) * RANKS
FT = TILES // RANKS + 1
FW = FT * 128
SPLIT = ((4, 1, 2), (1, 2, 4), (2, 4, 1))
MEET = ((2, 1, 4), (4, 2, 1), (1, 4, 2))
MEET_EARLY = ((2, 4, 1), (2, 1, 4))
BF = jnp.bfloat16
F32 = jnp.float32


def rank_of(rep, grp):
    return (grp // 2) * 4 + rep % 4


class Place:
    def __init__(self, copies):
        self.rep = lax.axis_index("rep")
        self.grp = lax.axis_index("grp")
        self.copies = copies
        self.dp = self.rep // 4
        self.core = self.grp % 2
        self.rank = rank_of(self.rep, self.grp)
        self.bits = {4: self.rank // 4, 2: self.rank // 2 % 2, 1: self.rank % 2}

    def flip(self, mask):
        total = 0
        for weight, bit in self.bits.items():
            total = total + weight * ((1 - bit) if mask & weight else bit)
        return total

    def peer(self, mask):
        rank = self.flip(mask)
        return (self.dp * 4 + rank % 4, (rank // 4) * 2 + self.core)

    def sibling(self):
        return (self.rep, self.grp + 1 - 2 * self.core)

    def copy_at(self, shift):
        return (((self.dp + shift) % self.copies) * 4 + self.rep % 4, self.grp)


def meet(devices):
    barrier = pltpu.get_barrier_semaphore()
    for device in devices:
        pl.semaphore_signal(barrier, inc=1, device_id=device, device_id_type=MESH)
    pl.semaphore_wait(barrier, len(devices))


def remote(src, dst, send, recv, device):
    return pltpu.make_async_remote_copy(
        src_ref=src, dst_ref=dst, send_sem=send, recv_sem=recv, device_id=device, device_id_type=MESH
    )


def row_parts(tokens, count):
    tiles = tokens // 16
    sizes = [16 * (tiles * (at + 1) // count - tiles * at // count) for at in range(count)]
    sizes.sort(reverse=True)
    return tuple((sum(sizes[:at]), sizes[at]) for at in range(count))


class Gather:
    def __init__(self, place, buf, parts, orders, send, recv):
        self.place, self.buf, self.parts, self.orders = place, buf, parts, orders
        self.send, self.recv = send, recv
        self.flights = {}

    def start(self, part, stage):
        order = self.orders[part]
        delta = order[stage]
        held = [0]
        for earlier in order[:stage]:
            held = held + [mask ^ earlier for mask in held]
        first, rows = self.parts[part]
        begin = 2**stage - 1
        here = []
        for at, mask in enumerate(held):
            block = self.buf.at[self.place.flip(mask), pl.ds(first, rows)]
            slot = begin + at
            copy = remote(
                block, block, self.send.at[part, slot], self.recv.at[part, slot], self.place.peer(delta)
            )
            copy.start()
            here.append(copy)
        self.flights[part, stage] = here

    def landed(self, part, stage):
        for copy in self.flights[part, stage]:
            copy.wait_recv()

    def finish(self):
        for here in self.flights.values():
            for copy in here:
                copy.wait_send()


class Scatter:
    def __init__(self, place, buf, land, parts, orders, send, recv):
        self.place, self.buf, self.land, self.parts, self.orders = place, buf, land, parts, orders
        self.send, self.recv = send, recv
        self.flights = {}
        self.sums = {}

    def held(self, part, stage, mask):
        first, rows = self.parts[part]
        if stage == 0:
            return self.buf.at[self.place.flip(mask), pl.ds(first, rows)]
        return self.land.at[self.sums[part, stage - 1][mask], pl.ds(first, rows)]

    def start(self, part, stage):
        order = self.orders[part]
        delta = order[stage]
        kept = [0]
        for later in order[stage + 1 :]:
            kept = kept + [mask ^ later for mask in kept]
        first, rows = self.parts[part]
        begin = (0, 4, 6)[stage]
        here = []
        for at, mask in enumerate(kept):
            slot = begin + at
            copy = remote(
                self.held(part, stage, mask ^ delta),
                self.land.at[slot, pl.ds(first, rows)],
                self.send.at[part, slot],
                self.recv.at[part, slot],
                self.place.peer(delta),
            )
            copy.start()
            here.append((copy, mask, slot))
        self.flights[part, stage] = here
        self.sums[part, stage] = {mask: slot for _, mask, slot in here}

    def add(self, part, stage):
        first, rows = self.parts[part]
        result = None
        for copy, mask, slot in self.flights[part, stage]:
            copy.wait_recv()
            total = self.held(part, stage, mask)[...].astype(F32) + self.land[
                slot, pl.ds(first, rows)
            ].astype(F32)
            if stage < 2:
                self.land[slot, pl.ds(first, rows)] = total.astype(BF)
            else:
                result = total
        return result

    def finish(self):
        for here in self.flights.values():
            for copy, _, _ in here:
                copy.wait_send()


def tile_start(rank):
    few = FT - 1
    return 128 * jnp.where(rank < FULL_RANKS, FT * rank, FULL_RANKS + few * rank)


def first_columns(rank):
    mixer = (
        (rank * QW, 0, QW),
        (KD + rank * QW, QW, QW),
        (2 * KD + rank * VW, 2 * QW, VW),
        (2 * KD + VD + rank * VW, 2 * QW + VW, VW),
        (EXTRA_START, 2 * QW + 2 * VW, EXTRA),
    )
    outward = ((MIX_END + rank * VW, 0, VW),)
    at = tile_start(rank)
    gates = ((FFN_START + at, 0, FW), (FFN_START + FF + at, FW, FW))
    down = ((DOWN_START + at, 0, FW),)
    return mixer, outward, gates, down


def feature_blocks(place):
    copies = place.copies
    width = D // (4 * copies)
    if width % 128:
        return [(0, 0, D)]
    found = []
    for core in range(2):
        for copy in range(copies):
            for x in range(2):
                block = (x * 2 + (place.core + core) % 2) * copies + (place.dp + copy) % copies
                found.append((block * width, ((core * copies + copy) * 2 + x) * width, width))
    return found


def columns(at, width):
    if not isinstance(at, int):
        at = pl.multiple_of(at, 128)
    return pl.ds(at, width)


def spread_kernel(copies, parts, w_ref, x_ref, dy_ref, s_ref, mix, outward, gates, down,
                  gates_side, down_side, xall, sall, x_own, dy_own,
                  pack, pack_sem, local, send, recv, seg_send, seg_recv,
                  ag_send, ag_recv, copy_send, copy_recv, core_send, core_recv, side_send, side_recv, turned):
    place = Place(copies)
    peers = [place.peer(mask) for mask in range(1, RANKS)]
    partners = [place.copy_at(shift) for shift in range(1, copies)]
    meet(peers + partners + [place.sibling()])
    me = place.rank
    targets = (mix.at[0, 0], outward.at[0, 0], gates, down)
    others = (None, None, gates_side, down_side)
    wide = (mix, outward)
    own = []
    firsts = (0, 5, 6, 8)
    packed = []
    for mask in range(RANKS):
        there = place.flip(mask)
        here = []
        for slot, (at, to, width) in enumerate(first_columns(there)[0]):
            copy = pltpu.make_async_copy(
                w_ref.at[:, columns(at, width)], pack.at[mask, :, pl.ds(to, width)], pack_sem.at[mask, slot]
            )
            copy.start()
            here.append(copy)
        packed.append(here)
    own_mix = pltpu.make_async_copy(pack.at[0], mix.at[0, 0, me], local.at[0])
    def send_group(group):
        flights = []
        for mask in range(1, RANKS):
            there = place.flip(mask)
            for slot, (at, to, width) in enumerate(first_columns(there)[group]):
                copy = remote(
                    w_ref.at[:, columns(at, width)],
                    targets[group].at[me, :, pl.ds(to, width)],
                    send.at[firsts[group] + slot, mask - 1],
                    recv.at[group, mask - 1],
                    place.peer(mask),
                )
                copy.start()
                flights.append(copy)
        return flights

    def got(group, mask):
        block = targets[group].at[place.flip(mask)]
        remote(block, block, send.at[0, mask - 1], recv.at[group, mask - 1], place.peer(mask)).wait_recv()

    sent = []
    onward = []

    def forward(group, mask, block):
        whole = wide[group]
        there = place.flip(mask)
        for shift in range(1, copies):
            copy = remote(
                block, whole.at[0, copies - shift, there],
                copy_send.at[group, shift - 1, mask], copy_recv.at[group, copies - shift - 1, mask],
                place.copy_at(shift),
            )
            copy.start()
            onward.append(copy)
        copy = remote(
            block, whole.at[1, 0, there],
            core_send.at[group, 0, mask], core_recv.at[group, 0, mask], place.sibling(),
        )
        copy.start()
        onward.append(copy)

    def got_and_forward(group, mask):
        got(group, mask)
        forward(group, mask, wide[group].at[0, 0, place.flip(mask)])

    def from_copies(group):
        whole = wide[group]
        for shift in range(1, copies):
            for mask in range(RANKS):
                there = place.flip(mask)
                block = whole.at[0, shift, there]
                remote(
                    block, block, copy_send.at[group, shift - 1, mask], copy_recv.at[group, shift - 1, mask],
                    place.copy_at(shift),
                ).wait_recv()
                copy = remote(
                    block, whole.at[1, shift, there],
                    core_send.at[group, shift, mask], core_recv.at[group, shift, mask], place.sibling(),
                )
                copy.start()
                onward.append(copy)

    def from_sibling(group):
        for shift in range(copies):
            for mask in range(RANKS):
                block = wide[group].at[1, shift, place.flip(mask)]
                remote(
                    block, block, core_send.at[group, shift, mask], core_recv.at[group, shift, mask], place.sibling()
                ).wait_recv()

    for mask in range(1, RANKS):
        for copy in packed[mask]:
            copy.wait()
        copy = remote(
            pack.at[mask], mix.at[0, 0, me], send.at[0, mask - 1], recv.at[0, mask - 1], place.peer(mask)
        )
        copy.start()
        sent.append(copy)
    for copy in packed[0]:
        copy.wait()
    own_mix.start()
    forward(0, 0, pack.at[0])
    turns = []
    for row, (source, target) in enumerate(((x_ref, xall.at[me]), (x_ref, x_own), (dy_ref, dy_own))):
        here = []
        for slot, (at, to, width) in enumerate(feature_blocks(place)):
            copy = pltpu.make_async_copy(
                source.at[:, columns(at, width)], target.at[:, pl.ds(to, width)], turned.at[row, slot]
            )
            copy.start()
            here.append(copy)
        turns.append(here)
    own_s = pltpu.make_async_copy(s_ref, sall.at[me], local.at[10])
    own_s.start()

    for group in range(1, 4):
        here = []
        for slot, (at, to, width) in enumerate(first_columns(me)[group]):
            copy = pltpu.make_async_copy(
                w_ref.at[:, columns(at, width)], targets[group].at[me, :, pl.ds(to, width)],
                local.at[firsts[group] + slot],
            )
            copy.start()
            here.append(copy)
        own.append(here)
    own_s.wait()
    seg_flights = []
    for mask in range(1, RANKS):
        copy = remote(s_ref, sall.at[me], seg_send.at[mask - 1], seg_recv.at[mask - 1], place.peer(mask))
        copy.start()
        seg_flights.append(copy)
    sent = sent + send_group(1)
    for mask in range(1, RANKS):
        got_and_forward(0, mask)
    for copy in turns[0]:
        copy.wait()
    gather = Gather(place, xall, parts, MEET_EARLY, ag_send, ag_recv)
    for part in range(len(parts)):
        gather.start(part, 0)
    for group in range(2, 4):
        sent = sent + send_group(group)
    for copy in own[0]:
        copy.wait()
    forward(1, 0, wide[1].at[0, 0, me])
    for mask in range(1, RANKS):
        got_and_forward(1, mask)
    for stage in range(3):
        for part in range(len(parts)):
            gather.landed(part, stage)
            if stage < 2:
                gather.start(part, stage + 1)
    from_copies(0)
    from_copies(1)
    for group in range(2, 4):
        for copy in own[group - 1]:
            copy.wait()
        for mask in range(RANKS):
            if mask:
                got(group, mask)
            copy = remote(
                targets[group].at[place.flip(mask)], others[group].at[place.flip(mask)],
                side_send.at[group - 2, mask], side_recv.at[group - 2, mask], place.sibling(),
            )
            copy.start()
            onward.append(copy)
    for group in range(2, 4):
        for mask in range(RANKS):
            block = others[group].at[place.flip(mask)]
            remote(
                block, block, side_send.at[group - 2, mask], side_recv.at[group - 2, mask], place.sibling()
            ).wait_recv()
    from_sibling(0)
    from_sibling(1)
    for copy in seg_flights:
        copy.wait()
    own_mix.wait()
    for here in turns[1:]:
        for copy in here:
            copy.wait()
    for copy in sent + onward:
        copy.wait_send()
    gather.finish()


def any_spec():
    return pl.BlockSpec(memory_space=pl.ANY)


def vmem_spec():
    return pl.BlockSpec(memory_space=pltpu.VMEM)


def takes(micros):
    return pl.CostEstimate(flops=0, bytes_accessed=int(micros * 1e3), transcendentals=0)


def dma(*shape):
    return pltpu.SemaphoreType.DMA(shape)


def spread(copies, weights, x, dy, seg):
    rows = weights.shape[0]
    tokens = x.shape[0]
    shape = jax.ShapeDtypeStruct
    return pl.pallas_call(
        functools.partial(spread_kernel, copies, ((0, tokens // 2), (tokens // 2, tokens // 2))),
        out_shape=(
            shape((2, copies, RANKS, rows, MIXW), BF),
            shape((2, copies, RANKS, rows, OW), BF),
        )
        + (
            shape((RANKS, rows, 2 * FW), BF),
            shape((RANKS, rows, FW), BF),
        )
        * 2
        + (
            shape((RANKS, tokens, D), BF),
            shape((RANKS,) + seg.shape, seg.dtype),
            shape((tokens, D), BF),
            shape((tokens, D), BF),
        ),
        in_specs=[any_spec(), vmem_spec(), vmem_spec(), any_spec()],
        out_specs=[any_spec()] * 10,
        scratch_shapes=[
            pltpu.VMEM((RANKS, rows, MIXW), BF), dma(RANKS, 5), dma(11), dma(9, RANKS - 1), dma(4, RANKS - 1),
            dma(RANKS - 1), dma(RANKS - 1), dma(3, 7), dma(3, 7),
            dma(2, copies - 1, RANKS), dma(2, copies - 1, RANKS), dma(2, copies, RANKS), dma(2, copies, RANKS),
            dma(2, RANKS), dma(2, RANKS), dma(3, 4 * copies),
        ],
        compiler_params=pltpu.CompilerParams(collective_id=1, has_side_effects=True, vmem_limit_bytes=BIG),
        cost_estimate=takes(5),
        name="spread",
    )(weights, x, dy, seg)


def norm_scale(values, epsilon):
    return lax.rsqrt(jnp.mean(values * values, axis=-1, keepdims=True) + epsilon)


def sum_then_gather(scatter, gather, finish_rows):
    parts = range(len(scatter.parts))
    for part in parts:
        scatter.start(part, 0)
    for stage in range(2):
        for part in parts:
            scatter.add(part, stage)
            scatter.start(part, stage + 1)
    for part in parts:
        finish_rows(part, scatter.add(part, 2))
        gather.start(part, 0)
    for stage in range(3):
        for part in parts:
            gather.landed(part, stage)
            if stage < 2:
                gather.start(part, stage + 1)
    scatter.finish()
    gather.finish()


def branch_kernel(copies, parts, part_ref, x_ref, gain_ref, hidden_ref, nall, land,
                  send, recv, ag_send, ag_recv):
    place = Place(copies)
    meet([place.peer(mask) for mask in (4, 2, 1)])
    me = place.rank
    scatter = Scatter(place, part_ref, land, parts, SPLIT, send, recv)
    gather = Gather(place, nall, parts, MEET, ag_send, ag_recv)

    def finish_rows(part, total):
        first, rows = parts[part]
        hidden = x_ref[pl.ds(first, rows)].astype(F32) + total
        hidden_ref[pl.ds(first, rows)] = hidden
        unit = hidden * norm_scale(hidden, EPS_NORM)
        nall[me, pl.ds(first, rows)] = (unit * gain_ref[...]).astype(BF)

    sum_then_gather(scatter, gather, finish_rows)


def cube_scratch(tokens):
    return [pltpu.VMEM((7, tokens, D), BF), dma(3, 7), dma(3, 7)]


def branch(copies, partial, x, gain):
    tokens = x.shape[0]
    shape = jax.ShapeDtypeStruct
    return pl.pallas_call(
        functools.partial(branch_kernel, copies, row_parts(tokens, 3)),
        out_shape=(shape((tokens, D), F32), shape((RANKS, tokens, D), BF)),
        in_specs=[vmem_spec()] * 3,
        out_specs=[vmem_spec()] * 2,
        scratch_shapes=cube_scratch(tokens) + [dma(3, 7), dma(3, 7)],
        compiler_params=pltpu.CompilerParams(collective_id=2, has_side_effects=True, vmem_limit_bytes=BIG),
        cost_estimate=takes(5),
        name="branch",
    )(partial, x, gain)


def norm_back(grad, values, gain, epsilon):
    scale = norm_scale(values, epsilon)
    unit = values * scale
    scaled = grad * gain
    back = scale * (scaled - unit * jnp.mean(scaled * unit, axis=1, keepdims=True))
    return back, grad * unit


def hidden_back_kernel(copies, parts, part_ref, h_ref, dy_ref, gain_ref, dh_ref, gain_grad, dall, land,
                       send, recv, ag_send, ag_recv):
    place = Place(copies)
    meet([place.peer(mask) for mask in (4, 2, 1)])
    me = place.rank
    scatter = Scatter(place, part_ref, land, parts, SPLIT, send, recv)
    gather = Gather(place, dall, parts, MEET, ag_send, ag_recv)
    gain_grad[...] = jnp.zeros_like(gain_grad)

    def finish_rows(part, total):
        first, rows = parts[part]
        back, gain_part = norm_back(total, h_ref[pl.ds(first, rows)], gain_ref[...], EPS_NORM)
        back = dy_ref[pl.ds(first, rows)].astype(F32) + back
        dh_ref[pl.ds(first, rows)] = back
        dall[me, pl.ds(first, rows)] = back.astype(BF)
        gain_grad[...] += jnp.sum(gain_part, axis=0, keepdims=True)

    sum_then_gather(scatter, gather, finish_rows)


def hidden_back(copies, partial, hidden, dy, gain):
    tokens = dy.shape[0]
    shape = jax.ShapeDtypeStruct
    return pl.pallas_call(
        functools.partial(hidden_back_kernel, copies, row_parts(tokens, 3)),
        out_shape=(shape((tokens, D), F32), shape((1, D), F32), shape((RANKS, tokens, D), BF)),
        in_specs=[vmem_spec()] * 4,
        out_specs=[vmem_spec()] * 3,
        scratch_shapes=cube_scratch(tokens) + [dma(3, 7), dma(3, 7)],
        compiler_params=pltpu.CompilerParams(collective_id=3, has_side_effects=True, vmem_limit_bytes=BIG),
        cost_estimate=takes(5),
        name="hidden_back",
    )(partial, hidden, dy, gain)


class Home:
    def __init__(self, place, groups, ins, out, local, send, recv):
        self.place, self.groups, self.ins, self.out = place, groups, ins, out
        self.local, self.send, self.recv = local, send, recv

    def pieces(self, rank):
        found = []
        for group, source in zip(self.groups, self.ins):
            for at, to, width in first_columns(rank)[group]:
                if group == 0 and to == 2 * QW + 2 * VW:
                    continue
                if group == 2:
                    found.append((source[to // FW], 0, at, width - 128, False))
                    found.append((source[to // FW], width - 128, at + width - 128, 128, True))
                elif group == 3:
                    found.append((source, 0, at, width - 128, False))
                    found.append((source, width - 128, at + width - 128, 128, True))
                else:
                    found.append((source, to, at, width, False))
        return found

    def when(self, flag, rank, act):
        if flag:
            pl.when(rank < FULL_RANKS)(act)
        else:
            act()

    def run(self, method):
        place = self.place
        me = place.rank
        for slot, (source, to, at, width, flag) in enumerate(self.pieces(me)):
            copy = pltpu.make_async_copy(
                source.at[me, :, pl.ds(to, width)],
                self.out.at[:, columns(at, width)],
                self.local.at[slot],
            )
            self.when(flag, me, getattr(copy, method))
        for mask in range(1, RANKS):
            there = place.flip(mask)
            for slot, (source, to, at, width, flag) in enumerate(self.pieces(me)):
                copy = remote(
                    source.at[there, :, pl.ds(to, width)],
                    self.out.at[:, columns(at, width)],
                    self.send.at[mask - 1, slot],
                    self.recv.at[mask - 1, slot],
                    place.peer(mask),
                )
                self.when(flag, me, copy.start if method == "start" else copy.wait_send)
            if method == "wait":
                for slot, (source, to, at, width, flag) in enumerate(self.pieces(there)):
                    block = self.out.at[:, columns(at, width)]
                    copy = remote(
                        block, block, self.send.at[mask - 1, slot], self.recv.at[mask - 1, slot], place.peer(mask)
                    )
                    self.when(flag, there, copy.wait_recv)


def home_scratch():
    return [dma(7), dma(RANKS - 1, 7), dma(RANKS - 1, 7)]


def home_kernel(copies, mix_ref, extra_ref, out, extra_out, local, send, recv, land, own, far, near):
    place = Place(copies)
    meet([place.peer(mask) for mask in range(1, RANKS)])
    way = Home(place, (0,), (mix_ref,), out, local, send, recv)
    flights = []
    for mask in range(1, RANKS):
        copy = remote(
            extra_ref.at[place.flip(mask)], land.at[mask - 1], far.at[mask - 1], near.at[mask - 1], place.peer(mask)
        )
        copy.start()
        flights.append(copy)
    way.run("start")
    mine = pltpu.make_async_copy(extra_ref.at[place.rank], own, local.at[6])
    mine.start()
    mine.wait()
    total = own[...]
    for mask in range(1, RANKS):
        flights[mask - 1].wait_recv()
        total = total + land[mask - 1]
    extra_out[...] = total
    for copy in flights:
        copy.wait_send()
    way.run("wait")


def home(copies, array, extra):
    rows = array.shape[1]
    shape = jax.ShapeDtypeStruct
    return pl.pallas_call(
        functools.partial(home_kernel, copies),
        out_shape=(shape((rows, MIX_END), BF), shape((rows, EXTRA), F32)),
        in_specs=[any_spec()] * 2,
        out_specs=(any_spec(), vmem_spec()),
        scratch_shapes=home_scratch()
        + [pltpu.VMEM((RANKS - 1, rows, EXTRA), F32), pltpu.VMEM((rows, EXTRA), F32), dma(RANKS - 1), dma(RANKS - 1)],
        compiler_params=pltpu.CompilerParams(collective_id=6, has_side_effects=True, vmem_limit_bytes=BIG),
        cost_estimate=takes(5),
        name="home",
    )(array, extra)


def home_rest_kernel(copies, out_rows, gate_rows, up_rows, down_rows, rest, local, send, recv):
    place = Place(copies)
    meet([place.peer(mask) for mask in range(1, RANKS)])
    way = Home(place, (1, 2, 3), (out_rows, (gate_rows, up_rows), down_rows), rest, local, send, recv)
    way.run("start")
    way.run("wait")


def home_rest(copies, grad_rows):
    rows = grad_rows[0].shape[1]
    return pl.pallas_call(
        functools.partial(home_rest_kernel, copies),
        out_shape=jax.ShapeDtypeStruct((rows, EXTRA_START), BF),
        in_specs=[any_spec()] * 4,
        out_specs=any_spec(),
        scratch_shapes=home_scratch(),
        compiler_params=pltpu.CompilerParams(collective_id=4, has_side_effects=True, vmem_limit_bytes=BIG),
        cost_estimate=takes(5),
        name="home_rest",
    )(*grad_rows)


def dot(left, right, axes):
    return lax.dot_general(left, right, (axes, ((), ())), preferred_element_type=F32)


def halves(values):
    high = values.astype(BF)
    return high, (values - high.astype(F32)).astype(BF)


def mul(left, right, axes):
    (left_axis,), (right_axis,) = axes
    both = jnp.concatenate(halves(right), axis=1 - right_axis)
    total = dot(
        jnp.concatenate(halves(left), axis=left_axis), jnp.concatenate([both, both], axis=right_axis), axes
    )
    width = right.shape[1 - right_axis]
    return total[:, :width] + total[:, width:]


def mul_mask(mask, right, axes):
    (left_axis,), (right_axis,) = axes
    return dot(
        jnp.concatenate([mask, mask], axis=left_axis), jnp.concatenate(halves(right), axis=right_axis), axes
    )


NN = ((1,), (0,))
NT = ((1,), (1,))
TN = ((0,), (0,))


def unit_lower_inverses(lowers, row, col):
    size = lowers[0].shape[0]
    pair = (row >> 1) == (col >> 1)
    inverses = [jnp.where(row == col, 1.0, jnp.where(pair, -lower, 0.0)) for lower in lowers]
    level = 1
    while 2**level < size:
        joined = ((row >> (level + 1)) == (col >> (level + 1))) & ((row >> level) != (col >> level))
        parts = [mul(jnp.where(joined, lower, 0.0), inverse, NN) for lower, inverse in zip(lowers, inverses)]
        inverses = [inverse - mul(inverse, part, NN) for inverse, part in zip(inverses, parts)]
        level = level + 1
    return inverses


class Sequence:
    def __init__(self, seg_row):
        tokens = seg_row.shape[1]
        self.tokens = tokens
        shape = (tokens, tokens)
        self.row = lax.broadcasted_iota(jnp.int32, shape, 0)
        self.col = lax.broadcasted_iota(jnp.int32, shape, 1)
        ids = jnp.broadcast_to(seg_row.astype(F32), shape)
        turned = ids.T
        same = turned == ids
        self.inclusive = same & (self.row >= self.col)
        self.strict = same & (self.row > self.col)
        self.lower = (self.row >= self.col).astype(BF)
        column = turned[:, :1]
        at = self.row[:, :1]
        self.near = [None]
        for back in range(1, CONV):
            before = pltpu.roll(turned, back, 0)[:, :1]
            self.near.append(((before == column) & (at >= back)).astype(F32))

    def conv(self, taps, values):
        total = taps[CONV - 1 : CONV] * values
        for back in range(1, CONV):
            total = total + taps[CONV - 1 - back : CONV - back] * (
                self.near[back] * pltpu.roll(values, back, 0)
            )
        return total

    def conv_back(self, taps, values, grad):
        total = taps[CONV - 1 : CONV] * grad
        rows = [jnp.sum(values * grad, axis=0, keepdims=True)]
        for back in range(1, CONV):
            masked = self.near[back] * grad
            total = total + taps[CONV - 1 - back : CONV - back] * pltpu.roll(
                masked, self.tokens - back, 0
            )
            rows.append(jnp.sum(masked * pltpu.roll(values, back, 0), axis=0, keepdims=True))
        return total, jnp.concatenate(rows[::-1], axis=0)


def pick_lane(block, lane):
    at = lax.broadcasted_iota(jnp.int32, block.shape, 1)
    return jnp.sum(jnp.where(at == lane, block, 0.0), axis=1, keepdims=True)


def softplus(values):
    return jnp.maximum(values, 0.0) + jnp.log1p(jnp.exp(-jnp.abs(values)))


class Head:
    def __init__(self, seq, head, rank, scalars, p_ref, taps_ref):
        q_at, k_at = head * DK, QW + head * DK
        v_at, g_at = 2 * QW + head * DV, 2 * QW + VW + head * DV
        self.q_at, self.k_at, self.v_at, self.g_at = q_at, k_at, v_at, g_at
        self.raw = [p_ref[:, q_at : q_at + DK], p_ref[:, k_at : k_at + DK], p_ref[:, v_at : v_at + DV]]
        self.taps = [taps_ref[:, q_at : q_at + DK], taps_ref[:, k_at : k_at + DK], taps_ref[:, v_at : v_at + DV]]
        self.pre = [seq.conv(taps, raw) for taps, raw in zip(self.taps, self.raw)]
        self.sig = [jax.nn.sigmoid(pre) for pre in self.pre]
        conv_q, conv_k, self.v = [pre * sig for pre, sig in zip(self.pre, self.sig)]
        self.q_scale = lax.rsqrt(jnp.sum(conv_q * conv_q, axis=1, keepdims=True) + EPS_NORM)
        self.k_scale = lax.rsqrt(jnp.sum(conv_k * conv_k, axis=1, keepdims=True) + EPS_NORM)
        self.q_unit = conv_q * self.q_scale
        self.q = self.q_unit * DK**-0.5
        self.k = conv_k * self.k_scale
        pair = p_ref[:, 2 * QW + 2 * VW :]
        self.lane_a = rank * HEADS + head
        self.lane_b = H + rank * HEADS + head
        self.a = pick_lane(pair, self.lane_a) + scalars[HEADS + head]
        self.rate = scalars[head]
        self.beta = jax.nn.sigmoid(pick_lane(pair, self.lane_b))
        self.decay = -self.rate * softplus(self.a)
        spread_out = jnp.where(seq.row > seq.col, jnp.broadcast_to(self.decay, seq.row.shape), 0.0)
        gap = mul_mask(seq.lower, spread_out, NN)
        self.pairs = jnp.where(seq.inclusive, jnp.exp(jnp.where(seq.inclusive, gap, 0.0)), 0.0)
        self.kk = mul(self.k, self.k, NT)
        self.qk = mul(self.q, self.k, NT)
        self.strict_pairs = jnp.where(seq.strict, self.pairs, 0.0)
        self.lower = self.beta * self.strict_pairs * self.kk
        self.attend = self.pairs * self.qk
        self.gate = p_ref[:, g_at : g_at + DV]


TOGETHER = 4
TOGETHER_BACK = 2


def in_turns(bodies):
    bodies = list(bodies)
    while bodies:
        bodies = [body for body in bodies if next(body, None) is not None]


def mixer_kernel(tokens, rank_ref, scalars, seg_ref, p_ref, taps_ref, gain_ref, z_ref, inv_ref, upd_ref):
    rank = rank_ref[0]
    places = [(at, head) for at in range(TOGETHER) for head in range(HEADS)]
    seqs = [Sequence(seg_ref[at, :1]) for at in range(TOGETHER)]
    ones = [
        Head(seqs[at], head, rank, scalars, p_ref.at[pl.ds(at * tokens, tokens)], taps_ref) for at, head in places
    ]
    inverses = unit_lower_inverses([one.lower for one in ones], seqs[0].row, seqs[0].col)
    updates = [mul(inverse, one.beta * one.v, NN) for inverse, one in zip(inverses, ones)]
    outs = [mul(one.attend, update, NN) for one, update in zip(ones, updates)]
    for (at, head), one, inverse, update, out in zip(places, ones, inverses, updates, outs):
        normed = out * norm_scale(out, EPS_GATED) * gain_ref[...]
        z_ref[pl.ds(at * tokens, tokens), head * DV : (head + 1) * DV] = (
            normed * (one.gate * jax.nn.sigmoid(one.gate))
        ).astype(BF)
        inv_ref[at, head] = inverse
        upd_ref[at, head] = update


def mixer_back_kernel(tokens, rank_ref, scalars, seg_ref, p_ref, taps_ref, gain_ref, inv_ref, upd_ref, dz_ref,
                      dp_ref, dtaps_ref, dgain_ref, dscal_ref):
    @pl.when(pl.program_id(0) == 0)
    def _():
        dtaps_ref[...] = jnp.zeros_like(dtaps_ref)
        dgain_ref[...] = jnp.zeros_like(dgain_ref)
        dscal_ref[...] = jnp.zeros_like(dscal_ref)

    rank = rank_ref[0]
    lane = lax.broadcasted_iota(jnp.int32, (tokens, EXTRA), 1)
    scal_row = lax.broadcasted_iota(jnp.int32, (8, 128), 0)
    scal_col = lax.broadcasted_iota(jnp.int32, (8, 128), 1)
    pair_grads = [jnp.zeros((tokens, EXTRA), F32) for _ in range(TOGETHER_BACK)]
    scal = [jnp.zeros((8, 128), F32)]
    sums = {}

    def add_to(key, value):
        sums[key] = sums[key] + value if key in sums else value

    def body(at, seq, head):
        mine = pl.ds(at * tokens, tokens)
        one = Head(seq, head, rank, scalars, p_ref.at[mine], taps_ref)
        yield True
        inverse = inv_ref[at, head]
        update = upd_ref[at, head]
        out = mul(one.attend, update, NN)
        yield True
        dz = dz_ref[mine, head * DV : (head + 1) * DV]
        scale = norm_scale(out, EPS_GATED)
        normed = out * scale
        sig = jax.nn.sigmoid(one.gate)
        gate = one.gate * sig
        d_gate = dz * normed * gain_ref[...] * (sig * (1 + one.gate * (1 - sig)))
        dp_ref[mine, one.g_at : one.g_at + DV] = d_gate.astype(BF)
        add_to("gain", jnp.sum(dz * normed * gate, axis=0, keepdims=True))
        d_normed = dz * gain_ref[...] * gate
        d_out = scale * (d_normed - normed * jnp.mean(d_normed * normed, axis=1, keepdims=True))
        yield True
        d_update = mul(one.attend, d_out, TN)
        yield True
        d_attend = jnp.where(seq.inclusive, mul(d_out, update, NT), 0.0)
        yield True
        d_scaled = mul(inverse, d_update, TN)
        yield True
        d_qk = d_attend * one.pairs
        d_q = mul(d_qk, one.k, NN)
        yield True
        d_lower = jnp.where(seq.strict, -mul(d_scaled, update, NT), 0.0)
        yield True
        d_k = mul(d_qk, one.q, TN)
        d_v = one.beta * d_scaled
        d_beta = jnp.sum(d_scaled * one.v, axis=1, keepdims=True) + jnp.sum(
            d_lower * one.strict_pairs * one.kk, axis=1, keepdims=True
        )
        d_gap = d_attend * one.attend + d_lower * one.lower
        d_kk = d_lower * (one.beta * one.strict_pairs)
        yield True
        d_k = d_k + mul(d_kk, one.k, NN) + mul(d_kk, one.k, TN)
        yield True
        reach = mul_mask(seq.lower, d_gap, TN)
        yield True
        d_decay = jnp.sum(jnp.where(seq.row > seq.col, reach, 0.0), axis=1, keepdims=True)
        d_a = d_decay * (-one.rate) * jax.nn.sigmoid(one.a)
        d_b = d_beta * one.beta * (1 - one.beta)
        pair_grads[at] = (
            pair_grads[at] + jnp.where(lane == one.lane_a, d_a, 0.0) + jnp.where(lane == one.lane_b, d_b, 0.0)
        )
        sum_rate = jnp.sum(d_decay * one.decay, axis=0, keepdims=True)
        sum_a = jnp.sum(d_a, axis=0, keepdims=True)
        scal[0] = scal[0] + jnp.where((scal_row == 0) & (scal_col == head), sum_rate, 0.0)
        scal[0] = scal[0] + jnp.where((scal_row == 0) & (scal_col == HEADS + head), sum_a, 0.0)
        dq_unit = d_q * DK**-0.5
        dc_q = one.q_scale * (dq_unit - one.q_unit * jnp.sum(dq_unit * one.q_unit, axis=1, keepdims=True))
        dc_k = one.k_scale * (d_k - one.k * jnp.sum(d_k * one.k, axis=1, keepdims=True))
        for grad, pre, sig, raw, taps, first, width in (
            (dc_q, one.pre[0], one.sig[0], one.raw[0], one.taps[0], one.q_at, DK),
            (dc_k, one.pre[1], one.sig[1], one.raw[1], one.taps[1], one.k_at, DK),
            (d_v, one.pre[2], one.sig[2], one.raw[2], one.taps[2], one.v_at, DV),
        ):
            d_pre = grad * (sig * (1 + pre * (1 - sig)))
            d_raw, d_taps = seq.conv_back(taps, raw, d_pre)
            dp_ref[mine, first : first + width] = d_raw.astype(BF)
            add_to((first, width), d_taps)
            yield True

    seqs = [Sequence(seg_ref[at, :1]) for at in range(TOGETHER_BACK)]
    in_turns(body(at, seqs[at], head) for at in range(TOGETHER_BACK) for head in range(HEADS))
    for key, value in sums.items():
        if key == "gain":
            dgain_ref[...] += value
        else:
            first, width = key
            dtaps_ref[:, first : first + width] += value
    for at in range(TOGETHER_BACK):
        dp_ref[pl.ds(at * tokens, tokens), 2 * QW + 2 * VW :] = pair_grads[at].astype(BF)
    dscal_ref[...] += scal[0]


def smem_spec():
    return pl.BlockSpec(memory_space=pltpu.SMEM)


def by_sequence(*shape):
    rest = (0,) * (len(shape) - 1)
    return pl.BlockSpec(shape, lambda at: (at,) + rest)


def whole_block(*shape):
    return pl.BlockSpec(shape, lambda at: (0,) * len(shape))


CHANNELS = 2 * QW + VW


def mixer(rank, scalars, seg, p, taps, gain, tokens):
    count = p.shape[0] // tokens
    shape = jax.ShapeDtypeStruct
    return pl.pallas_call(
        functools.partial(mixer_kernel, tokens),
        grid=(count // TOGETHER,),
        out_shape=(
            shape((p.shape[0], VW), BF),
            shape((count, HEADS, tokens, tokens), F32),
            shape((count, HEADS, tokens, DV), F32),
        ),
        in_specs=[
            smem_spec(), smem_spec(), by_sequence(TOGETHER, 8, tokens), by_sequence(TOGETHER * tokens, MIXW),
            whole_block(CONV, CHANNELS), whole_block(1, DV),
        ],
        out_specs=[
            by_sequence(TOGETHER * tokens, VW), by_sequence(TOGETHER, HEADS, tokens, tokens),
            by_sequence(TOGETHER, HEADS, tokens, DV),
        ],
        compiler_params=pltpu.CompilerParams(vmem_limit_bytes=BIG),
        cost_estimate=takes(5),
        name="mixer",
    )(rank, scalars, seg, p, taps, gain)


def mixer_back(rank, scalars, seg, p, taps, gain, inverse, update, dz, tokens):
    count = p.shape[0] // tokens
    shape = jax.ShapeDtypeStruct
    return pl.pallas_call(
        functools.partial(mixer_back_kernel, tokens),
        grid=(count // TOGETHER_BACK,),
        out_shape=(
            shape((p.shape[0], MIXW), BF),
            shape((CONV, CHANNELS), F32),
            shape((1, DV), F32),
            shape((8, 128), F32),
        ),
        in_specs=[
            smem_spec(), smem_spec(), by_sequence(TOGETHER_BACK, 8, tokens), by_sequence(TOGETHER_BACK * tokens, MIXW),
            whole_block(CONV, CHANNELS), whole_block(1, DV),
            by_sequence(TOGETHER_BACK, HEADS, tokens, tokens), by_sequence(TOGETHER_BACK, HEADS, tokens, DV),
            by_sequence(TOGETHER_BACK * tokens, VW),
        ],
        out_specs=[
            by_sequence(TOGETHER_BACK * tokens, MIXW), whole_block(CONV, CHANNELS), whole_block(1, DV),
            whole_block(8, 128),
        ],
        compiler_params=pltpu.CompilerParams(vmem_limit_bytes=BIG),
        cost_estimate=takes(5),
        name="mixer_back",
    )(rank, scalars, seg, p, taps, gain, inverse, update, dz)


def adam_kernel(filled, scalars, grad_ref, one_ref, two_ref, master_ref, *refs):
    grad_out, one_out, two_out, master_out, weight_out = refs[filled:]
    beta_one, beta_two, rate = scalars[0], scalars[1], scalars[2]
    grad = grad_ref[...].astype(F32)
    one = beta_one * one_ref[...] + (1 - beta_one) * grad
    two = beta_two * two_ref[...] + (1 - beta_two) * grad * grad
    master = master_ref[...]
    change = (one / scalars[3]) / (jnp.sqrt(two / scalars[4]) + EPS_ADAM) + DECAY_WEIGHT * master
    master = master - rate * change
    grad_out[...] = grad
    one_out[...] = one
    two_out[...] = two
    master_out[...] = master
    weight_out[...] = master.astype(BF)


def adam(scalars, grads, state, done, first, width, count):
    rows = grads.shape[0]
    at_first = first // width
    grad_first = at_first if grads.shape[1] > first else 0
    shape = jax.ShapeDtypeStruct
    there = pl.BlockSpec((rows, width), lambda at: (0, at + at_first))
    filled = () if done is None else tuple(done)
    return pl.pallas_call(
        functools.partial(adam_kernel, len(filled)),
        grid=(count,),
        out_shape=(shape((rows, COLS), F32),) * 4 + (shape((rows, COLS), BF),),
        in_specs=[smem_spec(), pl.BlockSpec((rows, width), lambda at: (0, at + grad_first))]
        + [there] * 3 + [any_spec()] * len(filled),
        out_specs=[there] * 5,
        input_output_aliases={5 + at: at for at in range(len(filled))},
        compiler_params=pltpu.CompilerParams(vmem_limit_bytes=BIG),
        cost_estimate=takes(5),
        name="adam",
    )(scalars, grads, *state, *filled)


def weight_grad_kernel(left_ref, right_ref, *refs):
    total = dot(left_ref[...], right_ref[...], TN)
    for ref in refs[:-1]:
        total = total + ref[...].astype(F32)
    refs[-1][...] = total.astype(BF)


def weight_grad(left, right, at, width, adds=(), count=None):
    tokens = right.shape[0]
    count = right.shape[1] if count is None else count
    tile = 768 if count % 768 == 0 else count

    def add_spec(row, column):
        return pl.BlockSpec((width, tile), lambda step: (row, step + column // tile))

    return pl.pallas_call(
        weight_grad_kernel,
        grid=(count // tile,),
        out_shape=jax.ShapeDtypeStruct((width, count), BF),
        in_specs=[
            pl.BlockSpec((tokens, width), lambda step: (0, at)),
            pl.BlockSpec((tokens, tile), lambda step: (0, step)),
        ]
        + [add_spec(row, column) for _, row, column in adds],
        out_specs=pl.BlockSpec((width, tile), lambda step: (0, step)),
        compiler_params=pltpu.CompilerParams(vmem_limit_bytes=BIG),
        cost_estimate=takes(1),
        name="weight_grad",
    )(left, right, *[array for array, _, _ in adds])


def input_back_kernel(grad_ref, w_ref, x_ref, scale_ref, out_ref, gain_ref):
    grad = dot(grad_ref[...], w_ref[...], NT)
    out_ref[...] = grad.astype(BF)
    unit = x_ref[...].astype(F32) * scale_ref[:, :1]
    gain_ref[...] = jnp.sum(grad * unit, axis=0, keepdims=True)


def input_back(grad, w, x, scale):
    tokens, count = grad.shape
    tile = 512
    shape = jax.ShapeDtypeStruct
    return pl.pallas_call(
        input_back_kernel,
        grid=(D // tile,),
        out_shape=(shape((tokens, D), BF), shape((1, D), F32)),
        in_specs=[
            whole_block(tokens, count),
            pl.BlockSpec((tile, count), lambda step: (step, 0)),
            pl.BlockSpec((tokens, tile), lambda step: (0, step)),
            whole_block(tokens, 128),
        ],
        out_specs=[
            pl.BlockSpec((tokens, tile), lambda step: (0, step)), pl.BlockSpec((1, tile), lambda step: (0, step)),
        ],
        compiler_params=pltpu.CompilerParams(vmem_limit_bytes=BIG),
        cost_estimate=takes(1),
        name="input_back",
    )(grad, w, x, scale)


def project_kernel(x_ref, w_ref, normed_ref, p_ref, gains_ref, scale_ref, gain):
    @pl.when(pl.program_id(0) == 0)
    def _():
        row = lax.broadcasted_iota(jnp.int32, (8, EXTRA), 0)
        col = lax.broadcasted_iota(jnp.int32, (8, EXTRA), 1)
        pick = (col == row + 2 * H).astype(BF)
        gain[...] = dot(pick, w_ref[:, MIXW - EXTRA :], NT)
        gains_ref[...] = gain[...]

    x = x_ref[...].astype(F32)
    scale = norm_scale(x, EPS_NORM)
    scale_ref[...] = jnp.broadcast_to(scale, scale_ref.shape)
    normed = (x * scale * gain[:1]).astype(BF)
    normed_ref[...] = normed
    p_ref[...] = dot(normed, w_ref[...], NN)


def project(x, w):
    count = x.shape[0]
    rows = 512 if count % 512 == 0 else 256
    shape = jax.ShapeDtypeStruct
    return pl.pallas_call(
        project_kernel,
        grid=(count // rows,),
        out_shape=(shape((count, D), BF), shape((count, MIXW), F32), shape((8, D), F32), shape((count, 128), F32)),
        in_specs=[by_sequence(rows, D), whole_block(D, MIXW)],
        out_specs=[by_sequence(rows, D), by_sequence(rows, MIXW), whole_block(8, D), by_sequence(rows, 128)],
        scratch_shapes=[pltpu.VMEM((8, D), F32)],
        compiler_params=pltpu.CompilerParams(vmem_limit_bytes=BIG),
        cost_estimate=takes(1),
        name="project",
    )(x, w)


def finish_kernel(copies, at_ref, hidden_ref, feed_ref, grad_ref, x_ref, d_hidden_ref, gain_ref, out_ref, in_grad_ref):
    out = (hidden_ref[...] + feed_ref[...].astype(F32)).astype(BF)
    back, _ = norm_back(grad_ref[...].astype(F32), x_ref[...].astype(F32), gain_ref[...], EPS_NORM)
    in_grad = (d_hidden_ref[...] + back).astype(BF)
    width = D // (4 * copies)
    for core in range(2):
        for copy in range(copies):
            for x in range(2):
                block = (x * 2 + (at_ref[0] + core) % 2) * copies + (at_ref[1] + copy) % copies
                to = pl.ds(pl.multiple_of(block * width, 128), width)
                at = ((core * copies + copy) * 2 + x) * width
                out_ref[:, to] = out[:, at : at + width]
                in_grad_ref[:, to] = in_grad[:, at : at + width]


def finish(place, copies, hidden, feed, grad, x, d_hidden, gain):
    shape = jax.ShapeDtypeStruct(x.shape, BF)
    return pl.pallas_call(
        functools.partial(finish_kernel, copies),
        out_shape=(shape, shape),
        in_specs=[smem_spec()] + [vmem_spec()] * 6,
        out_specs=[vmem_spec()] * 2,
        compiler_params=pltpu.CompilerParams(vmem_limit_bytes=BIG),
        cost_estimate=takes(1),
        name="finish",
    )(place, hidden, feed, grad, x, d_hidden, gain)


def turn(blocks, shift, axis):
    size = blocks.shape[axis]
    twice = jnp.concatenate([blocks, blocks], axis=axis)
    return lax.dynamic_slice_in_dim(twice, shift % size, size, axis)


class Order:
    def __init__(self, copies, core, dp):
        self.copies, self.core, self.dp = copies, core, dp

    def relative(self, values, axis):
        lead, tail = values.shape[:axis], values.shape[axis + 1 :]
        whole = values.reshape(lead + (2, 2, self.copies, D // (4 * self.copies)) + tail)
        whole = turn(turn(whole, self.core, axis + 1), self.dp, axis + 2)
        whole = jnp.moveaxis(whole, axis, axis + 2)
        return whole.reshape(values.shape)

    def plain(self, values, axis):
        lead, tail = values.shape[:axis], values.shape[axis + 1 :]
        whole = values.reshape(lead + (2, self.copies, 2, D // (4 * self.copies)) + tail)
        whole = jnp.moveaxis(whole, axis + 2, axis)
        whole = turn(turn(whole, 2 - self.core, axis + 1), self.copies - self.dp, axis + 2)
        return whole.reshape(values.shape)


def on_device(inputs, cotangent, segment_ids, weights, master, moment_one, moment_two,
              step, learn_rate, beta_one, beta_two):
    tokens = inputs.shape[0]
    rows = weights.shape[0]
    replicas = lax.axis_size("rep")
    copies = replicas // 4
    members = replicas * 4
    rep = lax.axis_index("rep")
    grp = lax.axis_index("grp")
    core = grp % 2
    dp = rep // 4
    rank = rank_of(rep, grp)
    order = Order(copies, core, dp)
    axes = ("rep", "grp")
    group_tokens = RANKS * tokens
    block_rows = RANKS * rows

    def pairs_to(move):
        return [(at, move(at // 4, at % 4)) for at in range(members)]

    core_pairs = pairs_to(lambda r, g: r * 4 + (g ^ 1))
    copy_pairs = [
        pairs_to(lambda r, g, shift=shift: ((r + 4 * shift) % replicas) * 4 + g) for shift in range(1, copies)
    ]

    in_place = (D // (4 * copies)) % 128 == 0
    x, dy = (inputs, cotangent) if in_place else (order.relative(inputs, 1), order.relative(cotangent, 1))
    seg = jnp.broadcast_to(segment_ids[None, :], (8, tokens))
    mix_blocks, out_blocks, gate_block, down_block, gate_side, down_side, x_all, seg_all, x, dy = spread(
        copies, weights, x, dy, seg
    )
    cubes = [
        [(copy * 4 + j % 4) * 4 + (j // 4) * 2 + side for j in range(RANKS)]
        for copy in range(copies)
        for side in range(2)
    ]
    dy_all = lax.all_gather(dy, axes, axis_index_groups=cubes, axis=0, tiled=True)
    x_all = x_all.reshape(group_tokens, D)
    w_mix = mix_blocks.reshape(D, MIXW)
    w_out = out_blocks.reshape(D, OW)

    def from_copies(blocks):
        block = blocks.reshape(block_rows, blocks.shape[2])
        return [lax.ppermute(block, axes, copy_pairs[copies - shift - 1]) for shift in range(1, copies)]

    def collect(blocks, side, landed):
        mine = [blocks.reshape(block_rows, blocks.shape[2])] + landed
        theirs = [side.reshape(block_rows, side.shape[2])]
        theirs = theirs + [lax.ppermute(one, axes, core_pairs) for one in landed]
        return jnp.concatenate(mine + theirs, axis=0)

    together = lax.optimization_barrier
    gate_landed = from_copies(gate_block)
    down_landed = from_copies(down_block)
    normed, p, gains, x_scale = project(x_all, w_mix)
    gain_one, gain_two = gains[:1], gains[1:2]
    extra = order.plain(w_mix[:, MIXW - EXTRA :], 0).astype(F32)
    conv_cols = CONV * (2 * KD + VD) // D
    conv_at = 2 * H + 2

    tap_rows = D // CONV
    table = extra[:, conv_at : conv_at + conv_cols].reshape(CONV, tap_rows, conv_cols)
    ranges = ((0, QW), (KD, QW), (2 * KD, VW))

    def own_channels(first, width):
        return first // conv_cols + rank * (width // conv_cols), width // conv_cols

    taps = jnp.concatenate(
        [
            lax.dynamic_slice_in_dim(table, *own_channels(first, width), 1).reshape(CONV, width)
            for first, width in ranges
        ],
        axis=1,
    )
    column = extra[: 2 * H + DV, conv_at + conv_cols]
    scalars = jnp.concatenate(
        [
            jnp.exp(lax.dynamic_slice_in_dim(column, rank * HEADS, HEADS, 0)),
            lax.dynamic_slice_in_dim(column, H + rank * HEADS, HEADS, 0),
        ]
    )
    out_gain = column[2 * H : 2 * H + DV][None]
    rank_arg = jnp.reshape(rank, (1,)).astype(jnp.int32)
    gated, inverse, update = mixer(rank_arg, scalars, seg_all, p, taps, out_gain, tokens)
    partial = dot(gated, w_out, NT).astype(BF)
    hidden, normed_two = branch(copies, partial.reshape(RANKS, tokens, D), x, gain_two)
    normed_two = normed_two.reshape(group_tokens, D)
    normed_two, gate_landed, down_landed = together((normed_two, gate_landed, down_landed))
    w_gates = collect(gate_block, gate_side, gate_landed)
    w_down = collect(down_block, down_side, down_landed)
    gate_up = dot(normed_two, w_gates, NN)
    gate_part, up_part = gate_up[:, :FW], gate_up[:, FW:]
    tile_count = jnp.where(rank < FULL_RANKS, FT, FT - 1)
    real = (jnp.arange(FW) < tile_count * 128)[None]
    sigmoid_gate = jax.nn.sigmoid(gate_part)
    activated = jnp.where(real, gate_part * sigmoid_gate * up_part, 0.0).astype(BF)
    half = copies * block_rows

    def block_of(values, at):
        return values[:, at * block_rows : (at + 1) * block_rows]

    def first_half(left, right):
        theirs = dot(left[:, half:], right, TN).astype(BF)
        return theirs, lax.ppermute(theirs, axes, core_pairs)

    def away_rows(left, right, got):
        return [
            (dot(block_of(left, at), right, TN) + got[at * block_rows : (at + 1) * block_rows].astype(F32)).astype(BF)
            for at in range(1, copies)
        ]

    def to_copies(away):
        return [lax.ppermute(one, axes, pairs) for one, pairs in zip(away, copy_pairs)]

    def for_copies(left, right, got):
        away = away_rows(left, right, got)
        return away, to_copies(away)

    down_half, down_got = first_half(dy_all, activated)
    down_half, activated = together((down_half, activated))
    d_act = dot(dy_all, w_down, NN)
    d_gate = d_act * up_part * sigmoid_gate * (1 + gate_part * (1 - sigmoid_gate))
    d_up = d_act * gate_part * sigmoid_gate
    real_two = jnp.concatenate([real, real], axis=1)
    d_gate_up = jnp.where(real_two, jnp.concatenate([d_gate, d_up], axis=1), 0.0).astype(BF)
    gate_half, gate_got = first_half(normed_two, d_gate_up)
    down_away, down_landed = for_copies(dy_all, activated, down_got)
    gate_half, down_away, d_gate_up = together((gate_half, down_away, d_gate_up))
    d_normed_two = dot(d_gate_up, w_gates, NT).astype(BF)
    d_gate_part, d_up_part = d_gate_up[:, :FW], d_gate_up[:, FW:]
    gate_away = away_rows(normed_two, d_gate_part, gate_got[:, :FW])
    up_away = away_rows(normed_two, d_up_part, gate_got[:, FW:])
    gate_away, up_away, d_normed_two = together((gate_away, up_away, d_normed_two))
    up_landed = to_copies(up_away)
    d_hidden, gain_two_grad, d_hidden_all = hidden_back(
        copies, d_normed_two.reshape(RANKS, tokens, D), hidden, dy, gain_two
    )
    d_hidden_all = d_hidden_all.reshape(group_tokens, D)
    d_hidden_all, up_landed, gate_away, down_landed, activated = together(
        (d_hidden_all, up_landed, gate_away, down_landed, activated)
    )
    feed = dot(activated, w_down, NT).astype(BF)
    feed, d_hidden_all = together((feed, d_hidden_all))
    feed = lax.psum_scatter(feed, axes, axis_index_groups=cubes, scatter_dimension=0, tiled=True)
    gate_landed = to_copies(gate_away)
    out_half, out_got = first_half(d_hidden_all, gated)
    out_half, d_hidden_all = together((out_half, d_hidden_all))
    d_gated = dot(d_hidden_all, w_out, NN)
    out_away = away_rows(d_hidden_all, gated, out_got)
    out_away, d_gated = together((out_away, d_gated))
    out_landed = to_copies(out_away)
    d_mix, d_taps, d_out_gain, d_scalars = mixer_back(
        rank_arg, scalars, seg_all, p, taps, out_gain, inverse, update, d_gated, tokens
    )

    def own_rows(left, right, got, column, landed, count=None):
        adds = ((got, 0, column),) + tuple((one, 0, 0) for one in landed)
        total = weight_grad(left, right, 0, block_rows, adds, count)
        return total.reshape(RANKS, rows, total.shape[1])

    mix_columns = MIXW - EXTRA
    mix_half = weight_grad(normed, d_mix, 1, half, (), mix_columns)
    mix_got = lax.ppermute(mix_half, axes, core_pairs)
    mix_half, d_mix, gate_landed, out_landed = together((mix_half, d_mix, gate_landed, out_landed))
    mix_away = [
        weight_grad(normed, d_mix, at, block_rows, ((mix_got, at, 0),), mix_columns) for at in range(1, copies)
    ]
    mix_landed = to_copies(mix_away)
    mix_away, d_mix, d_gate_part, d_up_part, activated, gated, d_taps, d_scalars, d_out_gain, gain_two_grad = together(
        (mix_away, d_mix, d_gate_part, d_up_part, activated, gated, d_taps, d_scalars, d_out_gain, gain_two_grad)
    )
    d_normed, gain_one_grad = input_back(d_mix, w_mix, x_all, x_scale)
    gain_one_grad = gain_one_grad[0]
    d_input = lax.psum_scatter(d_normed, axes, axis_index_groups=cubes, scatter_dimension=0, tiled=True)
    up_rows = own_rows(normed_two, d_up_part, gate_got, FW, up_landed)
    down_rows = own_rows(dy_all, activated, down_got, 0, down_landed)
    gate_rows = own_rows(normed_two, d_gate_part, gate_got, 0, gate_landed)
    out_rows = own_rows(d_hidden_all, gated, out_got, 0, out_landed)
    tap_grad = jnp.zeros((CONV, tap_rows, conv_cols), F32)
    at = 0
    for first, width in ranges:
        start, count = own_channels(first, width)
        piece = d_taps[:, at : at + width].reshape(CONV, count, conv_cols)
        tap_grad = lax.dynamic_update_slice(tap_grad, piece, (0, start, 0))
        at = at + width
    small = jnp.zeros((D,), F32)
    small = lax.dynamic_update_slice(small, d_scalars[0, :HEADS], (rank * HEADS,))
    small = lax.dynamic_update_slice(small, d_scalars[0, HEADS : 2 * HEADS], (H + rank * HEADS,))
    small = lax.dynamic_update_slice(small, d_out_gain[0], (2 * H,))
    core_grad = jnp.concatenate(
        [
            jnp.zeros((D, conv_at), F32),
            tap_grad.reshape(D, conv_cols),
            small[:, None],
            jnp.zeros((D, EXTRA - conv_at - 1 - conv_cols), F32),
        ],
        axis=1,
    )
    lanes = jnp.arange(EXTRA)[None]
    extra_grad = (
        dot(normed, d_mix[:, MIXW - EXTRA :], TN)
        + jnp.where(lanes == 2 * H, gain_one_grad[:, None], 0.0)
        + jnp.where(lanes == 2 * H + 1, gain_two_grad.reshape(D, 1), 0.0)
        + order.relative(core_grad, 0)
    )
    extra_got = lax.ppermute(extra_grad[half:], axes, core_pairs)
    extra_sum = extra_grad[:half] + extra_got
    extra_landed = [
        lax.ppermute(extra_sum[at * block_rows : (at + 1) * block_rows], axes, pairs)
        for at, pairs in zip(range(1, copies), copy_pairs)
    ]
    extra_sum, out_rows = together((extra_sum, out_rows))
    grads_rest = home_rest(copies, (out_rows, gate_rows, up_rows, down_rows))
    extra_rows = extra_sum[:block_rows]
    for one in extra_landed:
        extra_rows = extra_rows + one
    step_float = step[0].astype(F32)
    adam_scalars = jnp.stack(
        [beta_one[0], beta_two[0], learn_rate[0], 1 - beta_one[0] ** step_float, 1 - beta_two[0] ** step_float]
    )
    state = (moment_one, moment_two, master)
    done = adam(adam_scalars, grads_rest, state, None, MIX_END, 2048, 4)
    done = adam(adam_scalars, grads_rest, state, done, MIX_END + 4 * 2048, 2560, 5)
    done, extra_rows, normed = together((done, extra_rows, normed))
    mix_rows = own_rows(normed, d_mix, mix_got, 0, mix_landed, mix_columns)
    grads_mix, extra_rows = home(copies, mix_rows, extra_rows.reshape(RANKS, rows, EXTRA))
    grads_mix, d_input, feed = together((grads_mix, d_input, feed))
    if in_place:
        output, input_grad = finish(
            jnp.stack([core, dp]).astype(jnp.int32), copies, hidden, feed, d_input, x, d_hidden, gain_one
        )
    else:
        output = order.plain((hidden + feed.astype(F32)).astype(BF), 1)
        back, _ = norm_back(d_input.astype(F32), x.astype(F32), gain_one, EPS_NORM)
        input_grad = order.plain((d_hidden + back).astype(BF), 1)
    done = adam(adam_scalars, extra_rows, state, done, EXTRA_START, EXTRA, 1)
    done = adam(adam_scalars, grads_mix, state, done, 0, 2048, 6)
    gain_grads = extra_rows[:, 2 * H : 2 * H + 2]
    return (output, input_grad) + tuple(done) + (gain_grads,)


def solution(mesh):
    by_token = P(("rep", "grp"), None)
    by_row = P(("grp", "rep"), None)
    return jax.shard_map(
        on_device,
        mesh=mesh,
        in_specs=(by_token, by_token, P(("rep", "grp")), by_row, by_row, by_row, by_row, P(), P(), P(), P()),
        out_specs=(by_token, by_token) + (by_row,) * 6,
        check_vma=False,
    )
```
